256 devices in a mesh: rep: 8 (over x, core), shard: 32 (over y, z).
Axes of the slice: x: 4, y: 4, z: 8, core: 2. Of those that a mesh axis runs over, the one named last changes fastest.
Arguments:
- grads: bfloat16 [8, 5120, 1536], P('rep', 'shard'), may hold values from -2.5 to 2.5
- left_prev: float32 [64, 512, 512], P('shard'), as said below
- right_prev: float32 [64, 512, 512], P('shard'), as said below
- block_owner: int32 [30], replicated, may hold values from 0 to 31, as said below
- block_row: int32 [30], replicated, may hold values from 0 to 4608, as said below
- block_col: int32 [30], replicated, may hold values from 0 to 1024, as said below
Outputs:
- direction: bfloat16 [5120, 1536], P('shard')
- left_new: float32 [64, 512, 512], P('shard')
- right_new: float32 [64, 512, 512], P('shard')
The draws below stay inside these ranges and needn't reach their ends.
Inputs may be any that keep to these rules, and one draw needn't show every extreme that they name: `block_owner`: each owner holds at most 2 blocks and some owner holds exactly 2. `block_row`: multiples of 512; together with block_col the blocks cover the 5120 x 1536 matrix, each entry once. `block_col`: multiples of 512. `left_prev`: each slot holds a symmetric positive definite matrix. `right_prev`: each slot holds a symmetric positive definite matrix.
All inputs are finite; a program needn't handle non-finite values.
Results may differ from the reference program's by a relative error of at most 0.022.
Values may be sent and summed in bfloat16 or wider, within the bound.
A program may use at most 128 MiB of HBM per device.

```python
import math
import jax
import jax.numpy as jnp
from jax import lax

D = 5120
BLK = 512
COLB = 3
ITERS = 2
C = 1536
NB = 30
MAXB = 2
SLOTS = 64
REPS = 8
N_SHARD = 32


def block_tables(key):
    cells = jax.random.permutation(jax.random.fold_in(key, 11), NB)
    chosen_owner = jax.random.randint(jax.random.fold_in(key, 12), (), 0, N_SHARD)
    scores = jax.random.permutation(jax.random.fold_in(key, 13), SLOTS)
    holder = jnp.arange(SLOTS) // MAXB
    scores = jnp.where(holder == chosen_owner, scores - SLOTS, scores)
    picked = jnp.argsort(scores)[:NB]
    owners = (picked // MAXB).astype(jnp.int32)
    rows = (cells // COLB * BLK).astype(jnp.int32)
    cols = (cells % COLB * BLK).astype(jnp.int32)
    return (owners, rows, cols)


def draw_block_owner(key, part):
    return block_tables(key)[0]


def draw_block_row(key, part):
    return block_tables(key)[1]


def draw_block_col(key, part):
    return block_tables(key)[2]


def draw_grads(key, part):
    key = jax.random.fold_in(key, 31)
    key_own = jax.random.fold_in(key, 1)
    values = jax.random.normal(key_own, (REPS, D, C), jnp.float32) * 0.35
    return jnp.clip(values, -2.5, 2.5).astype(jnp.bfloat16)


def definite_slots(key, base, spread):
    key_diag = jax.random.fold_in(key, 1)
    key_off = jax.random.fold_in(key, 2)
    diag_part = base * jnp.exp(jax.random.uniform(key_diag, (SLOTS, BLK), jnp.float32) * math.log(spread))
    noise = jax.random.uniform(key_off, (SLOTS, BLK, BLK), jnp.float32, minval=-0.03, maxval=0.03)
    sym = (noise + jnp.swapaxes(noise, 1, 2)) * 0.7071
    ident = jnp.eye(BLK, dtype=jnp.float32)
    outer = jnp.sqrt(diag_part[:, :, None] * diag_part[:, None, :])
    return outer * (ident + sym * (1.0 - ident))


def draw_left_prev(key, part):
    key = jax.random.fold_in(key, 21)
    return definite_slots(key, 30.0, 10.0)


def draw_right_prev(key, part):
    key = jax.random.fold_in(key, 22)
    return definite_slots(key, 30.0, 10.0)


def setup_inputs(seed: int = 0) -> dict:
    splits = jax.random.split(jax.random.key(seed), 7)
    grads = draw_grads(jax.random.fold_in(splits[6], 71), 0)
    left_prev = draw_left_prev(jax.random.fold_in(splits[6], 71), 0)
    right_prev = draw_right_prev(jax.random.fold_in(splits[6], 71), 0)
    block_owner = draw_block_owner(jax.random.fold_in(splits[6], 71), 0)
    block_row = draw_block_row(jax.random.fold_in(splits[6], 71), 0)
    block_col = draw_block_col(jax.random.fold_in(splits[6], 71), 0)
    return dict(grads=grads, left_prev=left_prev, right_prev=right_prev, block_owner=block_owner, block_row=block_row, block_col=block_col)


def slot_table(owner, per_owner):
    count = owner.shape[0]
    index = jnp.arange(count, dtype=jnp.int32)
    same = (owner[:, None] == owner[None, :]) & (index[None, :] < index[:, None])
    return owner * per_owner + lax.optimization_barrier(jnp.sum(same.astype(jnp.int32), axis=1))

def inverse_root(mats, iterations):
    size = mats.shape[-1]
    highest = lax.Precision.HIGHEST
    ident = jnp.eye(size, dtype=jnp.float32)
    scale = jnp.trace(mats, axis1=1, axis2=2) / size
    coupled = mats / scale[:, None, None]
    factor = scale ** (-0.25)
    root = ident[None]
    for step in range(iterations):
        middle = (5.0 * ident - coupled) * 0.25
        if step == 0:
            root = factor[:, None, None] * middle
        else:
            root = jnp.einsum('kij,kjl->kil', root, middle, precision=highest)
        if step + 1 < iterations:
            square = jnp.einsum('kij,kjl->kil', middle, middle, precision=highest)
            fourth = jnp.einsum('kij,kjl->kil', square, square, precision=highest)
            coupled = jnp.einsum('kij,kjl->kil', fourth, coupled, precision=highest)
    return root

def reference(grads, left_prev, right_prev, block_owner, block_row, block_col):
    highest = lax.Precision.HIGHEST
    total = lax.optimization_barrier(jnp.sum(grads.astype(jnp.float32), axis=0))
    rounded = lax.optimization_barrier(total.astype(jnp.bfloat16)).astype(jnp.float32)
    slots = slot_table(block_owner.astype(jnp.int32), MAXB)

    def take(row0, col0):
        return lax.dynamic_slice(rounded, (row0.astype(jnp.int32), col0.astype(jnp.int32)), (BLK, BLK))
    blocks = jax.vmap(take)(block_row, block_col)
    left_blocks = left_prev[slots] + jnp.einsum('sik,sjk->sij', blocks, blocks, precision=highest)
    right_blocks = right_prev[slots] + jnp.einsum('ski,skj->sij', blocks, blocks, precision=highest)
    roots = inverse_root(jnp.concatenate([left_blocks, right_blocks], axis=0), ITERS)
    left_root = roots[:NB]
    right_root = roots[NB:]
    precond = jnp.einsum('sik,skl->sil', left_root, blocks, precision=highest)
    precond = jnp.einsum('sil,slj->sij', precond, right_root, precision=highest)
    ratio = jnp.sqrt(lax.optimization_barrier(jnp.sum(blocks * blocks, axis=(1, 2))) / (lax.optimization_barrier(jnp.sum(precond * precond, axis=(1, 2))) + 1e-06))
    dir_blocks = (precond * ratio[:, None, None]).astype(jnp.bfloat16)
    cells = block_row // BLK * COLB + block_col // BLK
    by_cell = jnp.zeros((NB, BLK, BLK), jnp.bfloat16).at[cells].set(dir_blocks)
    direction = by_cell.reshape(D // BLK, COLB, BLK, BLK).transpose(0, 2, 1, 3).reshape(D, C)
    left_new = jnp.zeros((SLOTS, BLK, BLK), jnp.float32).at[slots].set(left_blocks)
    right_new = jnp.zeros((SLOTS, BLK, BLK), jnp.float32).at[slots].set(right_blocks)
    return (direction, left_new, right_new)
```

```python
import jax
import jax.numpy as jnp
from jax import lax
from jax.experimental import pallas as pl
from jax.experimental.pallas import tpu as pltpu
from jax.sharding import PartitionSpec as P

BLK = 512
COLB = 3
ROWB = 10
CELLS = 30
SHARDS = 32
HALF = 16
TILES = 5
LANE = 128
SUB = 16
XS = 4
MESH = pl.DeviceIdType.MESH
BF = jnp.bfloat16
F32 = jnp.float32


def place():
    rep = lax.axis_index("rep")
    shard = lax.axis_index("shard")
    x = rep // 2
    h = rep % 2
    return rep, shard, x, h


def send(src, dst, send_sem, recv_sem, rep, shard):
    return pltpu.make_async_remote_copy(
        src_ref=src,
        dst_ref=dst,
        send_sem=send_sem,
        recv_sem=recv_sem,
        device_id=(rep, shard),
        device_id_type=MESH,
    )


def greet(barrier, rep, shard):
    pl.semaphore_signal(barrier, inc=1, device_id=(rep, shard), device_id_type=MESH)


def same(a, b):
    return (a == b).astype(jnp.int32)


def spread_rep(view, rep, shard, x, h, ssem, rsem):
    step = 1 - 2 * h
    xa = (x + step + XS) % XS
    xb = (x - step + XS) % XS
    xo = (x + 2) % XS
    ra, rb, partner = 2 * xa + h, 2 * xb + h, 2 * x + 1 - h
    mine = view(h, x)
    to_a = send(mine, mine, ssem.at[0], rsem.at[0], ra, shard)
    to_b = send(mine, mine, ssem.at[1], rsem.at[1], rb, shard)
    to_p = send(mine, mine, ssem.at[2], rsem.at[3], partner, shard)
    to_a.start()
    to_b.start()
    to_p.start()
    from_b, from_a, from_o = view(h, xb), view(h, xa), view(h, xo)
    pltpu.make_async_copy(from_b, from_b, rsem.at[0]).wait()
    on_a = send(from_b, from_b, ssem.at[3], rsem.at[2], ra, shard)
    on_p0 = send(from_b, from_b, ssem.at[4], rsem.at[4], partner, shard)
    on_a.start()
    on_p0.start()
    pltpu.make_async_copy(from_a, from_a, rsem.at[1]).wait()
    on_p1 = send(from_a, from_a, ssem.at[5], rsem.at[5], partner, shard)
    on_p1.start()
    pltpu.make_async_copy(from_o, from_o, rsem.at[2]).wait()
    on_p2 = send(from_o, from_o, ssem.at[6], rsem.at[6], partner, shard)
    on_p2.start()
    for index, col in ((3, x), (4, xa), (5, xb), (6, xo)):
        there = view(1 - h, col)
        pltpu.make_async_copy(there, there, rsem.at[index]).wait()
    for copy in (to_a, to_b, to_p, on_a, on_p0, on_p1, on_p2):
        copy.wait_send()


def gather_kernel(
    cell_of_slot, grads, g_out, own, pair, part, xin, red, mid, outb,
    own_sem, pair_sem, xs_sem, xr_sem, s1_sem, r1_sem, s2_sem, r2_sem, s3_sem, r3_sem,
):
    rep, shard, x, h = place()
    half = shard // HALF
    tile = shard % HALF
    partner = 2 * x + 1 - h
    barrier = pltpu.get_barrier_semaphore()

    load = pltpu.make_async_copy(grads.at[:, h], own, own_sem)
    load.start()

    def greet_source(r, carry):
        source = (HALF * r + tile) // TILES

        @pl.when(source != shard)
        def _():
            greet(barrier, rep, source)

        return carry

    lax.fori_loop(0, ROWB, greet_source, 0)

    def greet_half(r, carry):
        greet(barrier, rep, half * HALF + (tile + r) % HALF)
        return carry

    lax.fori_loop(1, HALF, greet_half, 0)
    greet(barrier, partner, shard)
    for d in range(1, XS):
        greet(barrier, 2 * ((x + d) % XS) + h, shard)
    waits = 2 * TILES + HALF - 1 + XS
    for i in range(TILES):
        waits = waits - same((TILES * shard + i) % HALF, tile)
    pl.semaphore_wait(barrier, waits)

    swap = send(grads.at[:, 1 - h], pair, pair_sem.at[0], pair_sem.at[1], partner, shard)
    swap.start()
    load.wait()
    swap.wait_recv()
    for q in range(XS):
        for c in range(COLB):
            lanes = slice(c * BLK + q * LANE, c * BLK + (q + 1) * LANE)
            part[q, :, c] = (own[:, :, lanes].astype(F32) + pair[:, :, lanes].astype(F32)).astype(BF)
    sends = []
    for d in range(1, XS):
        to = (x + d) % XS
        copy = send(part.at[to], xin.at[d - 1], xs_sem.at[d - 1], xr_sem.at[d - 1], 2 * to + h, shard)
        copy.start()
        sends.append(copy)
    for copy in sends:
        copy.wait_recv()
    red[...] = (
        (part[x].astype(F32) + xin[0].astype(F32)) + (xin[1].astype(F32) + xin[2].astype(F32))
    ).astype(BF)

    for i in range(TILES):
        u = TILES * shard + i
        for d in range(2):
            to = d * HALF + u % HALF
            dst = mid.at[pl.ds(COLB * (u // HALF), COLB)]

            @pl.when(to != shard)
            def _():
                send(red.at[i], dst, s1_sem.at[2 * i + d], r1_sem, rep, to).start()

            @pl.when(to == shard)
            def _():
                pltpu.make_async_copy(red.at[i], dst, r1_sem).start()

    pltpu.make_async_copy(mid, mid, r1_sem).wait()

    def pick(o, carry):
        for j in range(2):
            outb[o, j] = mid[cell_of_slot[2 * (half * HALF + o) + j]]
        to = half * HALF + o
        dst = g_out.at[tile, :, h, :, pl.ds(pl.multiple_of(x * LANE, LANE), LANE)]

        @pl.when(to != shard)
        def _():
            send(outb.at[o], dst, s2_sem.at[o], r2_sem, rep, to).start()

        @pl.when(to == shard)
        def _():
            pltpu.make_async_copy(outb.at[o], dst, r2_sem).start()

        return carry

    lax.fori_loop(0, HALF, pick, 0)

    def view(hh, col):
        return g_out.at[:, :, hh, :, pl.ds(pl.multiple_of(col * LANE, LANE), LANE)]

    mine = view(h, x)
    pltpu.make_async_copy(mine, mine, r2_sem).wait()
    spread_rep(view, rep, shard, x, h, s3_sem, r3_sem)

    swap.wait_send()
    for copy in sends:
        copy.wait_send()
    for i in range(TILES):
        u = TILES * shard + i
        for d in range(2):
            to = d * HALF + u % HALF

            @pl.when(to != shard)
            def _():
                send(red.at[i], red.at[i], s1_sem.at[2 * i + d], r1_sem, rep, to).wait_send()

    def drain(o, carry):
        to = half * HALF + o

        @pl.when(to != shard)
        def _():
            send(outb.at[o], outb.at[o], s2_sem.at[o], r2_sem, rep, to).wait_send()

        return carry

    lax.fori_loop(0, HALF, drain, 0)


def eye(size):
    row = lax.broadcasted_iota(jnp.int32, (size, size), 0)
    col = lax.broadcasted_iota(jnp.int32, (size, size), 1)
    return row == col


def mm(a, b):
    return jnp.dot(a, b, preferred_element_type=F32)


def root_less_one(new, scale):
    diag = eye(BLK)
    e = 0.25 * (jnp.where(diag, 1.0, 0.0) - new * (1.0 / scale))
    eb = e.astype(BF)
    u = 2.0 * e + mm(eb, eb)
    ub = u.astype(BF)
    v = 2.0 * u + mm(ub, ub)
    w = 4.0 * u - 5.0 * e
    z = (u - 0.25 * v) + 0.25 * mm(v.astype(BF), w.astype(BF))
    return z.astype(BF)


def work_kernel(live, g_in, left_prev, right_prev, left_new, right_new, p_out,
                lp, rp, ln, rn, pb, in_sem, out_sem):
    _, shard, x, h = place()
    loads = []
    for j in range(2):
        for src, dst, n in ((left_prev, lp, 0), (right_prev, rp, 1)):
            copy = pltpu.make_async_copy(src.at[j], dst.at[j], in_sem.at[2 * j + n])
            copy.start()
            loads.append(copy)
    stores = []
    for j in range(2):
        on = live[2 * shard + j] > 0
        g = g_in[:, j].reshape(BLK, BLK)
        g = jnp.where(on, g, jnp.zeros_like(g))
        gt = g.T
        diag = eye(BLK)
        roots = []
        for n, (prev, new, out, a, b) in enumerate(
            ((lp, ln, left_new, g, gt), (rp, rn, right_new, gt, g))
        ):
            loads[2 * j + n].wait()
            val = prev[j] + mm(a, b)
            val = jnp.where(on, val, jnp.zeros_like(val))
            new[j] = val
            copy = pltpu.make_async_copy(new.at[j], out.at[j], out_sem.at[2 * j + n])
            copy.start()
            stores.append(copy)
            scale = jnp.sum(jnp.where(diag, val, 0.0)) * (1.0 / BLK)
            scale = jnp.where(on, scale, 1.0)
            roots.append((root_less_one(val, scale), scale))
        (zl, cl), (zr, cr) = roots
        gf = g.astype(F32)
        y = lax.rsqrt(jnp.sqrt(jnp.full((8, LANE), cl, F32)))[0:1, 0:1] * (gf + mm(zl, g))
        p = lax.rsqrt(jnp.sqrt(jnp.full((8, LANE), cr, F32)))[0:1, 0:1] * (y + mm(y.astype(BF), zr))
        sg = jnp.full((8, LANE), jnp.sum(gf * gf), F32)
        sp = jnp.full((8, LANE), jnp.sum(p * p), F32)
        ratio = jnp.sqrt(sg / (sp + 1e-06))[0:1, 0:1]
        pb[...] = (p * ratio).astype(BF).reshape(HALF, 2, SUB, BLK)
        p_out[:, j] = pb[:, h, :, pl.ds(pl.multiple_of(x * LANE, LANE), LANE)]
    for copy in stores:
        copy.wait()


def return_kernel(
    slot_of_cell, p_in, d_out, mid, outb, land, full,
    s1_sem, r1_sem, s2_sem, r2_sem, s3_sem, r3_sem,
):
    rep, shard, x, h = place()
    half = shard // HALF
    tile = shard % HALF
    partner = 2 * x + 1 - h
    barrier = pltpu.get_barrier_semaphore()

    def greet_half(r, carry):
        greet(barrier, rep, half * HALF + (tile + r) % HALF)
        return carry

    lax.fori_loop(1, HALF, greet_half, 0)
    for i in range(TILES):
        for d in range(2):
            source = d * HALF + (TILES * shard + i) % HALF

            @pl.when(source != shard)
            def _():
                greet(barrier, rep, source)

    greet(barrier, partner, shard)
    greet(barrier, 2 * ((x + 1) % XS) + h, shard)
    greet(barrier, 2 * ((x + 3) % XS) + h, shard)
    waits = HALF - 1 + ROWB + 3
    for r in range(ROWB):
        waits = waits - same((HALF * r + tile) // TILES, shard)
    pl.semaphore_wait(barrier, waits)

    def give(k, carry):
        to = half * HALF + k
        dst = mid.at[pl.ds(2 * tile, 2)]

        @pl.when(to != shard)
        def _():
            send(p_in.at[k], dst, s1_sem.at[k], r1_sem, rep, to).start()

        @pl.when(to == shard)
        def _():
            pltpu.make_async_copy(p_in.at[k], dst, r1_sem).start()

        return carry

    lax.fori_loop(0, HALF, give, 0)
    pltpu.make_async_copy(mid, mid, r1_sem).wait()

    def pick(r, carry):
        for c in range(COLB):
            slot = slot_of_cell[COLB * r + c] - 2 * HALF * half
            inside = (slot >= 0) & (slot < 2 * HALF)
            value = mid[jnp.clip(slot, 0, 2 * HALF - 1)]
            outb[r, c] = jnp.where(inside, value, jnp.zeros_like(value))
        u = HALF * r + tile
        to = u // TILES
        dst = land.at[half, u % TILES]

        @pl.when(to != shard)
        def _():
            send(outb.at[r], dst, s2_sem.at[r], r2_sem, rep, to).start()

        @pl.when(to == shard)
        def _():
            pltpu.make_async_copy(outb.at[r], dst, r2_sem).start()

        return carry

    lax.fori_loop(0, ROWB, pick, 0)
    pltpu.make_async_copy(land, land, r2_sem).wait()

    def view(hh, col):
        return full.at[:, :, hh, :, pl.ds(pl.multiple_of(col * LANE, LANE), LANE)]

    for c in range(COLB):
        full[c, :, h, :, pl.ds(pl.multiple_of(x * LANE, LANE), LANE)] = land[0, :, c] + land[1, :, c]
    spread_rep(view, rep, shard, x, h, s3_sem, r3_sem)
    for c in range(COLB):
        d_out[:, :, :, c * BLK:(c + 1) * BLK] = full[c]

    def drain1(k, carry):
        to = half * HALF + k

        @pl.when(to != shard)
        def _():
            send(p_in.at[k], p_in.at[k], s1_sem.at[k], r1_sem, rep, to).wait_send()

        return carry

    lax.fori_loop(0, HALF, drain1, 0)

    def drain2(r, carry):
        to = (HALF * r + tile) // TILES

        @pl.when(to != shard)
        def _():
            send(outb.at[r], outb.at[r], s2_sem.at[r], r2_sem, rep, to).wait_send()

        return carry

    lax.fori_loop(0, ROWB, drain2, 0)


def tables(block_owner, block_row, block_col):
    count = block_owner.shape[0]
    index = jnp.arange(count, dtype=jnp.int32)
    earlier = (block_owner[:, None] == block_owner[None, :]) & (index[None, :] < index[:, None])
    slot = 2 * block_owner + jnp.sum(earlier.astype(jnp.int32), axis=1)
    cell = block_row // BLK * COLB + block_col // BLK
    at_slot = (slot[None, :] == jnp.arange(2 * SHARDS, dtype=jnp.int32)[:, None]).astype(jnp.int32)
    at_cell = (cell[None, :] == jnp.arange(CELLS, dtype=jnp.int32)[:, None]).astype(jnp.int32)
    cell_of_slot = jnp.sum(at_slot * cell[None, :], axis=1)
    live = jnp.sum(at_slot, axis=1)
    slot_of_cell = jnp.sum(at_cell * slot[None, :], axis=1)
    return cell_of_slot, live, slot_of_cell


SMEM = pl.BlockSpec(memory_space=pltpu.SMEM)
VMEM = pl.BlockSpec(memory_space=pltpu.VMEM)
ANY = pl.BlockSpec(memory_space=pl.ANY)
DMA = pltpu.SemaphoreType.DMA


def body(grads, left_prev, right_prev, block_owner, block_row, block_col):
    cell_of_slot, live, slot_of_cell = tables(block_owner, block_row, block_col)
    rows = grads.shape[1]
    gathered = pl.pallas_call(
        gather_kernel,
        out_shape=jax.ShapeDtypeStruct((HALF, 2, 2, SUB, BLK), BF),
        in_specs=[SMEM, ANY],
        out_specs=VMEM,
        scratch_shapes=[
            pltpu.VMEM((TILES, SUB, COLB * BLK), BF),
            pltpu.VMEM((TILES, SUB, COLB * BLK), BF),
            pltpu.VMEM((XS, TILES, COLB, SUB, LANE), BF),
            pltpu.VMEM((XS - 1, TILES, COLB, SUB, LANE), BF),
            pltpu.VMEM((TILES, COLB, SUB, LANE), BF),
            pltpu.VMEM((CELLS, SUB, LANE), BF),
            pltpu.VMEM((HALF, 2, SUB, LANE), BF),
            DMA, DMA((2,)), DMA((3,)), DMA((3,)), DMA((10,)), DMA, DMA((16,)), DMA, DMA((7,)), DMA((7,)),
        ],
        compiler_params=pltpu.CompilerParams(
            collective_id=0, has_side_effects=True, vmem_limit_bytes=32 * 1024 * 1024
        ),
        name="gather_blocks",
    )(cell_of_slot, grads.reshape(TILES, 2, SUB, COLB * BLK))

    sq = jax.ShapeDtypeStruct((2, BLK, BLK), F32)
    left_new, right_new, piece = pl.pallas_call(
        work_kernel,
        out_shape=(sq, sq, jax.ShapeDtypeStruct((HALF, 2, SUB, LANE), BF)),
        in_specs=[SMEM, VMEM, ANY, ANY],
        out_specs=(ANY, ANY, VMEM),
        scratch_shapes=[pltpu.VMEM((2, BLK, BLK), F32)] * 4
        + [pltpu.VMEM((HALF, 2, SUB, BLK), BF), DMA((4,)), DMA((4,))],
        compiler_params=pltpu.CompilerParams(vmem_limit_bytes=48 * 1024 * 1024),
        cost_estimate=pl.CostEstimate(flops=20 * 2 * BLK**3, bytes_accessed=8 * 2**20, transcendentals=0),
        name="precondition",
    )(live, gathered, left_prev, right_prev)

    direction = pl.pallas_call(
        return_kernel,
        out_shape=jax.ShapeDtypeStruct((TILES, 2, SUB, COLB * BLK), BF),
        in_specs=[SMEM, VMEM],
        out_specs=VMEM,
        scratch_shapes=[
            pltpu.VMEM((2 * HALF, SUB, LANE), BF),
            pltpu.VMEM((ROWB, COLB, SUB, LANE), BF),
            pltpu.VMEM((2, TILES, COLB, SUB, LANE), BF),
            pltpu.VMEM((COLB, TILES, 2, SUB, BLK), BF),
            DMA((16,)), DMA, DMA((10,)), DMA, DMA((7,)), DMA((7,)),
        ],
        compiler_params=pltpu.CompilerParams(
            collective_id=1, has_side_effects=True, vmem_limit_bytes=32 * 1024 * 1024
        ),
        name="return_blocks",
    )(slot_of_cell, piece)
    return direction.reshape(rows, COLB * BLK), left_new, right_new


def solution(mesh):
    in_specs = (P("rep", "shard", None), P("shard", None, None), P("shard", None, None), P(), P(), P())
    out_specs = (P("shard", None), P("shard", None, None), P("shard", None, None))
    return jax.shard_map(body, mesh=mesh, in_specs=in_specs, out_specs=out_specs, check_vma=False)
```

```python
import jax
import jax.numpy as jnp
from jax import lax
from jax.experimental import pallas as pl
from jax.experimental.pallas import tpu as pltpu
from jax.sharding import PartitionSpec as P

BLK = 512
COLB = 3
ROWB = 10
CELLS = 30
SHARDS = 32
HALF = 16
TILES = 5
LANE = 128
SUB = 16
XS = 4
MESH = pl.DeviceIdType.MESH
BF = jnp.bfloat16
F32 = jnp.float32


def place():
    rep = lax.axis_index("rep")
    shard = lax.axis_index("shard")
    x = rep // 2
    h = rep % 2
    return rep, shard, x, h


def send(src, dst, send_sem, recv_sem, rep, shard):
    return pltpu.make_async_remote_copy(
        src_ref=src,
        dst_ref=dst,
        send_sem=send_sem,
        recv_sem=recv_sem,
        device_id=(rep, shard),
        device_id_type=MESH,
    )


def greet(barrier, rep, shard):
    pl.semaphore_signal(barrier, inc=1, device_id=(rep, shard), device_id_type=MESH)


def same(a, b):
    return (a == b).astype(jnp.int32)


def spread_rep(view, rep, shard, x, h, ssem, rsem):
    partner = 2 * x + 1 - h
    mine = view(h, x)
    copies = []
    for n in (2, 1, 3):
        to = 2 * ((x + n) % XS) + h
        copies.append(send(mine, mine, ssem.at[n], rsem.at[n], to, shard))
    copies.append(send(mine, mine, ssem.at[0], rsem.at[0], partner, shard))
    for copy in copies:
        copy.start()
    for n in (1, 3, 2):
        piece = view(h, (x + XS - n) % XS)
        pltpu.make_async_copy(piece, piece, rsem.at[n]).wait()
        copy = send(piece, piece, ssem.at[3 + n], rsem.at[3 + n], partner, shard)
        copy.start()
        copies.append(copy)
    for index, n in ((0, 0), (4, 1), (6, 3), (5, 2)):
        there = view(1 - h, (x + XS - n) % XS)
        pltpu.make_async_copy(there, there, rsem.at[index]).wait()
    for copy in copies:
        copy.wait_send()


def eye(size):
    row = lax.broadcasted_iota(jnp.int32, (size, size), 0)
    col = lax.broadcasted_iota(jnp.int32, (size, size), 1)
    return row == col


def mm(a, b):
    return jnp.dot(a, b, preferred_element_type=F32)


def root_less_one(new, scale):
    diag = eye(BLK)
    e = 0.25 * (jnp.where(diag, 1.0, 0.0) - new * (1.0 / scale))
    eb = e.astype(BF)
    u = 2.0 * e + mm(eb, eb)
    ub = u.astype(BF)
    v = 2.0 * u + mm(ub, ub)
    w = 4.0 * u - 5.0 * e
    z = (u - 0.25 * v) + 0.25 * mm(v.astype(BF), w.astype(BF))
    return z.astype(BF)


def step_kernel(
    cell_of_slot, live, slot_of_cell, grads, left_prev, right_prev, d_out, g_out,
    own, pair, part, xin, red, mid, outb, lp, rp, pb, p_in, mid_b, outb_b, land, full,
    own_sem, pair_sem, xs_sem, xr_sem, s1_sem, r1_sem, s2_sem, r2_sem, s3_sem, r3_sem, in_sem,
    s4_sem, r4_sem, s5_sem, r5_sem, s6_sem, r6_sem,
):
    rep, shard, x, h = place()
    half = shard // HALF
    tile = shard % HALF
    partner = 2 * x + 1 - h
    barrier = pltpu.get_barrier_semaphore()

    load = pltpu.make_async_copy(grads.at[:, h], own, own_sem)
    load.start()
    loads = []
    for j in range(2):
        for src, dst, n in ((left_prev, lp, 0), (right_prev, rp, 1)):
            copy = pltpu.make_async_copy(src.at[j], dst.at[j], in_sem.at[2 * j + n])
            copy.start()
            loads.append(copy)

    def greet_source(r, carry):
        source = (HALF * r + tile) // TILES

        @pl.when(source != shard)
        def _():
            greet(barrier, rep, source)

        return carry

    lax.fori_loop(0, ROWB, greet_source, 0)

    def greet_half(r, carry):
        greet(barrier, rep, half * HALF + (tile + r) % HALF)
        return carry

    lax.fori_loop(1, HALF, greet_half, 0)
    for i in range(TILES):
        for d in range(2):
            source = d * HALF + (TILES * shard + i) % HALF

            @pl.when(source != shard)
            def _():
                greet(barrier, rep, source)

    greet(barrier, partner, shard)
    for d in range(1, XS):
        greet(barrier, 2 * ((x + d) % XS) + h, shard)
    waits = 2 * TILES + HALF - 1 + XS + ROWB
    for i in range(TILES):
        waits = waits - same((TILES * shard + i) % HALF, tile)
    for r in range(ROWB):
        waits = waits - same((HALF * r + tile) // TILES, shard)
    pl.semaphore_wait(barrier, waits)

    swap = send(grads.at[:, 1 - h], pair, pair_sem.at[0], pair_sem.at[1], partner, shard)
    swap.start()
    load.wait()
    swap.wait_recv()
    for q in range(XS):
        for c in range(COLB):
            lanes = slice(c * BLK + q * LANE, c * BLK + (q + 1) * LANE)
            part[q, :, c] = (own[:, :, lanes].astype(F32) + pair[:, :, lanes].astype(F32)).astype(BF)
    sends = []
    for d in range(1, XS):
        to = (x + d) % XS
        copy = send(part.at[to], xin.at[d - 1], xs_sem.at[d - 1], xr_sem.at[d - 1], 2 * to + h, shard)
        copy.start()
        sends.append(copy)
    for copy in sends:
        copy.wait_recv()
    red[...] = (
        (part[x].astype(F32) + xin[0].astype(F32)) + (xin[1].astype(F32) + xin[2].astype(F32))
    ).astype(BF)

    for i in range(TILES):
        u = TILES * shard + i
        for d in range(2):
            to = d * HALF + u % HALF
            dst = mid.at[pl.ds(COLB * (u // HALF), COLB)]

            @pl.when(to != shard)
            def _():
                send(red.at[i], dst, s1_sem.at[2 * i + d], r1_sem, rep, to).start()

            @pl.when(to == shard)
            def _():
                pltpu.make_async_copy(red.at[i], dst, r1_sem).start()

    pltpu.make_async_copy(mid, mid, r1_sem).wait()

    def pick(o, carry):
        for j in range(2):
            outb[o, j] = mid[cell_of_slot[2 * (half * HALF + o) + j]]
        to = half * HALF + o
        dst = g_out.at[tile, :, h, :, pl.ds(pl.multiple_of(x * LANE, LANE), LANE)]

        @pl.when(to != shard)
        def _():
            send(outb.at[o], dst, s2_sem.at[o], r2_sem, rep, to).start()

        @pl.when(to == shard)
        def _():
            pltpu.make_async_copy(outb.at[o], dst, r2_sem).start()

        return carry

    lax.fori_loop(0, HALF, pick, 0)

    def view(hh, col):
        return g_out.at[:, :, hh, :, pl.ds(pl.multiple_of(col * LANE, LANE), LANE)]

    mine = view(h, x)
    pltpu.make_async_copy(mine, mine, r2_sem).wait()
    spread_rep(view, rep, shard, x, h, s3_sem, r3_sem)

    swap.wait_send()
    for copy in sends:
        copy.wait_send()
    for i in range(TILES):
        u = TILES * shard + i
        for d in range(2):
            to = d * HALF + u % HALF

            @pl.when(to != shard)
            def _():
                send(red.at[i], red.at[i], s1_sem.at[2 * i + d], r1_sem, rep, to).wait_send()

    def drain(o, carry):
        to = half * HALF + o

        @pl.when(to != shard)
        def _():
            send(outb.at[o], outb.at[o], s2_sem.at[o], r2_sem, rep, to).wait_send()

        return carry

    lax.fori_loop(0, HALF, drain, 0)

    for j in range(2):
        on = live[2 * shard + j] > 0
        g = g_out[:, j].reshape(BLK, BLK)
        g = jnp.where(on, g, jnp.zeros_like(g))
        gt = g.T
        diag = eye(BLK)
        roots = []
        for n, (prev, a, b) in enumerate(((lp, g, gt), (rp, gt, g))):
            loads[2 * j + n].wait()
            val = prev[j] + mm(a, b)
            val = jnp.where(on, val, jnp.zeros_like(val))
            scale = jnp.sum(jnp.where(diag, val, 0.0)) * (1.0 / BLK)
            scale = jnp.where(on, scale, 1.0)
            roots.append((root_less_one(val, scale), scale))
        (zl, cl), (zr, cr) = roots
        gf = g.astype(F32)
        y = lax.rsqrt(jnp.sqrt(jnp.full((8, LANE), cl, F32)))[0:1, 0:1] * (gf + mm(zl, g))
        p = lax.rsqrt(jnp.sqrt(jnp.full((8, LANE), cr, F32)))[0:1, 0:1] * (y + mm(y.astype(BF), zr))
        sg = jnp.full((8, LANE), jnp.sum(gf * gf), F32)
        sp = jnp.full((8, LANE), jnp.sum(p * p), F32)
        ratio = jnp.sqrt(sg / (sp + 1e-06))[0:1, 0:1]
        pb[...] = (p * ratio).astype(BF).reshape(HALF, 2, SUB, BLK)
        p_in[:, j] = pb[:, h, :, pl.ds(pl.multiple_of(x * LANE, LANE), LANE)]

    def give(k, carry):
        to = half * HALF + k
        dst = mid_b.at[pl.ds(2 * tile, 2)]

        @pl.when(to != shard)
        def _():
            send(p_in.at[k], dst, s4_sem.at[k], r4_sem, rep, to).start()

        @pl.when(to == shard)
        def _():
            pltpu.make_async_copy(p_in.at[k], dst, r4_sem).start()

        return carry

    lax.fori_loop(0, HALF, give, 0)
    pltpu.make_async_copy(mid_b, mid_b, r4_sem).wait()

    def pick_cells(r, carry):
        for c in range(COLB):
            slot = slot_of_cell[COLB * r + c] - 2 * HALF * half
            inside = (slot >= 0) & (slot < 2 * HALF)
            value = mid_b[jnp.clip(slot, 0, 2 * HALF - 1)]
            outb_b[r, c] = jnp.where(inside, value, jnp.zeros_like(value))
        u = HALF * r + tile
        to = u // TILES
        dst = land.at[half, u % TILES]

        @pl.when(to != shard)
        def _():
            send(outb_b.at[r], dst, s5_sem.at[r], r5_sem, rep, to).start()

        @pl.when(to == shard)
        def _():
            pltpu.make_async_copy(outb_b.at[r], dst, r5_sem).start()

        return carry

    lax.fori_loop(0, ROWB, pick_cells, 0)
    pltpu.make_async_copy(land, land, r5_sem).wait()

    def view_d(hh, col):
        return full.at[:, :, hh, :, pl.ds(pl.multiple_of(col * LANE, LANE), LANE)]

    for c in range(COLB):
        full[c, :, h, :, pl.ds(pl.multiple_of(x * LANE, LANE), LANE)] = land[0, :, c] + land[1, :, c]
    spread_rep(view_d, rep, shard, x, h, s6_sem, r6_sem)
    for c in range(COLB):
        d_out[:, :, :, c * BLK:(c + 1) * BLK] = full[c]

    def drain1(k, carry):
        to = half * HALF + k

        @pl.when(to != shard)
        def _():
            send(p_in.at[k], p_in.at[k], s4_sem.at[k], r4_sem, rep, to).wait_send()

        return carry

    lax.fori_loop(0, HALF, drain1, 0)

    def drain2(r, carry):
        to = (HALF * r + tile) // TILES

        @pl.when(to != shard)
        def _():
            send(outb_b.at[r], outb_b.at[r], s5_sem.at[r], r5_sem, rep, to).wait_send()

        return carry

    lax.fori_loop(0, ROWB, drain2, 0)


def factors_kernel(live, g_in, left_prev, right_prev, left_new, right_new, lp, rp, ln, rn, in_sem, out_sem):
    shard = lax.axis_index("shard")
    loads = []
    for j in range(2):
        for src, dst, n in ((left_prev, lp, 0), (right_prev, rp, 1)):
            copy = pltpu.make_async_copy(src.at[j], dst.at[j], in_sem.at[2 * j + n])
            copy.start()
            loads.append(copy)
    stores = []
    for j in range(2):
        on = live[2 * shard + j] > 0
        g = g_in[:, j].reshape(BLK, BLK)
        g = jnp.where(on, g, jnp.zeros_like(g))
        gt = g.T
        for n, (prev, new, out, a, b) in enumerate(
            ((lp, ln, left_new, g, gt), (rp, rn, right_new, gt, g))
        ):
            prod = mm(a, b)
            loads[2 * j + n].wait()
            new[j] = jnp.where(on, prev[j] + prod, 0.0)
            copy = pltpu.make_async_copy(new.at[j], out.at[j], out_sem.at[2 * j + n])
            copy.start()
            stores.append(copy)
    for copy in stores:
        copy.wait()


def tables(block_owner, block_row, block_col):
    count = block_owner.shape[0]
    index = jnp.arange(count, dtype=jnp.int32)
    earlier = (block_owner[:, None] == block_owner[None, :]) & (index[None, :] < index[:, None])
    slot = 2 * block_owner + jnp.sum(earlier.astype(jnp.int32), axis=1)
    cell = block_row // BLK * COLB + block_col // BLK
    at_slot = (slot[None, :] == jnp.arange(2 * SHARDS, dtype=jnp.int32)[:, None]).astype(jnp.int32)
    at_cell = (cell[None, :] == jnp.arange(CELLS, dtype=jnp.int32)[:, None]).astype(jnp.int32)
    cell_of_slot = jnp.sum(at_slot * cell[None, :], axis=1)
    live = jnp.sum(at_slot, axis=1)
    slot_of_cell = jnp.sum(at_cell * slot[None, :], axis=1)
    return cell_of_slot, live, slot_of_cell


SMEM = pl.BlockSpec(memory_space=pltpu.SMEM)
VMEM = pl.BlockSpec(memory_space=pltpu.VMEM)
ANY = pl.BlockSpec(memory_space=pl.ANY)
DMA = pltpu.SemaphoreType.DMA


def body(grads, left_prev, right_prev, block_owner, block_row, block_col):
    cell_of_slot, live, slot_of_cell = tables(block_owner, block_row, block_col)
    rows = grads.shape[1]
    direction, gathered = pl.pallas_call(
        step_kernel,
        out_shape=(
            jax.ShapeDtypeStruct((TILES, 2, SUB, COLB * BLK), BF),
            jax.ShapeDtypeStruct((HALF, 2, 2, SUB, BLK), BF),
        ),
        in_specs=[SMEM, SMEM, SMEM, ANY, ANY, ANY],
        out_specs=(VMEM, VMEM),
        scratch_shapes=[
            pltpu.VMEM((TILES, SUB, COLB * BLK), BF),
            pltpu.VMEM((TILES, SUB, COLB * BLK), BF),
            pltpu.VMEM((XS, TILES, COLB, SUB, LANE), BF),
            pltpu.VMEM((XS - 1, TILES, COLB, SUB, LANE), BF),
            pltpu.VMEM((TILES, COLB, SUB, LANE), BF),
            pltpu.VMEM((CELLS, SUB, LANE), BF),
            pltpu.VMEM((HALF, 2, SUB, LANE), BF),
            pltpu.VMEM((2, BLK, BLK), F32),
            pltpu.VMEM((2, BLK, BLK), F32),
            pltpu.VMEM((HALF, 2, SUB, BLK), BF),
            pltpu.VMEM((HALF, 2, SUB, LANE), BF),
            pltpu.VMEM((2 * HALF, SUB, LANE), BF),
            pltpu.VMEM((ROWB, COLB, SUB, LANE), BF),
            pltpu.VMEM((2, TILES, COLB, SUB, LANE), BF),
            pltpu.VMEM((COLB, TILES, 2, SUB, BLK), BF),
            DMA, DMA((2,)), DMA((3,)), DMA((3,)), DMA((10,)), DMA, DMA((16,)), DMA, DMA((7,)), DMA((7,)), DMA((4,)),
            DMA((16,)), DMA, DMA((10,)), DMA, DMA((7,)), DMA((7,)),
        ],
        compiler_params=pltpu.CompilerParams(
            collective_id=0, has_side_effects=True, vmem_limit_bytes=58 * 1024 * 1024
        ),
        name="shampoo_step",
    )(cell_of_slot, live, slot_of_cell, grads.reshape(TILES, 2, SUB, COLB * BLK), left_prev, right_prev)

    sq = jax.ShapeDtypeStruct((2, BLK, BLK), F32)
    left_new, right_new = pl.pallas_call(
        factors_kernel,
        out_shape=(sq, sq),
        in_specs=[SMEM, VMEM, ANY, ANY],
        out_specs=(ANY, ANY),
        scratch_shapes=[pltpu.VMEM((2, BLK, BLK), F32)] * 4 + [DMA((4,)), DMA((4,))],
        compiler_params=pltpu.CompilerParams(vmem_limit_bytes=58 * 1024 * 1024),
        cost_estimate=pl.CostEstimate(flops=4 * 2 * BLK**3, bytes_accessed=8 * 2**20, transcendentals=0),
        name="new_factors",
    )(live, gathered, left_prev, right_prev)
    return direction.reshape(rows, COLB * BLK), left_new, right_new


def solution(mesh):
    in_specs = (P("rep", "shard", None), P("shard", None, None), P("shard", None, None), P(), P(), P())
    out_specs = (P("shard", None), P("shard", None, None), P("shard", None, None))
    return jax.shard_map(body, mesh=mesh, in_specs=in_specs, out_specs=out_specs, check_vma=False)
```

```python
import jax
import jax.numpy as jnp
from jax import lax
from jax.experimental import pallas as pl
from jax.experimental.pallas import tpu as pltpu
from jax.sharding import PartitionSpec as P

BLK = 512
COLB = 3
ROWB = 10
CELLS = 30
SHARDS = 32
HALF = 16
TILES = 5
LANE = 128
SUB = 16
XS = 4
MESH = pl.DeviceIdType.MESH
BF = jnp.bfloat16
F32 = jnp.float32


def place():
    rep = lax.axis_index("rep")
    shard = lax.axis_index("shard")
    x = rep // 2
    h = rep % 2
    return rep, shard, x, h


def send(src, dst, send_sem, recv_sem, rep, shard):
    return pltpu.make_async_remote_copy(
        src_ref=src,
        dst_ref=dst,
        send_sem=send_sem,
        recv_sem=recv_sem,
        device_id=(rep, shard),
        device_id_type=MESH,
    )


def greet(barrier, rep, shard):
    pl.semaphore_signal(barrier, inc=1, device_id=(rep, shard), device_id_type=MESH)


def eye(size):
    row = lax.broadcasted_iota(jnp.int32, (size, size), 0)
    col = lax.broadcasted_iota(jnp.int32, (size, size), 1)
    return row == col


def mm(a, b):
    return jnp.dot(a, b, preferred_element_type=F32)


def root_less_one(new, scale):
    diag = eye(BLK)
    e = 0.25 * (jnp.where(diag, 1.0, 0.0) - new * (1.0 / scale))
    eb = e.astype(BF)
    u = 2.0 * e + mm(eb, eb)
    ub = u.astype(BF)
    v = 2.0 * u + mm(ub, ub)
    w = 4.0 * u - 5.0 * e
    z = (u - 0.25 * v) + 0.25 * mm(v.astype(BF), w.astype(BF))
    return z.astype(BF)


def step_kernel(
    cell_of_slot, slot_of_cell, grads, left_prev, right_prev, d_out, g_own,
    own, pair, part, xin, red, pvf, pvb, pm, po, pv, gc, mid, outb, acc, zb, scl, pb, full,
    own_sem, pvf_sem, pair_sem, xs_sem, xr_sem, p1_sem, p1r_sem, p2_sem, p2r_sem, gs_sem, gr_sem, ge_sem,
    t1_sem, t1r_sem, t2_sem, t2r_sem, os_sem, or_sem, z_sem, ss_sem, sr_sem, ds_sem, dr_sem, ready,
):
    rep = lax.axis_index("rep")
    shard = lax.axis_index("shard")
    x = rep // 2
    h = rep % 2
    half = shard // HALF
    w = shard % HALF
    r = w // 3
    j = w % 3
    partner = 2 * x + 1 - h
    summing = x < COLB
    home = summing & (j == 1)
    passing = half == h
    lanes = pl.ds(pl.multiple_of(x * LANE, LANE), LANE)
    barrier = pltpu.get_barrier_semaphore()

    def pass_on(src, dst, send_sem, recv_sem, to_rep, to_shard):
        me = (to_rep == rep) & (to_shard == shard)

        @pl.when(jnp.logical_not(me))
        def _():
            send(src, dst, send_sem, recv_sem, to_rep, to_shard).start()

        @pl.when(me)
        def _():
            pltpu.make_async_copy(src, dst, recv_sem).start()

    def passed(src, send_sem, recv_sem, to_rep, to_shard):
        me = (to_rep == rep) & (to_shard == shard)

        @pl.when(jnp.logical_not(me))
        def _():
            send(src, src, send_sem, recv_sem, to_rep, to_shard).wait_send()

    def arrived(ref, sem):
        pltpu.make_async_copy(ref, ref, sem).wait()

    def loop(count, fn):
        def step(n, carry):
            fn(n)
            return carry

        lax.fori_loop(0, count, step, 0)

    load = pltpu.make_async_copy(grads.at[:, h], own, own_sem)
    load.start()

    @pl.when(h == 0)
    def _():
        pltpu.make_async_copy(left_prev.at[:, :, :, lanes], pvf, pvf_sem).start()

    @pl.when(h == 1)
    def _():
        pltpu.make_async_copy(right_prev.at[:, :, :, lanes], pvf, pvf_sem).start()

    loop(SHARDS - 1, lambda n: greet(barrier, rep, (shard + 1 + n) % SHARDS))
    for n in range(1, XS):
        greet(barrier, 2 * ((x + n) % XS) + h, shard)
    greet(barrier, partner, shard)
    arrived(pvf, pvf_sem)
    for n in range(2):
        pvb[:, n] = pvf[n].astype(BF)
    pl.semaphore_wait(barrier, SHARDS - 1 + XS)

    swap = send(grads.at[:, 1 - h], pair, pair_sem.at[0], pair_sem.at[1], partner, shard)
    swap.start()
    for n in range(1, XS):
        pl.semaphore_signal(
            ready, inc=1, device_id=(2 * ((x + n) % XS) + h, shard), device_id_type=MESH
        )
    mine = pm.at[pl.ds(2 * shard, 2)]
    loop(SHARDS, lambda t: pass_on(pvb.at[t], mine, p1_sem.at[t], p1r_sem, rep, t))

    load.wait()
    swap.wait_recv()
    for c in range(COLB):
        cols = slice(c * BLK, (c + 1) * BLK)
        part[c] = (own[:, :, cols].astype(F32) + pair[:, :, cols].astype(F32)).astype(BF)
    for c in range(COLB):

        @pl.when(x != c)
        def _():
            n = (c - x + XS) % XS - 1
            send(part.at[c], xin.at[n], xs_sem.at[c], xr_sem.at[n], 2 * c + h, shard).start()

    arrived(pm, p1r_sem)
    pl.semaphore_wait(ready, XS - 1)
    tile_at_home = pv.at[shard, :, lanes]

    def home_of(cell):
        row = cell // COLB
        return 2 * (cell % COLB) + h, HALF * (row // 5) + 3 * (row % 5) + 1

    def give_factor(cell):
        po[cell] = pm[slot_of_cell[cell]]
        to_rep, to_shard = home_of(cell)
        pass_on(po.at[cell], tile_at_home, p2_sem.at[cell], p2r_sem, to_rep, to_shard)

    loop(CELLS, give_factor)

    def to_homes(act):
        @pl.when(j == 2)
        def _():
            act(0, red, gc.at[pl.ds(10 - r, TILES), h], shard - 1)

        for n in range(6):

            @pl.when((j == 0) & (r == n))
            def _():
                if n > 0:
                    act(0, red.at[0:n], gc.at[16 - n:16, h], shard - 2)
                if n < TILES:
                    act(1, red.at[n:TILES], gc.at[0:TILES - n, h], shard + 1)

    def passing_tile(n):
        u = TILES * w + n // XS
        q = n % XS
        src = red.at[n // XS, :, pl.ds(pl.multiple_of(q * LANE, LANE), LANE)]
        return src, mid.at[COLB * (5 * half + u // HALF) + x], 2 * q + h, HALF * h + u % HALF

    @pl.when(summing)
    def _():
        for n in range(XS - 1):
            arrived(xin.at[n], xr_sem.at[n])
        red[...] = (
            (part[x].astype(F32) + xin[0].astype(F32)) + (xin[1].astype(F32) + xin[2].astype(F32))
        ).astype(BF)
        to_homes(lambda n, src, dst, to: send(src, dst, gs_sem.at[n], gr_sem, rep, to).start())

        @pl.when(j == 1)
        def _():
            pltpu.make_async_copy(red, gc.at[pl.ds(TILES - r, TILES), h], gr_sem).start()

        def give_tile(n):
            src, dst, to_rep, to_shard = passing_tile(n)
            pass_on(src, dst, t1_sem.at[n], t1r_sem, to_rep, to_shard)

        loop(TILES * XS, give_tile)

    half_block = send(gc.at[:, h], gc.at[:, h], ge_sem.at[0], ge_sem.at[1], partner, shard)

    @pl.when(home)
    def _():
        arrived(gc.at[:, h], gr_sem)
        half_block.start()

    def view(hh, col):
        return g_own.at[:, :, hh, :, pl.ds(pl.multiple_of(col * LANE, LANE), LANE)]

    @pl.when(passing)
    def _():
        arrived(mid, t1r_sem)

        def give_slots(o):
            for n in range(2):
                outb[o, n] = mid[cell_of_slot[2 * o + n]]
            pass_on(outb.at[o], g_own.at[w, :, h, :, lanes], t2_sem.at[o], t2r_sem, rep, o)

        loop(SHARDS, give_slots)

    root = send(zb.at[h], zb.at[h], z_sem.at[0], z_sem.at[1], partner, shard)
    root_scale = send(scl.at[h], scl.at[h], z_sem.at[2], z_sem.at[3], partner, shard)

    def to_rows(act, n):
        act(0, pb.at[0:TILES - n, h], full.at[x, n:TILES, h], shard - 1)
        act(1, pb.at[10 - n:15 - n, h], full.at[x, :, h], shard + 1)
        act(2, pb.at[15 - n:16, h], full.at[x, 0:1 + n, h], shard + 2)

    @pl.when(home)
    def _():
        other = gc.at[:, 1 - h]
        arrived(other, ge_sem.at[1])
        g = gc[...].reshape(BLK, BLK)
        gt = g.T
        arrived(pv, p2r_sem)

        @pl.when(h == 0)
        def _():
            acc[...] = mm(g, gt)

        @pl.when(h == 1)
        def _():
            acc[...] = mm(gt, g)

        val = acc[...] + pv[...].reshape(BLK, BLK).astype(F32)
        scale = jnp.sum(jnp.where(eye(BLK), val, 0.0)) * (1.0 / BLK)
        zb[h] = root_less_one(val, scale)
        scl[h] = lax.rsqrt(jnp.sqrt(jnp.full((8, LANE), scale, F32)))
        root.start()
        root_scale.start()
        gf = g.astype(F32)
        sg = jnp.full((8, LANE), jnp.sum(gf * gf), F32)
        arrived(zb.at[1 - h], z_sem.at[1])
        arrived(scl.at[1 - h], z_sem.at[3])
        y = scl[0, 0:1, 0:1] * (gf + mm(zb[0], g))
        p = scl[1, 0:1, 0:1] * (y + mm(y.astype(BF), zb[1]))
        sp = jnp.full((8, LANE), jnp.sum(p * p), F32)
        ratio = jnp.sqrt(sg / (sp + 1e-06))[0:1, 0:1]
        pb[...] = (p * ratio).astype(BF).reshape(HALF, 2, SUB, BLK)
        for n in range(TILES):

            @pl.when(r == n)
            def _():
                to_rows(lambda i, src, dst, to: send(src, dst, ss_sem.at[i], sr_sem, rep, to).start(), n)
                pltpu.make_async_copy(pb.at[5 - n:10 - n, h], full.at[x, :, h], sr_sem).start()

    owned = view(h, x)
    arrived(owned, t2r_sem)
    outs = []
    for n in (2, 1, 3):
        outs.append(send(owned, owned, os_sem.at[n], or_sem.at[n], 2 * ((x + n) % XS) + h, shard))
    outs.append(send(owned, owned, os_sem.at[0], or_sem.at[0], partner, shard))
    for copy in outs:
        copy.start()

    rows = full.at[x, :, h]
    row_sends = [
        send(rows, rows, ds_sem.at[n], dr_sem.at[x], 2 * ((x + n) % XS) + h, shard) for n in (2, 1, 3)
    ]
    row_sends.append(send(rows, rows, ds_sem.at[0], dr_sem.at[COLB + x], partner, shard))

    @pl.when(summing)
    def _():
        arrived(rows, sr_sem)
        for copy in row_sends:
            copy.start()

    for n in (1, 3, 2):
        piece = view(h, (x + XS - n) % XS)
        arrived(piece, or_sem.at[n])
        copy = send(piece, piece, os_sem.at[3 + n], or_sem.at[3 + n], partner, shard)
        copy.start()
        outs.append(copy)

    def onward(c):
        return send(
            full.at[c, :, h], full.at[c, :, h], ds_sem.at[XS + c], dr_sem.at[COLB + c], partner, shard
        )

    for c in range(COLB):

        @pl.when(x != c)
        def _():
            arrived(full.at[c, :, h], dr_sem.at[c])
            onward(c).start()

    for c in range(COLB):
        arrived(full.at[c, :, 1 - h], dr_sem.at[COLB + c])
        d_out[:, :, :, c * BLK:(c + 1) * BLK] = full[c]
    for index, n in ((0, 0), (4, 1), (6, 3), (5, 2)):
        arrived(view(1 - h, (x + XS - n) % XS), or_sem.at[index])

    swap.wait_send()
    loop(SHARDS, lambda t: passed(pvb.at[t], p1_sem.at[t], p1r_sem, rep, t))

    def gave_factor(cell):
        to_rep, to_shard = home_of(cell)
        passed(po.at[cell], p2_sem.at[cell], p2r_sem, to_rep, to_shard)

    loop(CELLS, gave_factor)
    for c in range(COLB):

        @pl.when(x != c)
        def _():
            n = (c - x + XS) % XS - 1
            send(part.at[c], xin.at[n], xs_sem.at[c], xr_sem.at[n], 2 * c + h, shard).wait_send()
            onward(c).wait_send()

    @pl.when(summing)
    def _():
        to_homes(lambda n, src, dst, to: send(src, dst, gs_sem.at[n], gr_sem, rep, to).wait_send())

        def gave_tile(n):
            src, _, to_rep, to_shard = passing_tile(n)
            passed(src, t1_sem.at[n], t1r_sem, to_rep, to_shard)

        loop(TILES * XS, gave_tile)
        for copy in row_sends:
            copy.wait_send()

    @pl.when(passing)
    def _():
        loop(SHARDS, lambda o: passed(outb.at[o], t2_sem.at[o], t2r_sem, rep, o))

    @pl.when(home)
    def _():
        half_block.wait_send()
        root.wait_send()
        root_scale.wait_send()
        for n in range(TILES):

            @pl.when(r == n)
            def _():
                to_rows(lambda i, src, dst, to: send(src, dst, ss_sem.at[i], sr_sem, rep, to).wait_send(), n)

    for copy in outs:
        copy.wait_send()


def factors_kernel(live, g_in, left_prev, right_prev, left_new, right_new, lp, rp, ln, rn, in_sem, out_sem):
    shard = lax.axis_index("shard")
    loads = []
    for j in range(2):
        for src, dst, n in ((left_prev, lp, 0), (right_prev, rp, 1)):
            copy = pltpu.make_async_copy(src.at[j], dst.at[j], in_sem.at[2 * j + n])
            copy.start()
            loads.append(copy)
    stores = []
    for j in range(2):
        on = live[2 * shard + j] > 0
        g = g_in[:, j].reshape(BLK, BLK)
        g = jnp.where(on, g, jnp.zeros_like(g))
        gt = g.T
        for n, (prev, new, out, a, b) in enumerate(
            ((lp, ln, left_new, g, gt), (rp, rn, right_new, gt, g))
        ):
            prod = mm(a, b)
            loads[2 * j + n].wait()
            new[j] = jnp.where(on, prev[j] + prod, 0.0)
            copy = pltpu.make_async_copy(new.at[j], out.at[j], out_sem.at[2 * j + n])
            copy.start()
            stores.append(copy)
    for copy in stores:
        copy.wait()


def tables(block_owner, block_row, block_col):
    count = block_owner.shape[0]
    index = jnp.arange(count, dtype=jnp.int32)
    earlier = (block_owner[:, None] == block_owner[None, :]) & (index[None, :] < index[:, None])
    slot = 2 * block_owner + jnp.sum(earlier.astype(jnp.int32), axis=1)
    cell = block_row // BLK * COLB + block_col // BLK
    at_slot = (slot[None, :] == jnp.arange(2 * SHARDS, dtype=jnp.int32)[:, None]).astype(jnp.int32)
    at_cell = (cell[None, :] == jnp.arange(CELLS, dtype=jnp.int32)[:, None]).astype(jnp.int32)
    cell_of_slot = jnp.sum(at_slot * cell[None, :], axis=1)
    live = jnp.sum(at_slot, axis=1)
    slot_of_cell = jnp.sum(at_cell * slot[None, :], axis=1)
    return cell_of_slot, live, slot_of_cell


SMEM = pl.BlockSpec(memory_space=pltpu.SMEM)
VMEM = pl.BlockSpec(memory_space=pltpu.VMEM)
ANY = pl.BlockSpec(memory_space=pl.ANY)
DMA = pltpu.SemaphoreType.DMA


def body(grads, left_prev, right_prev, block_owner, block_row, block_col):
    cell_of_slot, live, slot_of_cell = tables(block_owner, block_row, block_col)
    rows = grads.shape[1]
    direction, gathered = pl.pallas_call(
        step_kernel,
        out_shape=(
            jax.ShapeDtypeStruct((TILES, 2, SUB, COLB * BLK), BF),
            jax.ShapeDtypeStruct((HALF, 2, 2, SUB, BLK), BF),
        ),
        in_specs=[SMEM, SMEM, ANY, ANY, ANY],
        out_specs=(VMEM, VMEM),
        scratch_shapes=[
            pltpu.VMEM((TILES, SUB, COLB * BLK), BF),
            pltpu.VMEM((TILES, SUB, COLB * BLK), BF),
            pltpu.VMEM((COLB, TILES, SUB, BLK), BF),
            pltpu.VMEM((XS - 1, TILES, SUB, BLK), BF),
            pltpu.VMEM((TILES, SUB, BLK), BF),
            pltpu.VMEM((2, 2 * HALF, SUB, LANE), F32),
            pltpu.VMEM((2 * HALF, 2, SUB, LANE), BF),
            pltpu.VMEM((2 * SHARDS, SUB, LANE), BF),
            pltpu.VMEM((CELLS, SUB, LANE), BF),
            pltpu.VMEM((2 * HALF, SUB, BLK), BF),
            pltpu.VMEM((HALF, 2, SUB, BLK), BF),
            pltpu.VMEM((CELLS, SUB, LANE), BF),
            pltpu.VMEM((SHARDS, 2, SUB, LANE), BF),
            pltpu.VMEM((BLK, BLK), F32),
            pltpu.VMEM((2, BLK, BLK), BF),
            pltpu.VMEM((2, 8, LANE), F32),
            pltpu.VMEM((HALF, 2, SUB, BLK), BF),
            pltpu.VMEM((COLB, TILES, 2, SUB, BLK), BF),
            DMA, DMA, DMA((2,)), DMA((3,)), DMA((3,)),
            DMA((SHARDS,)), DMA, DMA((CELLS,)), DMA, DMA((2,)), DMA, DMA((2,)),
            DMA((TILES * XS,)), DMA, DMA((SHARDS,)), DMA, DMA((7,)), DMA((7,)),
            DMA((4,)), DMA((3,)), DMA, DMA((7,)), DMA((6,)), pltpu.SemaphoreType.REGULAR,
        ],
        compiler_params=pltpu.CompilerParams(
            collective_id=0, has_side_effects=True, vmem_limit_bytes=58 * 1024 * 1024
        ),
        name="shampoo_step",
    )(
        cell_of_slot,
        slot_of_cell,
        grads.reshape(TILES, 2, SUB, COLB * BLK),
        left_prev.reshape(2, 2 * HALF, SUB, BLK),
        right_prev.reshape(2, 2 * HALF, SUB, BLK),
    )

    sq = jax.ShapeDtypeStruct((2, BLK, BLK), F32)
    left_new, right_new = pl.pallas_call(
        factors_kernel,
        out_shape=(sq, sq),
        in_specs=[SMEM, VMEM, ANY, ANY],
        out_specs=(ANY, ANY),
        scratch_shapes=[pltpu.VMEM((2, BLK, BLK), F32)] * 4 + [DMA((4,)), DMA((4,))],
        compiler_params=pltpu.CompilerParams(vmem_limit_bytes=58 * 1024 * 1024),
        cost_estimate=pl.CostEstimate(flops=4 * 2 * BLK**3, bytes_accessed=8 * 2**20, transcendentals=0),
        name="new_factors",
    )(live, gathered, left_prev, right_prev)
    return direction.reshape(rows, COLB * BLK), left_new, right_new


def solution(mesh):
    in_specs = (P("rep", "shard", None), P("shard", None, None), P("shard", None, None), P(), P(), P())
    out_specs = (P("shard", None), P("shard", None, None), P("shard", None, None))
    return jax.shard_map(body, mesh=mesh, in_specs=in_specs, out_specs=out_specs, check_vma=False)
```

```python
import jax
import jax.numpy as jnp
from jax import lax
from jax.experimental import pallas as pl
from jax.experimental.pallas import tpu as pltpu
from jax.sharding import PartitionSpec as P

BLK = 512
COLB = 3
ROWB = 10
CELLS = 30
SHARDS = 32
HALF = 16
TILES = 5
LANE = 128
SUB = 16
XS = 4
MESH = pl.DeviceIdType.MESH
BF = jnp.bfloat16
F32 = jnp.float32


def place():
    rep = lax.axis_index("rep")
    shard = lax.axis_index("shard")
    x = rep // 2
    h = rep % 2
    return rep, shard, x, h


def send(src, dst, send_sem, recv_sem, rep, shard):
    return pltpu.make_async_remote_copy(
        src_ref=src,
        dst_ref=dst,
        send_sem=send_sem,
        recv_sem=recv_sem,
        device_id=(rep, shard),
        device_id_type=MESH,
    )


def greet(barrier, rep, shard):
    pl.semaphore_signal(barrier, inc=1, device_id=(rep, shard), device_id_type=MESH)


def eye(size):
    row = lax.broadcasted_iota(jnp.int32, (size, size), 0)
    col = lax.broadcasted_iota(jnp.int32, (size, size), 1)
    return row == col


def mm(a, b):
    return jnp.dot(a, b, preferred_element_type=F32)


def root_less_one(new, scale):
    diag = eye(BLK)
    e = 0.25 * (jnp.where(diag, 1.0, 0.0) - new * (1.0 / scale))
    eb = e.astype(BF)
    u = 2.0 * e + mm(eb, eb)
    ub = u.astype(BF)
    v = 2.0 * u + mm(ub, ub)
    w = 4.0 * u - 5.0 * e
    z = (u - 0.25 * v) + 0.25 * mm(v.astype(BF), w.astype(BF))
    return z.astype(BF)


def fill_tables(tab, block_owner, block_row, block_col):
    sub = lax.broadcasted_iota(jnp.int32, (32, LANE), 0)
    lane = lax.broadcasted_iota(jnp.int32, (32, LANE), 1)
    owner = jnp.full((32, LANE), -1, jnp.int32)
    other = jnp.full((32, LANE), -2, jnp.int32)
    cell = jnp.full((32, LANE), -1, jnp.int32)
    for b in range(CELLS):
        owner = jnp.where(sub == b, block_owner[b], owner)
        other = jnp.where(lane == b, block_owner[b], other)
        cell = jnp.where(sub == b, block_row[b] // BLK * COLB + block_col[b] // BLK, cell)
    earlier = ((owner == other) & (lane < sub)).astype(jnp.int32)
    slot = 2 * owner + jnp.sum(earlier, axis=1, keepdims=True)
    cells = jnp.sum(jnp.where(slot == lane, cell, 0), axis=0, keepdims=True)
    slots = jnp.sum(jnp.where(cell == lane, slot, 0), axis=0, keepdims=True)
    tab[0:1] = jnp.clip(cells, 0, CELLS - 1)
    tab[1:2] = jnp.clip(slots, 0, 2 * SHARDS - 1)


def step_kernel(
    block_owner, block_row, block_col, grads, left_prev, right_prev, d_out, g_out,
    g_own, own, pair, part, xin, red, pvf, pvb, pm, po, pv, gc, mid, outb, acc, zb, scl, pb, full, tab, look,
    own_sem, pvf_sem, pair_sem, xs_sem, xr_sem, p1_sem, p1r_sem, p2_sem, p2r_sem, gs_sem, gr_sem, ge_sem,
    t1_sem, t1r_sem, t2_sem, t2r_sem, os_sem, or_sem, z_sem, ss_sem, sr_sem, ds_sem, dr_sem, tab_sem, out_sem, ready,
):
    rep = lax.axis_index("rep")
    shard = lax.axis_index("shard")
    x = rep // 2
    h = rep % 2
    half = shard // HALF
    w = shard % HALF
    r = w // 3
    j = w % 3
    partner = 2 * x + 1 - h
    summing = x < COLB
    home = summing & (j == 1)
    passing = half == h
    lanes = pl.ds(pl.multiple_of(x * LANE, LANE), LANE)
    barrier = pltpu.get_barrier_semaphore()

    def pass_on(src, dst, send_sem, recv_sem, to_rep, to_shard):
        me = (to_rep == rep) & (to_shard == shard)

        @pl.when(jnp.logical_not(me))
        def _():
            send(src, dst, send_sem, recv_sem, to_rep, to_shard).start()

        @pl.when(me)
        def _():
            pltpu.make_async_copy(src, dst, recv_sem).start()

    def arrived(ref, sem):
        pltpu.make_async_copy(ref, ref, sem).wait()

    def loop(count, fn):
        def step(n, carry):
            fn(n)
            return carry

        lax.fori_loop(0, count, step, 0)

    load = pltpu.make_async_copy(grads.at[:, h], own, own_sem)
    load.start()

    @pl.when(h == 0)
    def _():
        pltpu.make_async_copy(left_prev.at[:, :, :, lanes], pvf, pvf_sem).start()

    @pl.when(h == 1)
    def _():
        pltpu.make_async_copy(right_prev.at[:, :, :, lanes], pvf, pvf_sem).start()

    loop(SHARDS - 1, lambda n: greet(barrier, rep, (shard + 1 + n) % SHARDS))
    for n in range(1, XS):
        greet(barrier, 2 * ((x + n) % XS) + h, shard)
    greet(barrier, partner, shard)
    fill_tables(tab, block_owner, block_row, block_col)
    tables = pltpu.make_async_copy(tab, look, tab_sem)
    tables.start()
    arrived(pvf, pvf_sem)
    for n in range(2):
        pvb[:, n] = pvf[n].astype(BF)
    pl.semaphore_wait(barrier, SHARDS - 1 + XS)

    tables.wait()
    swap = send(grads.at[:, 1 - h], pair, pair_sem.at[0], pair_sem.at[1], partner, shard)
    swap.start()
    for n in range(1, XS):
        pl.semaphore_signal(
            ready, inc=1, device_id=(2 * ((x + n) % XS) + h, shard), device_id_type=MESH
        )
    mine = pm.at[pl.ds(2 * shard, 2)]
    def give_old(n):
        t = (shard + 1 + n) % SHARDS
        send(pvb.at[t], mine, p1_sem, p1r_sem, rep, t).start()

    loop(SHARDS - 1, give_old)
    pltpu.make_async_copy(pvb.at[shard], mine, p1r_sem).start()

    load.wait()
    swap.wait_recv()
    for c in range(COLB):
        cols = slice(c * BLK, (c + 1) * BLK)
        part[c] = (own[:, :, cols].astype(F32) + pair[:, :, cols].astype(F32)).astype(BF)
    for c in range(COLB):

        @pl.when(x != c)
        def _():
            n = (c - x + XS) % XS - 1
            send(part.at[c], xin.at[n], xs_sem.at[c], xr_sem.at[n], 2 * c + h, shard).start()

    arrived(pm, p1r_sem)
    pl.semaphore_wait(ready, XS - 1)
    tile_at_home = pv.at[shard, :, lanes]

    def home_of(cell):
        row = cell // COLB
        return 2 * (cell % COLB) + h, HALF * (row // 5) + 3 * (row % 5) + 1

    own_cell = COLB * (5 * half + r) + x
    first = jnp.where(home, own_cell + 1, 0)

    def give_factor(n):
        cell = (first + n) % CELLS
        po[cell] = pm[look[1, cell]]
        to_rep, to_shard = home_of(cell)
        send(po.at[cell], tile_at_home, p2_sem, p2r_sem, to_rep, to_shard).start()

    loop(CELLS - home.astype(jnp.int32), give_factor)

    @pl.when(home)
    def _():
        po[own_cell] = pm[look[1, own_cell]]
        pltpu.make_async_copy(po.at[own_cell], tile_at_home, p2r_sem).start()


    def to_homes(act):
        @pl.when(j == 2)
        def _():
            act(0, red, gc.at[pl.ds(10 - r, TILES), h], shard - 1)

        for n in range(6):

            @pl.when((j == 0) & (r == n))
            def _():
                if n > 0:
                    act(0, red.at[0:n], gc.at[16 - n:16, h], shard - 2)
                if n < TILES:
                    act(1, red.at[n:TILES], gc.at[0:TILES - n, h], shard + 1)

    def passing_tile(n):
        u = TILES * w + n // XS
        q = n % XS
        src = red.at[n // XS, :, pl.ds(pl.multiple_of(q * LANE, LANE), LANE)]
        return src, mid.at[COLB * (5 * half + u // HALF) + x], 2 * q + h, HALF * h + u % HALF

    @pl.when(summing)
    def _():
        for n in range(XS - 1):
            arrived(xin.at[n], xr_sem.at[n])
        red[...] = (
            (part[x].astype(F32) + xin[0].astype(F32)) + (xin[1].astype(F32) + xin[2].astype(F32))
        ).astype(BF)
        to_homes(lambda n, src, dst, to: send(src, dst, gs_sem.at[n], gr_sem, rep, to).start())

        @pl.when(j == 1)
        def _():
            pltpu.make_async_copy(red, gc.at[pl.ds(TILES - r, TILES), h], gr_sem).start()

        def give_tile(n):
            src, dst, to_rep, to_shard = passing_tile(n)
            pass_on(src, dst, t1_sem, t1r_sem, to_rep, to_shard)

        loop(TILES * XS, give_tile)

    half_block = send(gc.at[:, h], gc.at[:, h], ge_sem.at[0], ge_sem.at[1], partner, shard)

    @pl.when(home)
    def _():
        arrived(gc.at[:, h], gr_sem)
        half_block.start()

    def view(hh, col):
        return g_own.at[:, :, hh, :, pl.ds(pl.multiple_of(col * LANE, LANE), LANE)]

    @pl.when(passing)
    def _():
        arrived(mid, t1r_sem)

        def fill(o):
            for n in range(2):
                outb[o, n] = mid[look[0, 2 * o + n]]

        slots_at_owner = g_own.at[w, :, h, :, lanes]

        def give_slots(n):
            o = (shard + 1 + n) % SHARDS
            fill(o)
            send(outb.at[o], slots_at_owner, t2_sem, t2r_sem, rep, o).start()

        loop(SHARDS - 1, give_slots)
        fill(shard)
        pltpu.make_async_copy(outb.at[shard], slots_at_owner, t2r_sem).start()

    root = send(zb.at[h], zb.at[h], z_sem.at[0], z_sem.at[1], partner, shard)
    root_scale = send(scl.at[h], scl.at[h], z_sem.at[2], z_sem.at[3], partner, shard)

    def to_rows(act, n):
        act(0, pb.at[0:TILES - n, h], full.at[x, n:TILES, h], shard - 1)
        act(1, pb.at[10 - n:15 - n, h], full.at[x, :, h], shard + 1)
        act(2, pb.at[15 - n:16, h], full.at[x, 0:1 + n, h], shard + 2)

    @pl.when(home)
    def _():
        other = gc.at[:, 1 - h]
        arrived(other, ge_sem.at[1])
        g = gc[...].reshape(BLK, BLK)
        gt = g.T
        arrived(pv, p2r_sem)

        @pl.when(h == 0)
        def _():
            acc[...] = mm(g, gt)

        @pl.when(h == 1)
        def _():
            acc[...] = mm(gt, g)

        val = acc[...] + pv[...].reshape(BLK, BLK).astype(F32)
        scale = jnp.sum(jnp.where(eye(BLK), val, 0.0)) * (1.0 / BLK)
        zb[h] = root_less_one(val, scale)
        scl[h] = lax.rsqrt(jnp.sqrt(jnp.full((8, LANE), scale, F32)))
        root.start()
        root_scale.start()
        gf = g.astype(F32)
        sg = jnp.full((8, LANE), jnp.sum(gf * gf), F32)
        arrived(zb.at[1 - h], z_sem.at[1])
        arrived(scl.at[1 - h], z_sem.at[3])
        y = scl[0, 0:1, 0:1] * (gf + mm(zb[0], g))
        p = scl[1, 0:1, 0:1] * (y + mm(y.astype(BF), zb[1]))
        sp = jnp.full((8, LANE), jnp.sum(p * p), F32)
        ratio = jnp.sqrt(sg / (sp + 1e-06))[0:1, 0:1]
        pb[...] = (p * ratio).astype(BF).reshape(HALF, 2, SUB, BLK)
        for n in range(TILES):

            @pl.when(r == n)
            def _():
                to_rows(lambda i, src, dst, to: send(src, dst, ss_sem.at[i], sr_sem, rep, to).start(), n)
                pltpu.make_async_copy(pb.at[5 - n:10 - n, h], full.at[x, :, h], sr_sem).start()

    owned = view(h, x)
    arrived(owned, t2r_sem)
    outs = []
    for n in (2, 1, 3):
        outs.append(send(owned, owned, os_sem.at[n], or_sem.at[n], 2 * ((x + n) % XS) + h, shard))
    outs.append(send(owned, owned, os_sem.at[0], or_sem.at[0], partner, shard))
    for copy in outs:
        copy.start()

    rows = full.at[x, :, h]
    row_sends = [
        send(rows, rows, ds_sem.at[n], dr_sem.at[x], 2 * ((x + n) % XS) + h, shard) for n in (2, 1, 3)
    ]
    row_sends.append(send(rows, rows, ds_sem.at[0], dr_sem.at[COLB + x], partner, shard))

    @pl.when(summing)
    def _():
        arrived(rows, sr_sem)
        for copy in row_sends:
            copy.start()

    for n in (1, 3, 2):
        piece = view(h, (x + XS - n) % XS)
        arrived(piece, or_sem.at[n])
        copy = send(piece, piece, os_sem.at[3 + n], or_sem.at[3 + n], partner, shard)
        copy.start()
        outs.append(copy)

    def onward(c):
        return send(
            full.at[c, :, h], full.at[c, :, h], ds_sem.at[XS + c], dr_sem.at[COLB + c], partner, shard
        )

    for c in range(COLB):

        @pl.when(x != c)
        def _():
            arrived(full.at[c, :, h], dr_sem.at[c])
            onward(c).start()

    for index, n in ((0, 0), (4, 1), (6, 3), (5, 2)):
        arrived(view(1 - h, (x + XS - n) % XS), or_sem.at[index])
    g_store = pltpu.make_async_copy(g_own, g_out, out_sem.at[COLB])
    g_store.start()
    d_stores = []
    for c in range(COLB):
        arrived(full.at[c, :, 1 - h], dr_sem.at[COLB + c])
        copy = pltpu.make_async_copy(full.at[c], d_out.at[:, :, :, pl.ds(c * BLK, BLK)], out_sem.at[c])
        copy.start()
        d_stores.append(copy)

    swap.wait_send()
    arrived(pvb.at[0:SHARDS - 1], p1_sem)

    @pl.when(home)
    def _():
        arrived(po.at[0:CELLS - 1], p2_sem)

    @pl.when(jnp.logical_not(home))
    def _():
        arrived(po, p2_sem)

    for c in range(COLB):

        @pl.when(x != c)
        def _():
            n = (c - x + XS) % XS - 1
            send(part.at[c], xin.at[n], xs_sem.at[c], xr_sem.at[n], 2 * c + h, shard).wait_send()
            onward(c).wait_send()

    @pl.when(summing)
    def _():
        to_homes(lambda n, src, dst, to: send(src, dst, gs_sem.at[n], gr_sem, rep, to).wait_send())

        kept = passing & ((12 * w) % HALF < TILES)

        @pl.when(kept)
        def _():
            arrived(mid.at[0:TILES * XS - 1], t1_sem)

        @pl.when(jnp.logical_not(kept))
        def _():
            arrived(mid.at[0:TILES * XS], t1_sem)

        for copy in row_sends:
            copy.wait_send()

    @pl.when(passing)
    def _():
        arrived(outb.at[0:SHARDS - 1], t2_sem)

    @pl.when(home)
    def _():
        half_block.wait_send()
        root.wait_send()
        root_scale.wait_send()
        for n in range(TILES):

            @pl.when(r == n)
            def _():
                to_rows(lambda i, src, dst, to: send(src, dst, ss_sem.at[i], sr_sem, rep, to).wait_send(), n)

    for copy in outs:
        copy.wait_send()
    g_store.wait()
    for copy in d_stores:
        copy.wait()


def finish_kernel(block_owner, d_in, g_in, left_prev, right_prev, d_out, left_new, right_new,
                  db, gb, lp, rp, ln, rn, d_sem, in_sem, out_sem):
    shard = lax.axis_index("shard")
    loads = []
    for j in range(2):
        for src, dst, n in ((g_in, gb, 2), (left_prev, lp, 0), (right_prev, rp, 1)):
            if n == 2:
                copy = pltpu.make_async_copy(src.at[:, j], dst.at[:, j], in_sem.at[3 * j + n])
            else:
                copy = pltpu.make_async_copy(src.at[j], dst.at[j], in_sem.at[3 * j + n])
            copy.start()
            loads.append(copy)
    d_load = pltpu.make_async_copy(d_in, db, d_sem.at[0])
    d_load.start()
    held = lax.fori_loop(0, CELLS, lambda b, n: n + (block_owner[b] == shard).astype(jnp.int32), 0)
    stores = []
    for j in range(2):
        on = held > j
        loads[3 * j].wait()
        g = gb[:, j].reshape(BLK, BLK)
        g = jnp.where(on, g, jnp.zeros_like(g))
        gt = g.T
        for n, (prev, new, out, a, b) in enumerate(
            ((lp, ln, left_new, g, gt), (rp, rn, right_new, gt, g))
        ):
            prod = mm(a, b)
            loads[3 * j + 1 + n].wait()
            new[j] = jnp.where(on, prev[j] + prod, 0.0)
            copy = pltpu.make_async_copy(new.at[j], out.at[j], out_sem.at[2 * j + n])
            copy.start()
            stores.append(copy)
    d_load.wait()
    d_store = pltpu.make_async_copy(db, d_out, d_sem.at[1])
    d_store.start()
    d_store.wait()
    for copy in stores:
        copy.wait()


SMEM = pl.BlockSpec(memory_space=pltpu.SMEM)
VMEM = pl.BlockSpec(memory_space=pltpu.VMEM)
ANY = pl.BlockSpec(memory_space=pl.ANY)
DMA = pltpu.SemaphoreType.DMA


def body(grads, left_prev, right_prev, block_owner, block_row, block_col):
    rows = grads.shape[1]
    direction, gathered = pl.pallas_call(
        step_kernel,
        out_shape=(
            jax.ShapeDtypeStruct((TILES, 2, SUB, COLB * BLK), BF),
            jax.ShapeDtypeStruct((HALF, 2, 2, SUB, BLK), BF),
        ),
        in_specs=[SMEM, SMEM, SMEM, ANY, ANY, ANY],
        out_specs=(ANY, ANY),
        scratch_shapes=[
            pltpu.VMEM((HALF, 2, 2, SUB, BLK), BF),
            pltpu.VMEM((TILES, SUB, COLB * BLK), BF),
            pltpu.VMEM((TILES, SUB, COLB * BLK), BF),
            pltpu.VMEM((COLB, TILES, SUB, BLK), BF),
            pltpu.VMEM((XS - 1, TILES, SUB, BLK), BF),
            pltpu.VMEM((TILES, SUB, BLK), BF),
            pltpu.VMEM((2, 2 * HALF, SUB, LANE), F32),
            pltpu.VMEM((2 * HALF, 2, SUB, LANE), BF),
            pltpu.VMEM((2 * SHARDS, SUB, LANE), BF),
            pltpu.VMEM((CELLS, SUB, LANE), BF),
            pltpu.VMEM((2 * HALF, SUB, BLK), BF),
            pltpu.VMEM((HALF, 2, SUB, BLK), BF),
            pltpu.VMEM((CELLS, SUB, LANE), BF),
            pltpu.VMEM((SHARDS, 2, SUB, LANE), BF),
            pltpu.VMEM((BLK, BLK), F32),
            pltpu.VMEM((2, BLK, BLK), BF),
            pltpu.VMEM((2, 8, LANE), F32),
            pltpu.VMEM((HALF, 2, SUB, BLK), BF),
            pltpu.VMEM((COLB, TILES, 2, SUB, BLK), BF),
            pltpu.VMEM((8, LANE), jnp.int32),
            pltpu.SMEM((8, LANE), jnp.int32),
            DMA, DMA, DMA((2,)), DMA((3,)), DMA((3,)),
            DMA, DMA, DMA, DMA, DMA((2,)), DMA, DMA((2,)), DMA, DMA, DMA, DMA, DMA((7,)), DMA((7,)),
            DMA((4,)), DMA((3,)), DMA, DMA((7,)), DMA((6,)), DMA, DMA((4,)), pltpu.SemaphoreType.REGULAR,
        ],
        compiler_params=pltpu.CompilerParams(
            collective_id=0, has_side_effects=True, vmem_limit_bytes=58 * 1024 * 1024
        ),
        name="shampoo_step",
    )(
        block_owner,
        block_row,
        block_col,
        grads.reshape(TILES, 2, SUB, COLB * BLK),
        left_prev.reshape(2, 2 * HALF, SUB, BLK),
        right_prev.reshape(2, 2 * HALF, SUB, BLK),
    )

    rows_t = jax.ShapeDtypeStruct((TILES, 2, SUB, COLB * BLK), BF)
    sq = jax.ShapeDtypeStruct((2, BLK, BLK), F32)
    direction, left_new, right_new = pl.pallas_call(
        finish_kernel,
        out_shape=(rows_t, sq, sq),
        in_specs=[SMEM, ANY, ANY, ANY, ANY],
        out_specs=(ANY, ANY, ANY),
        scratch_shapes=[
            pltpu.VMEM((TILES, 2, SUB, COLB * BLK), BF),
            pltpu.VMEM((HALF, 2, 2, SUB, BLK), BF),
        ]
        + [pltpu.VMEM((2, BLK, BLK), F32)] * 4
        + [DMA((2,)), DMA((6,)), DMA((4,))],
        compiler_params=pltpu.CompilerParams(vmem_limit_bytes=58 * 1024 * 1024),
        cost_estimate=pl.CostEstimate(flops=4 * 2 * BLK**3, bytes_accessed=10 * 2**20, transcendentals=0),
        name="new_factors",
    )(block_owner, direction, gathered, left_prev, right_prev)
    return direction.reshape(rows, COLB * BLK), left_new, right_new


def solution(mesh):
    in_specs = (P("rep", "shard", None), P("shard", None, None), P("shard", None, None), P(), P(), P())
    out_specs = (P("shard", None), P("shard", None, None), P("shard", None, None))
    return jax.shard_map(body, mesh=mesh, in_specs=in_specs, out_specs=out_specs, check_vma=False)
```

```python
import jax
import jax.numpy as jnp
from jax import lax
from jax.experimental import pallas as pl
from jax.experimental.pallas import tpu as pltpu
from jax.sharding import PartitionSpec as P

BLK = 512
COLB = 3
ROWB = 10
CELLS = 30
SHARDS = 32
HALF = 16
TILES = 5
LANE = 128
SUB = 16
XS = 4
MESH = pl.DeviceIdType.MESH
BF = jnp.bfloat16
F32 = jnp.float32


def place():
    rep = lax.axis_index("rep")
    shard = lax.axis_index("shard")
    x = rep // 2
    h = rep % 2
    return rep, shard, x, h


def send(src, dst, send_sem, recv_sem, rep, shard):
    return pltpu.make_async_remote_copy(
        src_ref=src,
        dst_ref=dst,
        send_sem=send_sem,
        recv_sem=recv_sem,
        device_id=(rep, shard),
        device_id_type=MESH,
    )


def greet(barrier, rep, shard):
    pl.semaphore_signal(barrier, inc=1, device_id=(rep, shard), device_id_type=MESH)


def eye(size):
    row = lax.broadcasted_iota(jnp.int32, (size, size), 0)
    col = lax.broadcasted_iota(jnp.int32, (size, size), 1)
    return row == col


def mm(a, b):
    return jnp.dot(a, b, preferred_element_type=F32)


def root_less_one(new, scale):
    diag = eye(BLK)
    e = 0.25 * (jnp.where(diag, 1.0, 0.0) - new * (1.0 / scale))
    eb = e.astype(BF)
    u = 2.0 * e + mm(eb, eb)
    ub = u.astype(BF)
    v = 2.0 * u + mm(ub, ub)
    w = 4.0 * u - 5.0 * e
    z = (u - 0.25 * v) + 0.25 * mm(v.astype(BF), w.astype(BF))
    return z.astype(BF)


def fill_tables(tab, block_owner, block_row, block_col):
    sub = lax.broadcasted_iota(jnp.int32, (32, LANE), 0)
    lane = lax.broadcasted_iota(jnp.int32, (32, LANE), 1)
    owner = jnp.full((32, LANE), -1, jnp.int32)
    other = jnp.full((32, LANE), -2, jnp.int32)
    cell = jnp.full((32, LANE), -1, jnp.int32)
    for b in range(CELLS):
        owner = jnp.where(sub == b, block_owner[b], owner)
        other = jnp.where(lane == b, block_owner[b], other)
        cell = jnp.where(sub == b, block_row[b] // BLK * COLB + block_col[b] // BLK, cell)
    earlier = ((owner == other) & (lane < sub)).astype(jnp.int32)
    slot = 2 * owner + jnp.sum(earlier, axis=1, keepdims=True)
    cells = jnp.sum(jnp.where(slot == lane, cell, 0), axis=0, keepdims=True)
    slots = jnp.sum(jnp.where(cell == lane, slot, 0), axis=0, keepdims=True)
    tab[0:1] = jnp.clip(cells, 0, CELLS - 1)
    tab[1:2] = jnp.clip(slots, 0, 2 * SHARDS - 1)
    tab[2:3] = jnp.sum((slot == lane).astype(jnp.int32), axis=0, keepdims=True)


def step_kernel(
    block_owner, block_row, block_col, grads, left_prev, right_prev, d_out, left_out, right_out,
    g_own, lp, rp, own, pair, part, xin, red, pvf, pvb, pm, po, pv, gc, mid, outb, acc, zb, scl, pb, full, tab, look,
    own_sem, pvf_sem, pair_sem, xs_sem, xr_sem, p1_sem, p1r_sem, p2_sem, p2r_sem, gs_sem, gr_sem, ge_sem,
    t1_sem, t1r_sem, t2_sem, t2r_sem, os_sem, or_sem, z_sem, ss_sem, sr_sem, ds_sem, dr_sem, tab_sem, in_sem, ready,
):
    rep = lax.axis_index("rep")
    shard = lax.axis_index("shard")
    x = rep // 2
    h = rep % 2
    half = shard // HALF
    w = shard % HALF
    r = w // 3
    j = w % 3
    partner = 2 * x + 1 - h
    summing = x < COLB
    home = summing & (j == 1)
    passing = half == h
    lanes = pl.ds(pl.multiple_of(x * LANE, LANE), LANE)
    barrier = pltpu.get_barrier_semaphore()

    def pass_on(src, dst, send_sem, recv_sem, to_rep, to_shard):
        me = (to_rep == rep) & (to_shard == shard)

        @pl.when(jnp.logical_not(me))
        def _():
            send(src, dst, send_sem, recv_sem, to_rep, to_shard).start()

        @pl.when(me)
        def _():
            pltpu.make_async_copy(src, dst, recv_sem).start()

    def arrived(ref, sem):
        pltpu.make_async_copy(ref, ref, sem).wait()

    def loop(count, fn):
        def step(n, carry):
            fn(n)
            return carry

        lax.fori_loop(0, count, step, 0)

    load = pltpu.make_async_copy(grads.at[:, h], own, own_sem)
    load.start()

    @pl.when(h == 0)
    def _():
        pltpu.make_async_copy(left_prev.at[:, :, :, lanes], pvf, pvf_sem).start()

    @pl.when(h == 1)
    def _():
        pltpu.make_async_copy(right_prev.at[:, :, :, lanes], pvf, pvf_sem).start()

    whole = [
        pltpu.make_async_copy(left_prev, lp, in_sem.at[0]),
        pltpu.make_async_copy(right_prev, rp, in_sem.at[1]),
    ]
    for copy in whole:
        copy.start()
    loop(SHARDS - 1, lambda n: greet(barrier, rep, (shard + 1 + n) % SHARDS))
    for n in range(1, XS):
        greet(barrier, 2 * ((x + n) % XS) + h, shard)
    greet(barrier, partner, shard)
    fill_tables(tab, block_owner, block_row, block_col)
    tables = pltpu.make_async_copy(tab, look, tab_sem)
    tables.start()
    arrived(pvf, pvf_sem)
    for n in range(2):
        pvb[:, n] = pvf[n].astype(BF)
    pl.semaphore_wait(barrier, SHARDS - 1 + XS)

    tables.wait()
    swap = send(grads.at[:, 1 - h], pair, pair_sem.at[0], pair_sem.at[1], partner, shard)
    swap.start()
    for n in range(1, XS):
        pl.semaphore_signal(
            ready, inc=1, device_id=(2 * ((x + n) % XS) + h, shard), device_id_type=MESH
        )
    mine = pm.at[pl.ds(2 * shard, 2)]
    def give_old(n):
        t = (shard + 1 + n) % SHARDS
        send(pvb.at[t], mine, p1_sem, p1r_sem, rep, t).start()

    loop(SHARDS - 1, give_old)
    pltpu.make_async_copy(pvb.at[shard], mine, p1r_sem).start()

    load.wait()
    swap.wait_recv()
    for c in range(COLB):
        cols = slice(c * BLK, (c + 1) * BLK)
        part[c] = (own[:, :, cols].astype(F32) + pair[:, :, cols].astype(F32)).astype(BF)
    for c in range(COLB):

        @pl.when(x != c)
        def _():
            n = (c - x + XS) % XS - 1
            send(part.at[c], xin.at[n], xs_sem.at[c], xr_sem.at[n], 2 * c + h, shard).start()

    arrived(pm, p1r_sem)
    pl.semaphore_wait(ready, XS - 1)
    tile_at_home = pv.at[shard, :, lanes]

    def home_of(cell):
        row = cell // COLB
        return 2 * (cell % COLB) + h, HALF * (row // 5) + 3 * (row % 5) + 1

    own_cell = COLB * (5 * half + r) + x
    first = jnp.where(home, own_cell + 1, 0)

    def give_factor(n):
        cell = (first + n) % CELLS
        po[cell] = pm[look[1, cell]]
        to_rep, to_shard = home_of(cell)
        send(po.at[cell], tile_at_home, p2_sem, p2r_sem, to_rep, to_shard).start()

    loop(CELLS - home.astype(jnp.int32), give_factor)

    @pl.when(home)
    def _():
        po[own_cell] = pm[look[1, own_cell]]
        pltpu.make_async_copy(po.at[own_cell], tile_at_home, p2r_sem).start()


    def to_homes(act):
        @pl.when(j == 2)
        def _():
            act(0, red, gc.at[pl.ds(10 - r, TILES), h], shard - 1)

        for n in range(6):

            @pl.when((j == 0) & (r == n))
            def _():
                if n > 0:
                    act(0, red.at[0:n], gc.at[16 - n:16, h], shard - 2)
                if n < TILES:
                    act(1, red.at[n:TILES], gc.at[0:TILES - n, h], shard + 1)

    def passing_tile(n):
        u = TILES * w + n // XS
        q = n % XS
        src = red.at[n // XS, :, pl.ds(pl.multiple_of(q * LANE, LANE), LANE)]
        return src, mid.at[COLB * (5 * half + u // HALF) + x], 2 * q + h, HALF * h + u % HALF

    @pl.when(summing)
    def _():
        for n in range(XS - 1):
            arrived(xin.at[n], xr_sem.at[n])
        red[...] = (
            (part[x].astype(F32) + xin[0].astype(F32)) + (xin[1].astype(F32) + xin[2].astype(F32))
        ).astype(BF)
        to_homes(lambda n, src, dst, to: send(src, dst, gs_sem.at[n], gr_sem, rep, to).start())

        @pl.when(j == 1)
        def _():
            pltpu.make_async_copy(red, gc.at[pl.ds(TILES - r, TILES), h], gr_sem).start()

        def give_tile(n):
            src, dst, to_rep, to_shard = passing_tile(n)
            pass_on(src, dst, t1_sem, t1r_sem, to_rep, to_shard)

        loop(TILES * XS, give_tile)

    half_block = send(gc.at[:, h], gc.at[:, h], ge_sem.at[0], ge_sem.at[1], partner, shard)

    @pl.when(home)
    def _():
        arrived(gc.at[:, h], gr_sem)
        half_block.start()

    def view(hh, col):
        return g_own.at[:, :, hh, :, pl.ds(pl.multiple_of(col * LANE, LANE), LANE)]

    @pl.when(passing)
    def _():
        arrived(mid, t1r_sem)

        def fill(o):
            for n in range(2):
                outb[o, n] = mid[look[0, 2 * o + n]]

        slots_at_owner = g_own.at[w, :, h, :, lanes]

        def give_slots(n):
            o = (shard + 1 + n) % SHARDS
            fill(o)
            send(outb.at[o], slots_at_owner, t2_sem, t2r_sem, rep, o).start()

        loop(SHARDS - 1, give_slots)
        fill(shard)
        pltpu.make_async_copy(outb.at[shard], slots_at_owner, t2r_sem).start()

    root = send(zb.at[h], zb.at[h], z_sem.at[0], z_sem.at[1], partner, shard)
    root_scale = send(scl.at[h], scl.at[h], z_sem.at[2], z_sem.at[3], partner, shard)

    def to_rows(act, n):
        act(0, pb.at[0:TILES - n, h], full.at[x, n:TILES, h], shard - 1)
        act(1, pb.at[10 - n:15 - n, h], full.at[x, :, h], shard + 1)
        act(2, pb.at[15 - n:16, h], full.at[x, 0:1 + n, h], shard + 2)

    @pl.when(home)
    def _():
        other = gc.at[:, 1 - h]
        arrived(other, ge_sem.at[1])
        g = gc[...].reshape(BLK, BLK)
        gt = g.T
        arrived(pv, p2r_sem)

        @pl.when(h == 0)
        def _():
            acc[...] = mm(g, gt)

        @pl.when(h == 1)
        def _():
            acc[...] = mm(gt, g)

        val = acc[...] + pv[...].reshape(BLK, BLK).astype(F32)
        scale = jnp.sum(jnp.where(eye(BLK), val, 0.0)) * (1.0 / BLK)
        zb[h] = root_less_one(val, scale)
        scl[h] = lax.rsqrt(jnp.sqrt(jnp.full((8, LANE), scale, F32)))
        root.start()
        root_scale.start()
        gf = g.astype(F32)
        sg = jnp.full((8, LANE), jnp.sum(gf * gf), F32)
        arrived(zb.at[1 - h], z_sem.at[1])
        arrived(scl.at[1 - h], z_sem.at[3])
        y = scl[0, 0:1, 0:1] * (gf + mm(zb[0], g))
        p = scl[1, 0:1, 0:1] * (y + mm(y.astype(BF), zb[1]))
        sp = jnp.full((8, LANE), jnp.sum(p * p), F32)
        ratio = jnp.sqrt(sg / (sp + 1e-06))[0:1, 0:1]
        pb[...] = (p * ratio).astype(BF).reshape(HALF, 2, SUB, BLK)
        for n in range(TILES):

            @pl.when(r == n)
            def _():
                to_rows(lambda i, src, dst, to: send(src, dst, ss_sem.at[i], sr_sem, rep, to).start(), n)
                pltpu.make_async_copy(pb.at[5 - n:10 - n, h], full.at[x, :, h], sr_sem).start()

    owned = view(h, x)
    arrived(owned, t2r_sem)
    outs = []
    for n in (2, 1, 3):
        outs.append(send(owned, owned, os_sem.at[n], or_sem.at[n], 2 * ((x + n) % XS) + h, shard))
    outs.append(send(owned, owned, os_sem.at[0], or_sem.at[0], partner, shard))
    for copy in outs:
        copy.start()

    rows = full.at[x, :, h]
    row_sends = [
        send(rows, rows, ds_sem.at[n], dr_sem.at[x], 2 * ((x + n) % XS) + h, shard) for n in (2, 1, 3)
    ]
    row_sends.append(send(rows, rows, ds_sem.at[0], dr_sem.at[COLB + x], partner, shard))

    @pl.when(summing)
    def _():
        arrived(rows, sr_sem)
        for copy in row_sends:
            copy.start()

    for n in (1, 3, 2):
        piece = view(h, (x + XS - n) % XS)
        arrived(piece, or_sem.at[n])
        copy = send(piece, piece, os_sem.at[3 + n], or_sem.at[3 + n], partner, shard)
        copy.start()
        outs.append(copy)

    def onward(c):
        return send(
            full.at[c, :, h], full.at[c, :, h], ds_sem.at[XS + c], dr_sem.at[COLB + c], partner, shard
        )

    for c in range(COLB):

        @pl.when(x != c)
        def _():
            arrived(full.at[c, :, h], dr_sem.at[c])
            onward(c).start()

    for index, n in ((0, 0), (4, 1), (6, 3), (5, 2)):
        arrived(view(1 - h, (x + XS - n) % XS), or_sem.at[index])
    for copy in whole:
        copy.wait()

    def factors(n):
        on = look[2, 2 * shard + n] > 0
        g = g_own[:, n].reshape(BLK, BLK)
        g = jnp.where(on, g, jnp.zeros_like(g))
        gt = g.T
        for prev, out, a, b in ((lp, left_out, g, gt), (rp, right_out, gt, g)):
            new = prev[n].reshape(BLK, BLK) + mm(a, b)
            out[n] = jnp.where(on, new, jnp.zeros_like(new))

    loop(2, factors)
    for c in range(COLB):
        arrived(full.at[c, :, 1 - h], dr_sem.at[COLB + c])
        d_out[:, :, :, c * BLK:(c + 1) * BLK] = full[c]

    swap.wait_send()
    arrived(pvb.at[0:SHARDS - 1], p1_sem)

    @pl.when(home)
    def _():
        arrived(po.at[0:CELLS - 1], p2_sem)

    @pl.when(jnp.logical_not(home))
    def _():
        arrived(po, p2_sem)

    for c in range(COLB):

        @pl.when(x != c)
        def _():
            n = (c - x + XS) % XS - 1
            send(part.at[c], xin.at[n], xs_sem.at[c], xr_sem.at[n], 2 * c + h, shard).wait_send()
            onward(c).wait_send()

    @pl.when(summing)
    def _():
        to_homes(lambda n, src, dst, to: send(src, dst, gs_sem.at[n], gr_sem, rep, to).wait_send())

        kept = passing & ((12 * w) % HALF < TILES)

        @pl.when(kept)
        def _():
            arrived(mid.at[0:TILES * XS - 1], t1_sem)

        @pl.when(jnp.logical_not(kept))
        def _():
            arrived(mid.at[0:TILES * XS], t1_sem)

        for copy in row_sends:
            copy.wait_send()

    @pl.when(passing)
    def _():
        arrived(outb.at[0:SHARDS - 1], t2_sem)

    @pl.when(home)
    def _():
        half_block.wait_send()
        root.wait_send()
        root_scale.wait_send()
        for n in range(TILES):

            @pl.when(r == n)
            def _():
                to_rows(lambda i, src, dst, to: send(src, dst, ss_sem.at[i], sr_sem, rep, to).wait_send(), n)

    for copy in outs:
        copy.wait_send()


def store_kernel(d_in, left_in, right_in, d_out, left_new, right_new, sem):
    copies = []
    for n, (src, dst) in enumerate(((left_in, left_new), (right_in, right_new))):
        for j in range(2):
            copies.append(pltpu.make_async_copy(src.at[j], dst.at[j], sem.at[2 * n + j]))
    copies.append(pltpu.make_async_copy(d_in, d_out, sem.at[4]))
    for copy in copies:
        copy.start()
    for copy in copies:
        copy.wait()


SMEM = pl.BlockSpec(memory_space=pltpu.SMEM)
VMEM = pl.BlockSpec(memory_space=pltpu.VMEM)
ANY = pl.BlockSpec(memory_space=pl.ANY)
DMA = pltpu.SemaphoreType.DMA


def body(grads, left_prev, right_prev, block_owner, block_row, block_col):
    rows = grads.shape[1]
    direction, left_new, right_new = pl.pallas_call(
        step_kernel,
        out_shape=(
            pltpu.VMEM((TILES, 2, SUB, COLB * BLK), BF),
            pltpu.VMEM((2, BLK, BLK), F32),
            pltpu.VMEM((2, BLK, BLK), F32),
        ),
        in_specs=[SMEM, SMEM, SMEM, ANY, ANY, ANY],
        out_specs=(VMEM, VMEM, VMEM),
        scratch_shapes=[
            pltpu.VMEM((HALF, 2, 2, SUB, BLK), BF),
            pltpu.VMEM((2, 2 * HALF, SUB, BLK), F32),
            pltpu.VMEM((2, 2 * HALF, SUB, BLK), F32),
            pltpu.VMEM((TILES, SUB, COLB * BLK), BF),
            pltpu.VMEM((TILES, SUB, COLB * BLK), BF),
            pltpu.VMEM((COLB, TILES, SUB, BLK), BF),
            pltpu.VMEM((XS - 1, TILES, SUB, BLK), BF),
            pltpu.VMEM((TILES, SUB, BLK), BF),
            pltpu.VMEM((2, 2 * HALF, SUB, LANE), F32),
            pltpu.VMEM((2 * HALF, 2, SUB, LANE), BF),
            pltpu.VMEM((2 * SHARDS, SUB, LANE), BF),
            pltpu.VMEM((CELLS, SUB, LANE), BF),
            pltpu.VMEM((2 * HALF, SUB, BLK), BF),
            pltpu.VMEM((HALF, 2, SUB, BLK), BF),
            pltpu.VMEM((CELLS, SUB, LANE), BF),
            pltpu.VMEM((SHARDS, 2, SUB, LANE), BF),
            pltpu.VMEM((BLK, BLK), F32),
            pltpu.VMEM((2, BLK, BLK), BF),
            pltpu.VMEM((2, 8, LANE), F32),
            pltpu.VMEM((HALF, 2, SUB, BLK), BF),
            pltpu.VMEM((COLB, TILES, 2, SUB, BLK), BF),
            pltpu.VMEM((8, LANE), jnp.int32),
            pltpu.SMEM((8, LANE), jnp.int32),
            DMA, DMA, DMA((2,)), DMA((3,)), DMA((3,)),
            DMA, DMA, DMA, DMA, DMA((2,)), DMA, DMA((2,)), DMA, DMA, DMA, DMA, DMA((7,)), DMA((7,)),
            DMA((4,)), DMA((3,)), DMA, DMA((7,)), DMA((6,)), DMA, DMA((2,)), pltpu.SemaphoreType.REGULAR,
        ],
        compiler_params=pltpu.CompilerParams(
            collective_id=0, has_side_effects=True, vmem_limit_bytes=58 * 1024 * 1024
        ),
        name="shampoo_step",
    )(
        block_owner,
        block_row,
        block_col,
        grads.reshape(TILES, 2, SUB, COLB * BLK),
        left_prev.reshape(2, 2 * HALF, SUB, BLK),
        right_prev.reshape(2, 2 * HALF, SUB, BLK),
    )

    sq = jax.ShapeDtypeStruct((2, BLK, BLK), F32)
    results = [pltpu.with_memory_space_constraint(v, pltpu.VMEM) for v in (direction, left_new, right_new)]
    direction, left_new, right_new = pl.pallas_call(
        store_kernel,
        out_shape=(jax.ShapeDtypeStruct((TILES, 2, SUB, COLB * BLK), BF), sq, sq),
        in_specs=[VMEM, VMEM, VMEM],
        out_specs=(ANY, ANY, ANY),
        scratch_shapes=[DMA((5,))],
        compiler_params=pltpu.CompilerParams(vmem_limit_bytes=16 * 1024 * 1024),
        cost_estimate=pl.CostEstimate(flops=0, bytes_accessed=9 * 2**20, transcendentals=0),
        name="store_results",
    )(*results)
    return direction.reshape(rows, COLB * BLK), left_new, right_new


def solution(mesh):
    in_specs = (P("rep", "shard", None), P("shard", None, None), P("shard", None, None), P(), P(), P())
    out_specs = (P("shard", None), P("shard", None, None), P("shard", None, None))
    return jax.shard_map(body, mesh=mesh, in_specs=in_specs, out_specs=out_specs, check_vma=False)
```

```python
import jax
import jax.numpy as jnp
from jax import lax
from jax.experimental import pallas as pl
from jax.experimental.pallas import tpu as pltpu
from jax.sharding import PartitionSpec as P

BLK = 512
COLB = 3
ROWB = 10
CELLS = 30
SHARDS = 32
HALF = 16
TILES = 5
LANE = 128
SUB = 16
XS = 4
MESH = pl.DeviceIdType.MESH
BF = jnp.bfloat16
F32 = jnp.float32


def place():
    rep = lax.axis_index("rep")
    shard = lax.axis_index("shard")
    x = rep // 2
    h = rep % 2
    return rep, shard, x, h


def send(src, dst, send_sem, recv_sem, rep, shard):
    return pltpu.make_async_remote_copy(
        src_ref=src,
        dst_ref=dst,
        send_sem=send_sem,
        recv_sem=recv_sem,
        device_id=(rep, shard),
        device_id_type=MESH,
    )


def greet(barrier, rep, shard):
    pl.semaphore_signal(barrier, inc=1, device_id=(rep, shard), device_id_type=MESH)


def eye(size):
    row = lax.broadcasted_iota(jnp.int32, (size, size), 0)
    col = lax.broadcasted_iota(jnp.int32, (size, size), 1)
    return row == col


def mm(a, b):
    return jnp.dot(a, b, preferred_element_type=F32)


def root_less_one(new, scale):
    diag = eye(BLK)
    e = 0.25 * (jnp.where(diag, 1.0, 0.0) - new * (1.0 / scale))
    eb = e.astype(BF)
    u = 2.0 * e + mm(eb, eb)
    ub = u.astype(BF)
    v = 2.0 * u + mm(ub, ub)
    w = 4.0 * u - 5.0 * e
    z = (u - 0.25 * v) + 0.25 * mm(v.astype(BF), w.astype(BF))
    return z.astype(BF)


def fill_tables(tab, block_owner, block_row, block_col):
    sub = lax.broadcasted_iota(jnp.int32, (32, LANE), 0)
    lane = lax.broadcasted_iota(jnp.int32, (32, LANE), 1)
    owner = jnp.full((32, LANE), -1, jnp.int32)
    other = jnp.full((32, LANE), -2, jnp.int32)
    cell = jnp.full((32, LANE), -1, jnp.int32)
    for b in range(CELLS):
        owner = jnp.where(sub == b, block_owner[b], owner)
        other = jnp.where(lane == b, block_owner[b], other)
        cell = jnp.where(sub == b, block_row[b] // BLK * COLB + block_col[b] // BLK, cell)
    earlier = ((owner == other) & (lane < sub)).astype(jnp.int32)
    slot = 2 * owner + jnp.sum(earlier, axis=1, keepdims=True)
    cells = jnp.sum(jnp.where(slot == lane, cell, 0), axis=0, keepdims=True)
    slots = jnp.sum(jnp.where(cell == lane, slot, 0), axis=0, keepdims=True)
    tab[0:1] = jnp.clip(cells, 0, CELLS - 1)
    tab[1:2] = jnp.clip(slots, 0, 2 * SHARDS - 1)
    tab[2:3] = jnp.sum((slot == lane).astype(jnp.int32), axis=0, keepdims=True)


def step_kernel(
    block_owner, block_row, block_col, grads, left_prev, right_prev, d_out, left_out, right_out,
    g_own, lp, rp, own, pair, part, xin, red, xq, redq, pvf, pvb, pm, po, pv, gc, mid, outb, acc, zb, scl, pb, full, tab, look,
    own_sem, pvf_sem, pair_sem, xs_sem, xr_sem, p1_sem, p1r_sem, p2_sem, p2r_sem, gs_sem, gr_sem, ge_sem,
    t1_sem, t1r_sem, t2_sem, t2r_sem, os_sem, or_sem, z_sem, ss_sem, sr_sem, ds_sem, dr_sem, tab_sem, in_sem, qs_sem, qr_sem, ready, rows_in,
):
    rep = lax.axis_index("rep")
    shard = lax.axis_index("shard")
    x = rep // 2
    h = rep % 2
    half = shard // HALF
    w = shard % HALF
    r = w // 3
    j = w % 3
    partner = 2 * x + 1 - h
    summing = x < COLB
    home = summing & (j == 1)
    place_h = (2 * w) // 3 - 3 * h
    passing = (j != 1) & (place_h >= 0) & (place_h < 8)
    passed_tile = jnp.where(passing, 8 * half + place_h, 0)
    lanes = pl.ds(pl.multiple_of(x * LANE, LANE), LANE)
    barrier = pltpu.get_barrier_semaphore()

    def pass_on(src, dst, send_sem, recv_sem, to_rep, to_shard):
        me = (to_rep == rep) & (to_shard == shard)

        @pl.when(jnp.logical_not(me))
        def _():
            send(src, dst, send_sem, recv_sem, to_rep, to_shard).start()

        @pl.when(me)
        def _():
            pltpu.make_async_copy(src, dst, recv_sem).start()

    def arrived(ref, sem):
        pltpu.make_async_copy(ref, ref, sem).wait()

    def loop(count, fn):
        def step(n, carry):
            fn(n)
            return carry

        lax.fori_loop(0, count, step, 0)

    load = pltpu.make_async_copy(grads.at[:, h], own, own_sem)
    load.start()

    @pl.when(h == 0)
    def _():
        pltpu.make_async_copy(left_prev.at[:, :, :, lanes], pvf, pvf_sem).start()

    @pl.when(h == 1)
    def _():
        pltpu.make_async_copy(right_prev.at[:, :, :, lanes], pvf, pvf_sem).start()

    whole = [
        pltpu.make_async_copy(left_prev, lp, in_sem.at[0]),
        pltpu.make_async_copy(right_prev, rp, in_sem.at[1]),
    ]
    for copy in whole:
        copy.start()
    row0 = shard // 8 * 8
    loop(7, lambda n: greet(barrier, rep, row0 + (shard + 1 + n) % 8))
    loop(3, lambda n: greet(barrier, rep, (shard + 8 * n + 8) % SHARDS))
    for n in range(1, XS):
        greet(barrier, 2 * ((x + n) % XS) + h, shard)
    greet(barrier, partner, shard)
    fill_tables(tab, block_owner, block_row, block_col)
    tables = pltpu.make_async_copy(tab, look, tab_sem)
    tables.start()
    arrived(pvf, pvf_sem)
    for n in range(2):
        pvb[:, n] = pvf[n].astype(BF)
    pl.semaphore_wait(barrier, 10 + XS)

    tables.wait()
    swap = send(grads.at[:, 1 - h], pair, pair_sem.at[0], pair_sem.at[1], partner, shard)
    swap.start()
    def row_in(n):
        pl.semaphore_signal(
            rows_in, inc=1, device_id=(rep, (shard + 8 * n + 8) % SHARDS), device_id_type=MESH
        )

    loop(3, row_in)
    pl.semaphore_wait(rows_in, 3)
    for n in range(1, XS):
        pl.semaphore_signal(
            ready, inc=1, device_id=(2 * ((x + n) % XS) + h, shard), device_id_type=MESH
        )
    def taker(n):
        e = n % 8
        free = (3 * (e - 5 + 8 * (1 - h)) + 1) // 2
        group = jnp.where(n < 8, x, (x + 1) % COLB)
        to = HALF * (n // 8) + jnp.where(e < 5, 3 * e + 1, free)
        return jnp.where(summing, 8 * group + e, n), jnp.where(summing, to, n)

    free_place = (2 * w) // 3 - 8 * (1 - h)
    old_here = jnp.logical_not(summing) | (j == 1) | ((free_place >= 0) & (free_place < 3))
    old_place = jnp.where(summing, 8 * half + jnp.where(j == 1, r, 5 + free_place), shard)
    old_place = jnp.where(old_here, old_place, 0)
    old_tiles = jnp.where(summing, HALF, SHARDS)
    old_first = jnp.where(old_here, old_place + 1, shard)
    old_tile, _ = taker(old_place)
    mine = pm.at[pl.ds(2 * shard, 2)]
    def give_old(n):
        t, to = taker((old_first + n) % old_tiles)
        send(pvb.at[t], mine, p1_sem, p1r_sem, rep, to).start()

    loop(old_tiles - old_here.astype(jnp.int32), give_old)

    @pl.when(old_here)
    def _():
        pltpu.make_async_copy(pvb.at[old_tile], mine, p1r_sem).start()

    load.wait()
    swap.wait_recv()
    for c in range(COLB):
        cols = slice(c * BLK, (c + 1) * BLK)
        part[c] = (own[:, :, cols].astype(F32) + pair[:, :, cols].astype(F32)).astype(BF)
    for c in range(COLB):

        @pl.when(x != c)
        def _():
            n = (c - x + XS) % XS - 1
            send(part.at[c], xin.at[n], xs_sem.at[c], xr_sem.at[n], 2 * c + h, shard).start()

    shares = []
    for n in range(1, XS):
        to = (x + n) % XS
        cols = pl.ds(pl.multiple_of(to * LANE, LANE), LANE)
        shares.append(
            send(part.at[:, :, :, cols], xq.at[n - 1], qs_sem.at[n - 1], qr_sem.at[n - 1], 2 * to + h, shard)
        )
    for copy in shares:
        copy.start()

    pl.semaphore_wait(ready, XS - 1)
    def to_homes(act):
        @pl.when(j == 2)
        def _():
            act(0, red, gc.at[pl.ds(10 - r, TILES), h], shard - 1)

        for n in range(6):

            @pl.when((j == 0) & (r == n))
            def _():
                if n > 0:
                    act(0, red.at[0:n], gc.at[16 - n:16, h], shard - 2)
                if n < TILES:
                    act(1, red.at[n:TILES], gc.at[0:TILES - n, h], shard + 1)

    def passing_tile(n):
        u = TILES * w + n
        k = u % HALF
        to = HALF * (k // 8) + (3 * (k % 8 + 3 * h) + 1) // 2
        return redq.at[n], mid.at[pl.ds(COLB * (5 * half + u // HALF), COLB)], to

    @pl.when(summing)
    def _():
        for n in range(XS - 1):
            arrived(xin.at[n], xr_sem.at[n])
        red[...] = (
            (part[x].astype(F32) + xin[0].astype(F32)) + (xin[1].astype(F32) + xin[2].astype(F32))
        ).astype(BF)
        to_homes(lambda n, src, dst, to: send(src, dst, gs_sem.at[n], gr_sem, rep, to).start())

        @pl.when(j == 1)
        def _():
            pltpu.make_async_copy(red, gc.at[pl.ds(TILES - r, TILES), h], gr_sem).start()

    tile_at_home = pv.at[old_tile, :, lanes]

    def home_of(cell):
        row = cell // COLB
        return 2 * (cell % COLB) + h, HALF * (row // 5) + 3 * (row % 5) + 1

    own_cell = COLB * (5 * half + r) + x
    first = jnp.where(home, own_cell + 1, 0)

    def give_factor(n):
        cell = (first + n) % CELLS
        po[cell] = pm[look[1, cell]]
        to_rep, to_shard = home_of(cell)
        send(po.at[cell], tile_at_home, p2_sem, p2r_sem, to_rep, to_shard).start()

    @pl.when(old_here)
    def _():
        arrived(pm, p1r_sem)
        loop(CELLS - home.astype(jnp.int32), give_factor)

        @pl.when(home)
        def _():
            po[own_cell] = pm[look[1, own_cell]]
            pltpu.make_async_copy(po.at[own_cell], tile_at_home, p2r_sem).start()


    for copy in shares:
        copy.wait_recv()
    for c in range(COLB):
        redq[:, c] = (
            (part[c, :, :, lanes].astype(F32) + xq[0, c].astype(F32))
            + (xq[1, c].astype(F32) + xq[2, c].astype(F32))
        ).astype(BF)
    for n in range(TILES):
        src, dst, to = passing_tile(n)
        pass_on(src, dst, t1_sem, t1r_sem, rep, to)

    half_block = send(gc.at[:, h], gc.at[:, h], ge_sem.at[0], ge_sem.at[1], partner, shard)

    @pl.when(home)
    def _():
        arrived(gc.at[:, h], gr_sem)
        half_block.start()

    def view(hh, col):
        return g_own.at[:, :, hh, :, pl.ds(pl.multiple_of(col * LANE, LANE), LANE)]

    def slot_view(slot, hh, col):
        return g_own.at[:, slot, hh, :, pl.ds(pl.multiple_of(col * LANE, LANE), LANE)]

    @pl.when(passing)
    def _():
        arrived(mid, t1r_sem)

        def fill(o):
            for n in range(2):
                outb[o, n] = mid[look[0, 2 * o + n]]

        slots_at_owner = g_own.at[passed_tile, :, h, :, lanes]

        def give_slots(n):
            o = (shard + 1 + n) % SHARDS
            fill(o)
            send(outb.at[o], slots_at_owner, t2_sem, t2r_sem, rep, o).start()

        loop(SHARDS - 1, give_slots)
        fill(shard)
        pltpu.make_async_copy(outb.at[shard], slots_at_owner, t2r_sem).start()

    root = send(zb.at[h], zb.at[h], z_sem.at[0], z_sem.at[1], partner, shard)
    root_scale = send(scl.at[h], scl.at[h], z_sem.at[2], z_sem.at[3], partner, shard)

    def to_rows(act, n):
        act(0, pb.at[0:TILES - n, h], full.at[x, n:TILES, h], shard - 1)
        act(1, pb.at[10 - n:15 - n, h], full.at[x, :, h], shard + 1)
        act(2, pb.at[15 - n:16, h], full.at[x, 0:1 + n, h], shard + 2)

    @pl.when(home)
    def _():
        other = gc.at[:, 1 - h]
        arrived(other, ge_sem.at[1])
        g = gc[...].reshape(BLK, BLK)
        gt = g.T
        gf = g.astype(F32)
        sg = jnp.full((8, LANE), jnp.sum(gf * gf), F32)

        @pl.when(h == 0)
        def _():
            acc[...] = mm(g, gt)

        @pl.when(h == 1)
        def _():
            acc[...] = mm(gt, g)

        arrived(pv.at[0:20], p2r_sem)
        for a, b in ((2, 0), (0, 1), (1, 2), (3, 0), (3, 1), (3, 2)):
            there = pv[8 * b:8 * b + 8, :, a * LANE:(a + 1) * LANE].reshape(LANE, LANE)
            pv[8 * a:8 * a + 8, :, b * LANE:(b + 1) * LANE] = there.T.reshape(8, SUB, LANE)
        val = acc[...] + pv[...].reshape(BLK, BLK).astype(F32)
        scale = jnp.sum(jnp.where(eye(BLK), val, 0.0)) * (1.0 / BLK)
        zb[h] = root_less_one(val, scale)
        scl[h] = lax.rsqrt(jnp.sqrt(jnp.full((8, LANE), scale, F32)))
        root.start()
        root_scale.start()
        arrived(zb.at[1 - h], z_sem.at[1])
        arrived(scl.at[1 - h], z_sem.at[3])
        y = scl[0, 0:1, 0:1] * (gf + mm(zb[0], g))
        p = scl[1, 0:1, 0:1] * (y + mm(y.astype(BF), zb[1]))
        sp = jnp.full((8, LANE), jnp.sum(p * p), F32)
        ratio = jnp.sqrt(sg / (sp + 1e-06))[0:1, 0:1]
        pb[...] = (p * ratio).astype(BF).reshape(HALF, 2, SUB, BLK)
        for n in range(TILES):

            @pl.when(r == n)
            def _():
                to_rows(lambda i, src, dst, to: send(src, dst, ss_sem.at[i], sr_sem, rep, to).start(), n)
                pltpu.make_async_copy(pb.at[5 - n:10 - n, h], full.at[x, :, h], sr_sem).start()

    arrived(view(h, x), t2r_sem)
    outs = []
    for slot in range(2):
        owned = slot_view(slot, h, x)
        for n in (2, 1, 3):
            to = 2 * ((x + n) % XS) + h
            outs.append(send(owned, owned, os_sem.at[7 * slot + n], or_sem.at[7 * slot + n], to, shard))
        outs.append(send(owned, owned, os_sem.at[7 * slot], or_sem.at[7 * slot], partner, shard))
    for copy in outs:
        copy.start()

    rows = full.at[x, :, h]
    row_sends = [
        send(rows, rows, ds_sem.at[n], dr_sem.at[x], 2 * ((x + n) % XS) + h, shard) for n in (2, 1, 3)
    ]
    row_sends.append(send(rows, rows, ds_sem.at[0], dr_sem.at[COLB + x], partner, shard))

    @pl.when(summing)
    def _():
        arrived(rows, sr_sem)
        for copy in row_sends:
            copy.start()

    def to_partner(slot):
        for n in (1, 3, 2):
            piece = slot_view(slot, h, (x + XS - n) % XS)
            arrived(piece, or_sem.at[7 * slot + n])
            sem = 7 * slot + 3 + n
            copy = send(piece, piece, os_sem.at[sem], or_sem.at[sem], partner, shard)
            copy.start()
            outs.append(copy)

    to_partner(0)

    def onward(c):
        return send(
            full.at[c, :, h], full.at[c, :, h], ds_sem.at[XS + c], dr_sem.at[COLB + c], partner, shard
        )

    for c in range(COLB):

        @pl.when(x != c)
        def _():
            arrived(full.at[c, :, h], dr_sem.at[c])
            onward(c).start()

    to_partner(1)
    for copy in whole:
        copy.wait()

    def factors(n):
        for index, m in ((0, 0), (4, 1), (6, 3), (5, 2)):
            arrived(slot_view(n, 1 - h, (x + XS - m) % XS), or_sem.at[7 * n + index])
        on = look[2, 2 * shard + n] > 0
        g = g_own[:, n].reshape(BLK, BLK)
        g = jnp.where(on, g, jnp.zeros_like(g))
        gt = g.T
        for prev, out, a, b in ((lp, left_out, g, gt), (rp, right_out, gt, g)):
            new = prev[n].reshape(BLK, BLK) + mm(a, b)
            out[n] = jnp.where(on, new, jnp.zeros_like(new))

    for n in range(2):
        factors(n)
    for c in range(COLB):
        arrived(full.at[c, :, 1 - h], dr_sem.at[COLB + c])
        d_out[:, :, :, c * BLK:(c + 1) * BLK] = full[c]

    kept = passing & ((passed_tile - TILES * w + 5 * HALF) % HALF < TILES)

    @pl.when(kept)
    def _():
        arrived(mid.at[0:COLB * (TILES - 1)], t1_sem)

    @pl.when(jnp.logical_not(kept))
    def _():
        arrived(mid.at[0:COLB * TILES], t1_sem)

    for copy in shares:
        copy.wait_send()
    swap.wait_send()
    for count, kept in ((16, 0), (16, 1), (32, 1)):

        @pl.when((old_tiles == count) & (old_here.astype(jnp.int32) == kept))
        def _():
            arrived(pvb.at[0:count - kept], p1_sem)

    @pl.when(old_here & home)
    def _():
        arrived(po.at[0:CELLS - 1], p2_sem)

    @pl.when(old_here & jnp.logical_not(home))
    def _():
        arrived(po, p2_sem)

    for c in range(COLB):

        @pl.when(x != c)
        def _():
            n = (c - x + XS) % XS - 1
            send(part.at[c], xin.at[n], xs_sem.at[c], xr_sem.at[n], 2 * c + h, shard).wait_send()
            onward(c).wait_send()

    @pl.when(summing)
    def _():
        to_homes(lambda n, src, dst, to: send(src, dst, gs_sem.at[n], gr_sem, rep, to).wait_send())

        for copy in row_sends:
            copy.wait_send()

    @pl.when(passing)
    def _():
        arrived(outb.at[0:SHARDS - 1], t2_sem)

    @pl.when(home)
    def _():
        half_block.wait_send()
        root.wait_send()
        root_scale.wait_send()
        for n in range(TILES):

            @pl.when(r == n)
            def _():
                to_rows(lambda i, src, dst, to: send(src, dst, ss_sem.at[i], sr_sem, rep, to).wait_send(), n)

    for copy in outs:
        copy.wait_send()


def store_kernel(d_in, left_in, right_in, d_out, left_new, right_new, sem):
    copies = []
    for n, (src, dst) in enumerate(((left_in, left_new), (right_in, right_new))):
        for j in range(2):
            copies.append(pltpu.make_async_copy(src.at[j], dst.at[j], sem.at[2 * n + j]))
    copies.append(pltpu.make_async_copy(d_in, d_out, sem.at[4]))
    for copy in copies:
        copy.start()
    for copy in copies:
        copy.wait()


SMEM = pl.BlockSpec(memory_space=pltpu.SMEM)
VMEM = pl.BlockSpec(memory_space=pltpu.VMEM)
ANY = pl.BlockSpec(memory_space=pl.ANY)
DMA = pltpu.SemaphoreType.DMA


def body(grads, left_prev, right_prev, block_owner, block_row, block_col):
    rows = grads.shape[1]
    direction, left_new, right_new = pl.pallas_call(
        step_kernel,
        out_shape=(
            pltpu.VMEM((TILES, 2, SUB, COLB * BLK), BF),
            pltpu.VMEM((2, BLK, BLK), F32),
            pltpu.VMEM((2, BLK, BLK), F32),
        ),
        in_specs=[SMEM, SMEM, SMEM, ANY, ANY, ANY],
        out_specs=(VMEM, VMEM, VMEM),
        scratch_shapes=[
            pltpu.VMEM((HALF, 2, 2, SUB, BLK), BF),
            pltpu.VMEM((2, 2 * HALF, SUB, BLK), F32),
            pltpu.VMEM((2, 2 * HALF, SUB, BLK), F32),
            pltpu.VMEM((TILES, SUB, COLB * BLK), BF),
            pltpu.VMEM((TILES, SUB, COLB * BLK), BF),
            pltpu.VMEM((COLB, TILES, SUB, BLK), BF),
            pltpu.VMEM((XS - 1, TILES, SUB, BLK), BF),
            pltpu.VMEM((TILES, SUB, BLK), BF),
            pltpu.VMEM((XS - 1, COLB, TILES, SUB, LANE), BF),
            pltpu.VMEM((TILES, COLB, SUB, LANE), BF),
            pltpu.VMEM((2, 2 * HALF, SUB, LANE), F32),
            pltpu.VMEM((2 * HALF, 2, SUB, LANE), BF),
            pltpu.VMEM((2 * SHARDS, SUB, LANE), BF),
            pltpu.VMEM((CELLS, SUB, LANE), BF),
            pltpu.VMEM((2 * HALF, SUB, BLK), BF),
            pltpu.VMEM((HALF, 2, SUB, BLK), BF),
            pltpu.VMEM((CELLS, SUB, LANE), BF),
            pltpu.VMEM((SHARDS, 2, SUB, LANE), BF),
            pltpu.VMEM((BLK, BLK), F32),
            pltpu.VMEM((2, BLK, BLK), BF),
            pltpu.VMEM((2, 8, LANE), F32),
            pltpu.VMEM((HALF, 2, SUB, BLK), BF),
            pltpu.VMEM((COLB, TILES, 2, SUB, BLK), BF),
            pltpu.VMEM((8, LANE), jnp.int32),
            pltpu.SMEM((8, LANE), jnp.int32),
            DMA, DMA, DMA((2,)), DMA((3,)), DMA((3,)),
            DMA, DMA, DMA, DMA, DMA((2,)), DMA, DMA((2,)), DMA, DMA, DMA, DMA, DMA((14,)), DMA((14,)),
            DMA((4,)), DMA((3,)), DMA, DMA((7,)), DMA((6,)), DMA, DMA((2,)), DMA((3,)), DMA((3,)), pltpu.SemaphoreType.REGULAR, pltpu.SemaphoreType.REGULAR,
        ],
        compiler_params=pltpu.CompilerParams(
            collective_id=0, has_side_effects=True, vmem_limit_bytes=58 * 1024 * 1024
        ),
        name="shampoo_step",
    )(
        block_owner,
        block_row,
        block_col,
        grads.reshape(TILES, 2, SUB, COLB * BLK),
        left_prev.reshape(2, 2 * HALF, SUB, BLK),
        right_prev.reshape(2, 2 * HALF, SUB, BLK),
    )

    sq = jax.ShapeDtypeStruct((2, BLK, BLK), F32)
    results = [pltpu.with_memory_space_constraint(v, pltpu.VMEM) for v in (direction, left_new, right_new)]
    direction, left_new, right_new = pl.pallas_call(
        store_kernel,
        out_shape=(jax.ShapeDtypeStruct((TILES, 2, SUB, COLB * BLK), BF), sq, sq),
        in_specs=[VMEM, VMEM, VMEM],
        out_specs=(ANY, ANY, ANY),
        scratch_shapes=[DMA((5,))],
        compiler_params=pltpu.CompilerParams(vmem_limit_bytes=16 * 1024 * 1024),
        cost_estimate=pl.CostEstimate(flops=0, bytes_accessed=9 * 2**20, transcendentals=0),
        name="store_results",
    )(*results)
    return direction.reshape(rows, COLB * BLK), left_new, right_new


def solution(mesh):
    in_specs = (P("rep", "shard", None), P("shard", None, None), P("shard", None, None), P(), P(), P())
    out_specs = (P("shard", None), P("shard", None, None), P("shard", None, None))
    return jax.shard_map(body, mesh=mesh, in_specs=in_specs, out_specs=out_specs, check_vma=False)
```

```python
import jax
import jax.numpy as jnp
from jax import lax
from jax.experimental import pallas as pl
from jax.experimental.pallas import tpu as pltpu
from jax.sharding import PartitionSpec as P

BLK = 512
COLB = 3
ROWB = 10
CELLS = 30
SHARDS = 32
HALF = 16
TILES = 5
LANE = 128
SUB = 16
XS = 4
MESH = pl.DeviceIdType.MESH
BF = jnp.bfloat16
F32 = jnp.float32


def place():
    rep = lax.axis_index("rep")
    shard = lax.axis_index("shard")
    x = rep // 2
    h = rep % 2
    return rep, shard, x, h


def send(src, dst, send_sem, recv_sem, rep, shard):
    return pltpu.make_async_remote_copy(
        src_ref=src,
        dst_ref=dst,
        send_sem=send_sem,
        recv_sem=recv_sem,
        device_id=(rep, shard),
        device_id_type=MESH,
    )


def greet(barrier, rep, shard):
    pl.semaphore_signal(barrier, inc=1, device_id=(rep, shard), device_id_type=MESH)


def eye(size):
    row = lax.broadcasted_iota(jnp.int32, (size, size), 0)
    col = lax.broadcasted_iota(jnp.int32, (size, size), 1)
    return row == col


def mm(a, b):
    return jnp.dot(a, b, preferred_element_type=F32)


def root_less_one(new, scale):
    diag = eye(BLK)
    e = 0.25 * (jnp.where(diag, 1.0, 0.0) - new * (1.0 / scale))
    eb = e.astype(BF)
    u = 2.0 * e + mm(eb, eb)
    ub = u.astype(BF)
    v = 2.0 * u + mm(ub, ub)
    w = 4.0 * u - 5.0 * e
    return u - 0.25 * v, v.astype(BF), w.astype(BF)


def fill_tables(tab, block_owner, block_row, block_col):
    sub = lax.broadcasted_iota(jnp.int32, (32, LANE), 0)
    lane = lax.broadcasted_iota(jnp.int32, (32, LANE), 1)
    owner = jnp.full((32, LANE), -1, jnp.int32)
    other = jnp.full((32, LANE), -2, jnp.int32)
    cell = jnp.full((32, LANE), -1, jnp.int32)
    for b in range(CELLS):
        owner = jnp.where(sub == b, block_owner[b], owner)
        other = jnp.where(lane == b, block_owner[b], other)
        cell = jnp.where(sub == b, block_row[b] // BLK * COLB + block_col[b] // BLK, cell)
    earlier = ((owner == other) & (lane < sub)).astype(jnp.int32)
    slot = 2 * owner + jnp.sum(earlier, axis=1, keepdims=True)
    cells = jnp.sum(jnp.where(slot == lane, cell, 0), axis=0, keepdims=True)
    slots = jnp.sum(jnp.where(cell == lane, slot, 0), axis=0, keepdims=True)
    tab[0:1] = jnp.clip(cells, 0, CELLS - 1)
    tab[1:2] = jnp.clip(slots, 0, 2 * SHARDS - 1)
    tab[2:3] = jnp.sum((slot == lane).astype(jnp.int32), axis=0, keepdims=True)


def step_kernel(
    block_owner, block_row, block_col, grads, left_prev, right_prev, d_out, left_out, right_out,
    g_own, lp, rp, own, pair, part, xin, red, xq, redq, pvf, pvb, pm, po, pv, gc, mid, outb, acc, zb, scl, pb, full, tab, look,
    own_sem, pvf_sem, pair_sem, xs_sem, xr_sem, p1_sem, p1r_sem, p2_sem, p2r_sem, gs_sem, gr_sem, ge_sem,
    t1_sem, t1r_sem, t2_sem, t2r_sem, os_sem, or_sem, z_sem, ss_sem, sr_sem, ds_sem, dr_sem, tab_sem, in_sem, qs_sem, qr_sem, ready, rows_in,
):
    rep = lax.axis_index("rep")
    shard = lax.axis_index("shard")
    x = rep // 2
    h = rep % 2
    half = shard // HALF
    w = shard % HALF
    r = w // 3
    j = w % 3
    partner = 2 * x + 1 - h
    summing = x < COLB
    home_row = ((j == 1) & (r < 3)) | ((j == 2) & (r >= 3))
    home = summing & home_row
    number = w
    for n in (1, 4, 7, 11, 14):
        number = number - (w > n).astype(jnp.int32)
    passing = jnp.logical_not(home_row) & (number >= 3 * h) & (number < 3 * h + 8)

    def numbered(n):
        return (3 * n + 1 - (n > 6).astype(jnp.int32)) // 2

    def home_shard(group):
        return 3 * group + 1 + (group > 2).astype(jnp.int32)

    passed_tile = jnp.where(passing, 8 * half + number - 3 * h, 0)
    lanes = pl.ds(pl.multiple_of(x * LANE, LANE), LANE)
    barrier = pltpu.get_barrier_semaphore()

    def pass_on(src, dst, send_sem, recv_sem, to_rep, to_shard):
        me = (to_rep == rep) & (to_shard == shard)

        @pl.when(jnp.logical_not(me))
        def _():
            send(src, dst, send_sem, recv_sem, to_rep, to_shard).start()

        @pl.when(me)
        def _():
            pltpu.make_async_copy(src, dst, recv_sem).start()

    def arrived(ref, sem):
        pltpu.make_async_copy(ref, ref, sem).wait()

    def loop(count, fn):
        def step(n, carry):
            fn(n)
            return carry

        lax.fori_loop(0, count, step, 0)

    row0 = shard // 8 * 8
    loop(7, lambda n: greet(barrier, rep, row0 + (shard + 1 + n) % 8))
    loop(3, lambda n: greet(barrier, rep, (shard + 8 * n + 8) % SHARDS))
    for n in range(1, XS):
        greet(barrier, 2 * ((x + n) % XS) + h, shard)
    greet(barrier, partner, shard)
    load = pltpu.make_async_copy(grads.at[:, h], own, own_sem)
    load.start()

    @pl.when(h == 0)
    def _():
        pltpu.make_async_copy(left_prev.at[:, :, :, lanes], pvf, pvf_sem).start()

    @pl.when(h == 1)
    def _():
        pltpu.make_async_copy(right_prev.at[:, :, :, lanes], pvf, pvf_sem).start()

    whole = [
        pltpu.make_async_copy(left_prev, lp, in_sem.at[0]),
        pltpu.make_async_copy(right_prev, rp, in_sem.at[1]),
    ]
    arrived(pvf, pvf_sem)
    for n in range(2):
        pvb[:, n] = pvf[n].astype(BF)
    pl.semaphore_wait(barrier, 10 + XS)

    swap = send(grads.at[:, 1 - h], pair, pair_sem.at[0], pair_sem.at[1], partner, shard)
    swap.start()
    def row_in(n):
        pl.semaphore_signal(
            rows_in, inc=1, device_id=(rep, (shard + 8 * n + 8) % SHARDS), device_id_type=MESH
        )

    loop(3, row_in)
    pl.semaphore_wait(rows_in, 3)
    for n in range(1, XS):
        pl.semaphore_signal(
            ready, inc=1, device_id=(2 * ((x + n) % XS) + h, shard), device_id_type=MESH
        )
    def taker(n):
        e = n % 8
        free = numbered(jnp.maximum(e - 5 + 8 * (1 - h), 0))
        group = jnp.where(n < 8, x, (x + 1) % COLB)
        to = HALF * (n // 8) + jnp.where(e < 5, home_shard(e), free)
        return jnp.where(summing, 8 * group + e, n), jnp.where(summing, to, n)

    free_place = number - 8 * (1 - h)
    old_here = jnp.logical_not(summing) | home_row | ((free_place >= 0) & (free_place < 3))
    old_place = jnp.where(summing, 8 * half + jnp.where(home_row, r, 5 + free_place), shard)
    old_place = jnp.where(old_here, old_place, 0)
    old_tiles = jnp.where(summing, HALF, SHARDS)
    old_first = jnp.where(old_here, old_place + 1, shard)
    old_tile, _ = taker(old_place)
    mine = pm.at[pl.ds(2 * shard, 2)]
    def give_old(n):
        t, to = taker((old_first + n) % old_tiles)
        send(pvb.at[t], mine, p1_sem, p1r_sem, rep, to).start()

    loop(old_tiles - old_here.astype(jnp.int32), give_old)

    @pl.when(old_here)
    def _():
        pltpu.make_async_copy(pvb.at[old_tile], mine, p1r_sem).start()

    fill_tables(tab, block_owner, block_row, block_col)
    tables = pltpu.make_async_copy(tab, look, tab_sem)
    tables.start()
    for copy in whole:
        copy.start()
    load.wait()
    swap.wait_recv()
    for c in range(COLB):
        cols = slice(c * BLK, (c + 1) * BLK)
        part[c] = (own[:, :, cols].astype(F32) + pair[:, :, cols].astype(F32)).astype(BF)
    shares = []
    for n in range(1, XS):
        to = (x + n) % XS
        cols = pl.ds(pl.multiple_of(to * LANE, LANE), LANE)
        shares.append(
            send(part.at[:, :, :, cols], xq.at[n - 1], qs_sem.at[n - 1], qr_sem.at[n - 1], 2 * to + h, shard)
        )
    for copy in shares:
        copy.start()

    for c in range(COLB):

        @pl.when(x != c)
        def _():
            n = (c - x + XS) % XS - 1
            send(part.at[c], xin.at[n], xs_sem.at[c], xr_sem.at[n], 2 * c + h, shard).start()

    tables.wait()
    pl.semaphore_wait(ready, XS - 1)
    def to_homes(act):
        @pl.when((j == 2) & (r < 3))
        def _():
            act(0, red, gc.at[pl.ds(10 - r, TILES), h], shard - 1)

        @pl.when((j == 1) & (r >= 3))
        def _():
            act(0, red, gc.at[pl.ds(TILES - r, TILES), h], shard + 1)

        for n in range(6):

            @pl.when((j == 0) & (r == n))
            def _():
                if n > 0:
                    act(0, red.at[0:n], gc.at[16 - n:16, h], shard - (2 if n < 4 else 1))
                if n < TILES:
                    act(1, red.at[n:TILES], gc.at[0:TILES - n, h], shard + (1 if n < 3 else 2))

    def passing_tile(n):
        u = TILES * w + n
        k = u % HALF
        to = HALF * (k // 8) + numbered(k % 8 + 3 * h)
        return redq.at[n], mid.at[pl.ds(COLB * (5 * half + u // HALF), COLB)], to

    tile_at_home = pv.at[old_tile, :, lanes]

    def home_of(cell):
        row = cell // COLB
        return 2 * (cell % COLB) + h, HALF * (row // 5) + home_shard(row % 5)

    own_cell = COLB * (5 * half + r) + x
    first = jnp.where(home, own_cell + 1, 0)

    def give_factor(n):
        cell = (first + n) % CELLS
        po[cell] = pm[look[1, cell]]
        to_rep, to_shard = home_of(cell)
        send(po.at[cell], tile_at_home, p2_sem, p2r_sem, to_rep, to_shard).start()

    @pl.when(old_here)
    def _():
        arrived(pm, p1r_sem)
        loop(CELLS - home.astype(jnp.int32), give_factor)

        @pl.when(home)
        def _():
            po[own_cell] = pm[look[1, own_cell]]
            pltpu.make_async_copy(po.at[own_cell], tile_at_home, p2r_sem).start()


    for copy in shares:
        copy.wait_recv()
    for c in range(COLB):
        redq[:, c] = (
            (part[c, :, :, lanes].astype(F32) + xq[0, c].astype(F32))
            + (xq[1, c].astype(F32) + xq[2, c].astype(F32))
        ).astype(BF)
    for n in range(TILES):
        src, dst, to = passing_tile(n)
        pass_on(src, dst, t1_sem, t1r_sem, rep, to)

    @pl.when(summing)
    def _():
        for n in range(XS - 1):
            arrived(xin.at[n], xr_sem.at[n])
        red[...] = (
            (part[x].astype(F32) + xin[0].astype(F32)) + (xin[1].astype(F32) + xin[2].astype(F32))
        ).astype(BF)
        to_homes(lambda n, src, dst, to: send(src, dst, gs_sem.at[n], gr_sem, rep, to).start())

        @pl.when(home)
        def _():
            pltpu.make_async_copy(red, gc.at[pl.ds(TILES * j - r, TILES), h], gr_sem).start()

    half_block = send(gc.at[:, h], gc.at[:, h], ge_sem.at[0], ge_sem.at[1], partner, shard)

    @pl.when(home)
    def _():
        arrived(gc.at[:, h], gr_sem)
        half_block.start()

    def view(hh, col):
        return g_own.at[:, :, hh, :, pl.ds(pl.multiple_of(col * LANE, LANE), LANE)]

    def slot_view(slot, hh, col):
        return g_own.at[:, slot, hh, :, pl.ds(pl.multiple_of(col * LANE, LANE), LANE)]

    @pl.when(passing)
    def _():
        arrived(mid, t1r_sem)

        def fill(o):
            for n in range(2):
                outb[o, n] = mid[look[0, 2 * o + n]]

        slots_at_owner = g_own.at[passed_tile, :, h, :, lanes]

        def give_slots(n):
            o = (shard + 1 + n) % SHARDS
            fill(o)
            send(outb.at[o], slots_at_owner, t2_sem, t2r_sem, rep, o).start()

        loop(SHARDS - 1, give_slots)
        fill(shard)
        pltpu.make_async_copy(outb.at[shard], slots_at_owner, t2r_sem).start()

    halves = (pl.ds(0, BLK // 2), pl.ds(BLK // 2, BLK // 2))
    roots = [
        send(zb.at[h, rows], zb.at[h, rows], z_sem.at[n], z_sem.at[3 + n], partner, shard)
        for n, rows in enumerate(halves)
    ]
    roots.append(send(scl.at[h], scl.at[h], z_sem.at[2], z_sem.at[5], partner, shard))

    def to_rows(act, n):
        early = n < 3
        act(0, pb.at[0:TILES - n, h], full.at[x, n:TILES, h], shard - (1 if early else 2))
        if early:
            act(1, pb.at[10 - n:15 - n, h], full.at[x, :, h], shard + 1)
        else:
            act(1, pb.at[5 - n:10 - n, h], full.at[x, :, h], shard - 1)
        act(2, pb.at[15 - n:16, h], full.at[x, 0:1 + n, h], shard + (2 if early else 1))

    @pl.when(home)
    def _():
        other = gc.at[:, 1 - h]
        arrived(other, ge_sem.at[1])
        g = gc[...].reshape(BLK, BLK)
        gt = g.T
        gf = g.astype(F32)
        sg = jnp.full((8, LANE), jnp.sum(gf * gf), F32)

        @pl.when(h == 0)
        def _():
            acc[...] = mm(g, gt)

        @pl.when(h == 1)
        def _():
            acc[...] = mm(gt, g)

        arrived(pv.at[0:20], p2r_sem)
        for a, b in ((2, 0), (0, 1), (1, 2), (3, 0), (3, 1), (3, 2)):
            there = pv[8 * b:8 * b + 8, :, a * LANE:(a + 1) * LANE].reshape(LANE, LANE)
            pv[8 * a:8 * a + 8, :, b * LANE:(b + 1) * LANE] = there.T.reshape(8, SUB, LANE)
        val = acc[...] + pv[...].reshape(BLK, BLK).astype(F32)
        scale = jnp.sum(jnp.where(eye(BLK), val, 0.0)) * (1.0 / BLK)
        scl[h] = lax.rsqrt(jnp.sqrt(jnp.full((8, LANE), scale, F32)))
        roots[2].start()
        rest, v, u = root_less_one(val, scale)
        for n, rows in enumerate(halves):
            part_v = v[n * (BLK // 2):(n + 1) * (BLK // 2)]
            zb[h, rows] = (rest[n * (BLK // 2):(n + 1) * (BLK // 2)] + 0.25 * mm(part_v, u)).astype(BF)
            roots[n].start()

        @pl.when(h == 0)
        def _():
            acc[...] = scl[0, 0:1, 0:1] * (gf + mm(zb[0], g))

        @pl.when(h == 1)
        def _():
            acc[...] = scl[1, 0:1, 0:1] * (gf + mm(g, zb[1]))

        y = acc[...]
        for n, rows in enumerate(halves):
            arrived(zb.at[1 - h, rows], z_sem.at[3 + n])
        arrived(scl.at[1 - h], z_sem.at[5])

        @pl.when(h == 0)
        def _():
            acc[...] = scl[1, 0:1, 0:1] * (y + mm(y.astype(BF), zb[1]))

        @pl.when(h == 1)
        def _():
            acc[...] = scl[0, 0:1, 0:1] * (y + mm(zb[0], y.astype(BF)))

        p = acc[...]
        sp = jnp.full((8, LANE), jnp.sum(p * p), F32)
        ratio = jnp.sqrt(sg / (sp + 1e-06))[0:1, 0:1]
        pb[...] = (p * ratio).astype(BF).reshape(HALF, 2, SUB, BLK)
        for n in range(TILES):

            @pl.when(r == n)
            def _():
                to_rows(lambda i, src, dst, to: send(src, dst, ss_sem.at[i], sr_sem, rep, to).start(), n)
                at = (5 if n < 3 else 10) - n
                pltpu.make_async_copy(pb.at[at:at + TILES, h], full.at[x, :, h], sr_sem).start()

    arrived(view(h, x), t2r_sem)
    outs = []
    for slot in range(2):
        owned = slot_view(slot, h, x)
        for n in (2, 1, 3):
            to = 2 * ((x + n) % XS) + h
            outs.append(send(owned, owned, os_sem.at[7 * slot + n], or_sem.at[7 * slot + n], to, shard))
        outs.append(send(owned, owned, os_sem.at[7 * slot], or_sem.at[7 * slot], partner, shard))
    for copy in outs:
        copy.start()

    rows = full.at[x, :, h]
    row_sends = [
        send(rows, rows, ds_sem.at[n], dr_sem.at[x], 2 * ((x + n) % XS) + h, shard) for n in (2, 1, 3)
    ]
    row_sends.append(send(rows, rows, ds_sem.at[0], dr_sem.at[COLB + x], partner, shard))

    @pl.when(summing)
    def _():
        arrived(rows, sr_sem)
        for copy in row_sends:
            copy.start()

    def to_partner(slot):
        for n in (1, 3, 2):
            piece = slot_view(slot, h, (x + XS - n) % XS)
            arrived(piece, or_sem.at[7 * slot + n])
            sem = 7 * slot + 3 + n
            copy = send(piece, piece, os_sem.at[sem], or_sem.at[sem], partner, shard)
            copy.start()
            outs.append(copy)

    to_partner(0)

    def onward(c):
        return send(
            full.at[c, :, h], full.at[c, :, h], ds_sem.at[XS + c], dr_sem.at[COLB + c], partner, shard
        )

    for c in range(COLB):

        @pl.when(x != c)
        def _():
            arrived(full.at[c, :, h], dr_sem.at[c])
            onward(c).start()

    to_partner(1)
    for copy in whole:
        copy.wait()

    def factors(n):
        for index, m in ((0, 0), (4, 1), (6, 3), (5, 2)):
            arrived(slot_view(n, 1 - h, (x + XS - m) % XS), or_sem.at[7 * n + index])
        on = look[2, 2 * shard + n] > 0
        g = g_own[:, n].reshape(BLK, BLK)
        g = jnp.where(on, g, jnp.zeros_like(g))
        gt = g.T
        for prev, out, a, b in ((lp, left_out, g, gt), (rp, right_out, gt, g)):
            new = prev[n].reshape(BLK, BLK) + mm(a, b)
            out[n] = jnp.where(on, new, jnp.zeros_like(new))

    for n in range(2):
        factors(n)
    for c in range(COLB):
        arrived(full.at[c, :, 1 - h], dr_sem.at[COLB + c])
        d_out[:, :, :, c * BLK:(c + 1) * BLK] = full[c]

    kept = passing & ((passed_tile - TILES * w + 5 * HALF) % HALF < TILES)

    @pl.when(kept)
    def _():
        arrived(mid.at[0:COLB * (TILES - 1)], t1_sem)

    @pl.when(jnp.logical_not(kept))
    def _():
        arrived(mid.at[0:COLB * TILES], t1_sem)

    for copy in shares:
        copy.wait_send()
    swap.wait_send()
    for count, kept in ((16, 0), (16, 1), (32, 1)):

        @pl.when((old_tiles == count) & (old_here.astype(jnp.int32) == kept))
        def _():
            arrived(pvb.at[0:count - kept], p1_sem)

    @pl.when(old_here & home)
    def _():
        arrived(po.at[0:CELLS - 1], p2_sem)

    @pl.when(old_here & jnp.logical_not(home))
    def _():
        arrived(po, p2_sem)

    for c in range(COLB):

        @pl.when(x != c)
        def _():
            n = (c - x + XS) % XS - 1
            send(part.at[c], xin.at[n], xs_sem.at[c], xr_sem.at[n], 2 * c + h, shard).wait_send()
            onward(c).wait_send()

    @pl.when(summing)
    def _():
        to_homes(lambda n, src, dst, to: send(src, dst, gs_sem.at[n], gr_sem, rep, to).wait_send())

        for copy in row_sends:
            copy.wait_send()

    @pl.when(passing)
    def _():
        arrived(outb.at[0:SHARDS - 1], t2_sem)

    @pl.when(home)
    def _():
        half_block.wait_send()
        for copy in roots:
            copy.wait_send()
        for n in range(TILES):

            @pl.when(r == n)
            def _():
                to_rows(lambda i, src, dst, to: send(src, dst, ss_sem.at[i], sr_sem, rep, to).wait_send(), n)

    for copy in outs:
        copy.wait_send()


def store_kernel(d_in, left_in, right_in, d_out, left_new, right_new, sem):
    copies = []
    for n, (src, dst) in enumerate(((left_in, left_new), (right_in, right_new))):
        for j in range(2):
            copies.append(pltpu.make_async_copy(src.at[j], dst.at[j], sem.at[2 * n + j]))
    copies.append(pltpu.make_async_copy(d_in, d_out, sem.at[4]))
    for copy in copies:
        copy.start()
    for copy in copies:
        copy.wait()


SMEM = pl.BlockSpec(memory_space=pltpu.SMEM)
VMEM = pl.BlockSpec(memory_space=pltpu.VMEM)
ANY = pl.BlockSpec(memory_space=pl.ANY)
DMA = pltpu.SemaphoreType.DMA


def body(grads, left_prev, right_prev, block_owner, block_row, block_col):
    rows = grads.shape[1]
    direction, left_new, right_new = pl.pallas_call(
        step_kernel,
        out_shape=(
            pltpu.VMEM((TILES, 2, SUB, COLB * BLK), BF),
            pltpu.VMEM((2, BLK, BLK), F32),
            pltpu.VMEM((2, BLK, BLK), F32),
        ),
        in_specs=[SMEM, SMEM, SMEM, ANY, ANY, ANY],
        out_specs=(VMEM, VMEM, VMEM),
        scratch_shapes=[
            pltpu.VMEM((HALF, 2, 2, SUB, BLK), BF),
            pltpu.VMEM((2, 2 * HALF, SUB, BLK), F32),
            pltpu.VMEM((2, 2 * HALF, SUB, BLK), F32),
            pltpu.VMEM((TILES, SUB, COLB * BLK), BF),
            pltpu.VMEM((TILES, SUB, COLB * BLK), BF),
            pltpu.VMEM((COLB, TILES, SUB, BLK), BF),
            pltpu.VMEM((XS - 1, TILES, SUB, BLK), BF),
            pltpu.VMEM((TILES, SUB, BLK), BF),
            pltpu.VMEM((XS - 1, COLB, TILES, SUB, LANE), BF),
            pltpu.VMEM((TILES, COLB, SUB, LANE), BF),
            pltpu.VMEM((2, 2 * HALF, SUB, LANE), F32),
            pltpu.VMEM((2 * HALF, 2, SUB, LANE), BF),
            pltpu.VMEM((2 * SHARDS, SUB, LANE), BF),
            pltpu.VMEM((CELLS, SUB, LANE), BF),
            pltpu.VMEM((2 * HALF, SUB, BLK), BF),
            pltpu.VMEM((HALF, 2, SUB, BLK), BF),
            pltpu.VMEM((CELLS, SUB, LANE), BF),
            pltpu.VMEM((SHARDS, 2, SUB, LANE), BF),
            pltpu.VMEM((BLK, BLK), F32),
            pltpu.VMEM((2, BLK, BLK), BF),
            pltpu.VMEM((2, 8, LANE), F32),
            pltpu.VMEM((HALF, 2, SUB, BLK), BF),
            pltpu.VMEM((COLB, TILES, 2, SUB, BLK), BF),
            pltpu.VMEM((8, LANE), jnp.int32),
            pltpu.SMEM((8, LANE), jnp.int32),
            DMA, DMA, DMA((2,)), DMA((3,)), DMA((3,)),
            DMA, DMA, DMA, DMA, DMA((2,)), DMA, DMA((2,)), DMA, DMA, DMA, DMA, DMA((14,)), DMA((14,)),
            DMA((6,)), DMA((3,)), DMA, DMA((7,)), DMA((6,)), DMA, DMA((2,)), DMA((3,)), DMA((3,)), pltpu.SemaphoreType.REGULAR, pltpu.SemaphoreType.REGULAR,
        ],
        compiler_params=pltpu.CompilerParams(
            collective_id=0, has_side_effects=True, vmem_limit_bytes=58 * 1024 * 1024
        ),
        name="shampoo_step",
    )(
        block_owner,
        block_row,
        block_col,
        grads.reshape(TILES, 2, SUB, COLB * BLK),
        left_prev.reshape(2, 2 * HALF, SUB, BLK),
        right_prev.reshape(2, 2 * HALF, SUB, BLK),
    )

    sq = jax.ShapeDtypeStruct((2, BLK, BLK), F32)
    results = [pltpu.with_memory_space_constraint(v, pltpu.VMEM) for v in (direction, left_new, right_new)]
    direction, left_new, right_new = pl.pallas_call(
        store_kernel,
        out_shape=(jax.ShapeDtypeStruct((TILES, 2, SUB, COLB * BLK), BF), sq, sq),
        in_specs=[VMEM, VMEM, VMEM],
        out_specs=(ANY, ANY, ANY),
        scratch_shapes=[DMA((5,))],
        compiler_params=pltpu.CompilerParams(vmem_limit_bytes=16 * 1024 * 1024),
        cost_estimate=pl.CostEstimate(flops=0, bytes_accessed=9 * 2**20, transcendentals=0),
        name="store_results",
    )(*results)
    return direction.reshape(rows, COLB * BLK), left_new, right_new


def solution(mesh):
    in_specs = (P("rep", "shard", None), P("shard", None, None), P("shard", None, None), P(), P(), P())
    out_specs = (P("shard", None), P("shard", None, None), P("shard", None, None))
    return jax.shard_map(body, mesh=mesh, in_specs=in_specs, out_specs=out_specs, check_vma=False)
```

```python
import jax
import jax.numpy as jnp
from jax import lax
from jax.experimental import pallas as pl
from jax.experimental.pallas import tpu as pltpu
from jax.sharding import PartitionSpec as P

BLK = 512
COLB = 3
ROWB = 10
CELLS = 30
SHARDS = 32
HALF = 16
TILES = 5
LANE = 128
SUB = 16
XS = 4
MESH = pl.DeviceIdType.MESH
BF = jnp.bfloat16
F32 = jnp.float32


def place():
    rep = lax.axis_index("rep")
    shard = lax.axis_index("shard")
    x = rep // 2
    h = rep % 2
    return rep, shard, x, h


def send(src, dst, send_sem, recv_sem, rep, shard):
    return pltpu.make_async_remote_copy(
        src_ref=src,
        dst_ref=dst,
        send_sem=send_sem,
        recv_sem=recv_sem,
        device_id=(rep, shard),
        device_id_type=MESH,
    )


def greet(barrier, rep, shard):
    pl.semaphore_signal(barrier, inc=1, device_id=(rep, shard), device_id_type=MESH)


def eye(size):
    row = lax.broadcasted_iota(jnp.int32, (size, size), 0)
    col = lax.broadcasted_iota(jnp.int32, (size, size), 1)
    return row == col


def mm(a, b):
    return jnp.dot(a, b, preferred_element_type=F32)


def root_less_one(new, scale):
    diag = eye(BLK)
    e = 0.25 * (jnp.where(diag, 1.0, 0.0) - new * (1.0 / scale))
    eb = e.astype(BF)
    u = 2.0 * e + mm(eb, eb)
    ub = u.astype(BF)
    v = 2.0 * u + mm(ub, ub)
    w = 4.0 * u - 5.0 * e
    return u - 0.25 * v, v.astype(BF), w.astype(BF)


def fill_tables(tab, block_owner, block_row, block_col):
    sub = lax.broadcasted_iota(jnp.int32, (32, LANE), 0)
    lane = lax.broadcasted_iota(jnp.int32, (32, LANE), 1)
    owner = jnp.full((32, LANE), -1, jnp.int32)
    other = jnp.full((32, LANE), -2, jnp.int32)
    cell = jnp.full((32, LANE), -1, jnp.int32)
    for b in range(CELLS):
        owner = jnp.where(sub == b, block_owner[b], owner)
        other = jnp.where(lane == b, block_owner[b], other)
        cell = jnp.where(sub == b, block_row[b] // BLK * COLB + block_col[b] // BLK, cell)
    earlier = ((owner == other) & (lane < sub)).astype(jnp.int32)
    slot = 2 * owner + jnp.sum(earlier, axis=1, keepdims=True)
    cells = jnp.sum(jnp.where(slot == lane, cell, 0), axis=0, keepdims=True)
    slots = jnp.sum(jnp.where(cell == lane, slot, 0), axis=0, keepdims=True)
    tab[0:1] = jnp.clip(cells, 0, CELLS - 1)
    tab[1:2] = jnp.clip(slots, 0, 2 * SHARDS - 1)
    tab[2:3] = jnp.sum((slot == lane).astype(jnp.int32), axis=0, keepdims=True)


def step_kernel(
    block_owner, block_row, block_col, grads, left_prev, right_prev, d_out, left_out, right_out,
    g_own, lp, rp, own, pair, part, xin, red, xq, redq, pvf, pvb, pm, po, pv, gc, mid, outb, acc, zb, scl, pb, full, tab, look,
    own_sem, pvf_sem, pair_sem, xs_sem, xr_sem, p1_sem, p1r_sem, p2_sem, p2r_sem, gs_sem, gr_sem, ge_sem,
    t1_sem, t1r_sem, t2_sem, t2r_sem, os_sem, or_sem, z_sem, ss_sem, sr_sem, ds_sem, dr_sem, tab_sem, in_sem, qs_sem, qr_sem, ready, rows_in,
):
    rep = lax.axis_index("rep")
    shard = lax.axis_index("shard")
    x = rep // 2
    h = rep % 2
    half = shard // HALF
    w = shard % HALF
    r = w // 3
    j = w % 3
    partner = 2 * x + 1 - h
    summing = x < COLB
    def spot(a_shard):
        at = a_shard % HALF
        group, side = at // 3, at % 3
        is_home = ((side == 1) & (group < 3)) | ((side == 2) & (group >= 3))
        number = at
        for n in (1, 4, 7, 11, 14):
            number = number - (at > n).astype(jnp.int32)
        return a_shard // HALF, group, is_home, number

    _, _, home_row, number = spot(shard)
    home = summing & home_row
    passing = jnp.logical_not(home_row) & (number >= 3 * h) & (number < 3 * h + 8)

    def numbered(n):
        return (3 * n + 1 - (n > 6).astype(jnp.int32)) // 2

    def home_shard(group):
        return 3 * group + 1 + (group > 2).astype(jnp.int32)

    passed_tile = jnp.where(passing, 8 * half + number - 3 * h, 0)
    lanes = pl.ds(pl.multiple_of(x * LANE, LANE), LANE)
    barrier = pltpu.get_barrier_semaphore()

    def pass_on(src, dst, send_sem, recv_sem, to_rep, to_shard):
        me = (to_rep == rep) & (to_shard == shard)

        @pl.when(jnp.logical_not(me))
        def _():
            send(src, dst, send_sem, recv_sem, to_rep, to_shard).start()

        @pl.when(me)
        def _():
            pltpu.make_async_copy(src, dst, recv_sem).start()

    def arrived(ref, sem):
        pltpu.make_async_copy(ref, ref, sem).wait()

    def loop(count, fn):
        def step(n, carry):
            fn(n)
            return carry

        lax.fori_loop(0, count, step, 0)

    def far(n):
        i, m = n // 4, n % 4
        dz = 4 + jnp.where(i % 2 == 0, i // 2, -((i + 1) // 2))
        dy = 2 + jnp.where(m % 2 == 0, m // 2, -((m + 1) // 2))
        return (shard // 8 + dy) % 4 * 8 + (shard % 8 + dz) % 8

    row0 = shard // 8 * 8
    loop(7, lambda n: greet(barrier, rep, row0 + (shard + 1 + n) % 8))
    loop(3, lambda n: greet(barrier, rep, (shard + 8 * n + 8) % SHARDS))
    for n in range(1, XS):
        greet(barrier, 2 * ((x + n) % XS) + h, shard)
    greet(barrier, partner, shard)
    load = pltpu.make_async_copy(grads.at[:, h], own, own_sem)
    load.start()

    @pl.when(h == 0)
    def _():
        pltpu.make_async_copy(left_prev.at[:, :, :, lanes], pvf, pvf_sem).start()

    @pl.when(h == 1)
    def _():
        pltpu.make_async_copy(right_prev.at[:, :, :, lanes], pvf, pvf_sem).start()

    whole = [
        pltpu.make_async_copy(left_prev, lp, in_sem.at[0]),
        pltpu.make_async_copy(right_prev, rp, in_sem.at[1]),
    ]
    arrived(pvf, pvf_sem)
    for n in range(2):
        pvb[:, n] = pvf[n].astype(BF)
    pl.semaphore_wait(barrier, 10 + XS)

    swap = send(grads.at[:, 1 - h], pair, pair_sem.at[0], pair_sem.at[1], partner, shard)
    swap.start()
    def row_in(n):
        pl.semaphore_signal(
            rows_in, inc=1, device_id=(rep, (shard + 8 * n + 8) % SHARDS), device_id_type=MESH
        )

    loop(3, row_in)
    pl.semaphore_wait(rows_in, 3)
    for n in range(1, XS):
        pl.semaphore_signal(
            ready, inc=1, device_id=(2 * ((x + n) % XS) + h, shard), device_id_type=MESH
        )
    def taker(a_shard):
        of, group, is_home, number = spot(a_shard)
        free = number - 8 * (1 - h)
        here = jnp.logical_not(summing) | is_home | ((free >= 0) & (free < 3))
        rows = 8 * jnp.where(of == 0, x, (x + 1) % COLB) + jnp.where(is_home, group, 5 + free)
        return here, jnp.where(here, jnp.where(summing, rows, a_shard), 0)

    old_here, old_tile = taker(shard)
    mine = pm.at[pl.ds(2 * shard, 2)]
    def give_old(n):
        to = far(n)
        here, t = taker(to)

        @pl.when(here)
        def _():
            send(pvb.at[t], mine, p1_sem, p1r_sem, rep, to).start()

    loop(SHARDS - 1, give_old)

    @pl.when(old_here)
    def _():
        pltpu.make_async_copy(pvb.at[old_tile], mine, p1r_sem).start()

    fill_tables(tab, block_owner, block_row, block_col)
    tables = pltpu.make_async_copy(tab, look, tab_sem)
    tables.start()
    for copy in whole:
        copy.start()
    load.wait()
    swap.wait_recv()
    for c in range(COLB):
        cols = slice(c * BLK, (c + 1) * BLK)
        part[c] = (own[:, :, cols].astype(F32) + pair[:, :, cols].astype(F32)).astype(BF)
    shares = []
    for n in range(1, XS):
        to = (x + n) % XS
        cols = pl.ds(pl.multiple_of(to * LANE, LANE), LANE)
        shares.append(
            send(part.at[:, :, :, cols], xq.at[n - 1], qs_sem.at[n - 1], qr_sem.at[n - 1], 2 * to + h, shard)
        )
    for copy in shares:
        copy.start()

    for c in range(COLB):

        @pl.when(x != c)
        def _():
            n = (c - x + XS) % XS - 1
            send(part.at[c], xin.at[n], xs_sem.at[c], xr_sem.at[n], 2 * c + h, shard).start()

    tables.wait()
    pl.semaphore_wait(ready, XS - 1)
    def to_homes(act):
        @pl.when((j == 2) & (r < 3))
        def _():
            act(0, red, gc.at[pl.ds(10 - r, TILES), h], shard - 1)

        @pl.when((j == 1) & (r >= 3))
        def _():
            act(0, red, gc.at[pl.ds(TILES - r, TILES), h], shard + 1)

        for n in range(6):

            @pl.when((j == 0) & (r == n))
            def _():
                if n > 0:
                    act(0, red.at[0:n], gc.at[16 - n:16, h], shard - (2 if n < 4 else 1))
                if n < TILES:
                    act(1, red.at[n:TILES], gc.at[0:TILES - n, h], shard + (1 if n < 3 else 2))

    def passing_tile(n):
        u = TILES * w + n
        k = u % HALF
        to = HALF * (k // 8) + numbered(k % 8 + 3 * h)
        return redq.at[n], mid.at[pl.ds(COLB * (5 * half + u // HALF), COLB)], to

    tile_at_home = pv.at[old_tile, :, lanes]

    def give_group(to, start):
        of, group, _, _ = spot(to)
        for c in range(COLB):
            cell = COLB * (5 * of + group) + c
            po[cell] = pm[look[1, cell]]
            start(po.at[cell], tile_at_home, p2_sem, p2r_sem, 2 * c + h, to)

    def give_factors(n):
        to = far(n)

        @pl.when(spot(to)[2])
        def _():
            give_group(to, lambda *args: send(*args).start())

    @pl.when(old_here)
    def _():
        arrived(pm, p1r_sem)
        loop(SHARDS - 1, give_factors)

        @pl.when(home_row)
        def _():
            give_group(shard, pass_on)


    for copy in shares:
        copy.wait_recv()
    for c in range(COLB):
        redq[:, c] = (
            (part[c, :, :, lanes].astype(F32) + xq[0, c].astype(F32))
            + (xq[1, c].astype(F32) + xq[2, c].astype(F32))
        ).astype(BF)
    for n in range(TILES):
        src, dst, to = passing_tile(n)
        pass_on(src, dst, t1_sem, t1r_sem, rep, to)

    @pl.when(summing)
    def _():
        for n in range(XS - 1):
            arrived(xin.at[n], xr_sem.at[n])
        red[...] = (
            (part[x].astype(F32) + xin[0].astype(F32)) + (xin[1].astype(F32) + xin[2].astype(F32))
        ).astype(BF)
        to_homes(lambda n, src, dst, to: send(src, dst, gs_sem.at[n], gr_sem, rep, to).start())

        @pl.when(home)
        def _():
            pltpu.make_async_copy(red, gc.at[pl.ds(TILES * j - r, TILES), h], gr_sem).start()

    half_block = send(gc.at[:, h], gc.at[:, h], ge_sem.at[0], ge_sem.at[1], partner, shard)

    @pl.when(home)
    def _():
        arrived(gc.at[:, h], gr_sem)
        half_block.start()

    def view(hh, col):
        return g_own.at[:, :, hh, :, pl.ds(pl.multiple_of(col * LANE, LANE), LANE)]

    @pl.when(passing)
    def _():
        arrived(mid, t1r_sem)

        def fill(o):
            for n in range(2):
                outb[o, n] = mid[look[0, 2 * o + n]]

        slots_at_owner = g_own.at[passed_tile, :, h, :, lanes]

        def give_slots(n):
            o = far(n)
            fill(o)
            send(outb.at[o], slots_at_owner, t2_sem, t2r_sem, rep, o).start()

        loop(SHARDS - 1, give_slots)
        fill(shard)
        pltpu.make_async_copy(outb.at[shard], slots_at_owner, t2r_sem).start()

    halves = (pl.ds(0, BLK // 2), pl.ds(BLK // 2, BLK // 2))
    roots = [
        send(zb.at[h, rows], zb.at[h, rows], z_sem.at[n], z_sem.at[3 + n], partner, shard)
        for n, rows in enumerate(halves)
    ]
    roots.append(send(scl.at[h], scl.at[h], z_sem.at[2], z_sem.at[5], partner, shard))

    def to_rows(act, n):
        early = n < 3
        act(0, pb.at[0:TILES - n, h], full.at[x, n:TILES, h], shard - (1 if early else 2))
        if early:
            act(1, pb.at[10 - n:15 - n, h], full.at[x, :, h], shard + 1)
        else:
            act(1, pb.at[5 - n:10 - n, h], full.at[x, :, h], shard - 1)
        act(2, pb.at[15 - n:16, h], full.at[x, 0:1 + n, h], shard + (2 if early else 1))

    @pl.when(home)
    def _():
        other = gc.at[:, 1 - h]
        arrived(other, ge_sem.at[1])
        g = gc[...].reshape(BLK, BLK)
        gt = g.T
        gf = g.astype(F32)
        sg = jnp.full((8, LANE), jnp.sum(gf * gf), F32)

        @pl.when(h == 0)
        def _():
            acc[...] = mm(g, gt)

        @pl.when(h == 1)
        def _():
            acc[...] = mm(gt, g)

        arrived(pv.at[0:20], p2r_sem)
        for a, b in ((2, 0), (0, 1), (1, 2), (3, 0), (3, 1), (3, 2)):
            there = pv[8 * b:8 * b + 8, :, a * LANE:(a + 1) * LANE].reshape(LANE, LANE)
            pv[8 * a:8 * a + 8, :, b * LANE:(b + 1) * LANE] = there.T.reshape(8, SUB, LANE)
        val = acc[...] + pv[...].reshape(BLK, BLK).astype(F32)
        scale = jnp.sum(jnp.where(eye(BLK), val, 0.0)) * (1.0 / BLK)
        scl[h] = lax.rsqrt(jnp.sqrt(jnp.full((8, LANE), scale, F32)))
        roots[2].start()
        rest, v, u = root_less_one(val, scale)
        for n, rows in enumerate(halves):
            part_v = v[n * (BLK // 2):(n + 1) * (BLK // 2)]
            zb[h, rows] = (rest[n * (BLK // 2):(n + 1) * (BLK // 2)] + 0.25 * mm(part_v, u)).astype(BF)
            roots[n].start()

        @pl.when(h == 0)
        def _():
            acc[...] = scl[0, 0:1, 0:1] * (gf + mm(zb[0], g))

        @pl.when(h == 1)
        def _():
            acc[...] = scl[1, 0:1, 0:1] * (gf + mm(g, zb[1]))

        y = acc[...]
        for n, rows in enumerate(halves):
            arrived(zb.at[1 - h, rows], z_sem.at[3 + n])
        arrived(scl.at[1 - h], z_sem.at[5])

        @pl.when(h == 0)
        def _():
            acc[...] = scl[1, 0:1, 0:1] * (y + mm(y.astype(BF), zb[1]))

        @pl.when(h == 1)
        def _():
            acc[...] = scl[0, 0:1, 0:1] * (y + mm(zb[0], y.astype(BF)))

        p = acc[...]
        sp = jnp.full((8, LANE), jnp.sum(p * p), F32)
        ratio = jnp.sqrt(sg / (sp + 1e-06))[0:1, 0:1]
        pb[...] = (p * ratio).astype(BF).reshape(HALF, 2, SUB, BLK)
        for n in range(TILES):

            @pl.when(r == n)
            def _():
                to_rows(lambda i, src, dst, to: send(src, dst, ss_sem.at[i], sr_sem, rep, to).start(), n)
                at = (5 if n < 3 else 10) - n
                pltpu.make_async_copy(pb.at[at:at + TILES, h], full.at[x, :, h], sr_sem).start()

    owned = view(h, x)
    arrived(owned, t2r_sem)
    outs = []
    for n in (2, 1, 3):
        outs.append(send(owned, owned, os_sem.at[n], or_sem.at[n], 2 * ((x + n) % XS) + h, shard))
    outs.append(send(owned, owned, os_sem.at[0], or_sem.at[0], partner, shard))
    for copy in outs:
        copy.start()

    rows = full.at[x, :, h]
    row_sends = [
        send(rows, rows, ds_sem.at[n], dr_sem.at[x], 2 * ((x + n) % XS) + h, shard) for n in (2, 1, 3)
    ]
    row_sends.append(send(rows, rows, ds_sem.at[0], dr_sem.at[COLB + x], partner, shard))

    @pl.when(summing)
    def _():
        arrived(rows, sr_sem)
        for copy in row_sends:
            copy.start()

    def to_partner(n):
        piece = view(h, (x + XS - n) % XS)
        arrived(piece, or_sem.at[n])
        copy = send(piece, piece, os_sem.at[3 + n], or_sem.at[3 + n], partner, shard)
        copy.start()
        outs.append(copy)

    for n in (1, 3, 2):
        to_partner(n)

    def onward(c):
        return send(
            full.at[c, :, h], full.at[c, :, h], ds_sem.at[XS + c], dr_sem.at[COLB + c], partner, shard
        )

    for c in range(COLB):

        @pl.when(x != c)
        def _():
            arrived(full.at[c, :, h], dr_sem.at[c])
            onward(c).start()

    for copy in whole:
        copy.wait()

    def factors(n):
        on = look[2, 2 * shard + n] > 0
        g = g_own[:, n].reshape(BLK, BLK)
        g = jnp.where(on, g, jnp.zeros_like(g))
        gt = g.T
        for prev, out, a, b in ((lp, left_out, g, gt), (rp, right_out, gt, g)):
            new = prev[n].reshape(BLK, BLK) + mm(a, b)
            out[n] = jnp.where(on, new, jnp.zeros_like(new))

    for index, m in ((0, 0), (4, 1), (6, 3), (5, 2)):
        arrived(view(1 - h, (x + XS - m) % XS), or_sem.at[index])
    for n in range(2):
        factors(n)
    for c in range(COLB):
        arrived(full.at[c, :, 1 - h], dr_sem.at[COLB + c])
        d_out[:, :, :, c * BLK:(c + 1) * BLK] = full[c]

    kept = passing & ((passed_tile - TILES * w + 5 * HALF) % HALF < TILES)

    @pl.when(kept)
    def _():
        arrived(mid.at[0:COLB * (TILES - 1)], t1_sem)

    @pl.when(jnp.logical_not(kept))
    def _():
        arrived(mid.at[0:COLB * TILES], t1_sem)

    for copy in shares:
        copy.wait_send()
    swap.wait_send()
    for count, kept in ((16, 0), (16, 1), (32, 1)):

        @pl.when((jnp.where(summing, HALF, SHARDS) == count) & (old_here.astype(jnp.int32) == kept))
        def _():
            arrived(pvb.at[0:count - kept], p1_sem)

    @pl.when(old_here & home)
    def _():
        arrived(po.at[0:CELLS - 1], p2_sem)

    @pl.when(old_here & jnp.logical_not(home))
    def _():
        arrived(po, p2_sem)

    for c in range(COLB):

        @pl.when(x != c)
        def _():
            n = (c - x + XS) % XS - 1
            send(part.at[c], xin.at[n], xs_sem.at[c], xr_sem.at[n], 2 * c + h, shard).wait_send()
            onward(c).wait_send()

    @pl.when(summing)
    def _():
        to_homes(lambda n, src, dst, to: send(src, dst, gs_sem.at[n], gr_sem, rep, to).wait_send())

        for copy in row_sends:
            copy.wait_send()

    @pl.when(passing)
    def _():
        arrived(outb.at[0:SHARDS - 1], t2_sem)

    @pl.when(home)
    def _():
        half_block.wait_send()
        for copy in roots:
            copy.wait_send()
        for n in range(TILES):

            @pl.when(r == n)
            def _():
                to_rows(lambda i, src, dst, to: send(src, dst, ss_sem.at[i], sr_sem, rep, to).wait_send(), n)

    for copy in outs:
        copy.wait_send()


def store_kernel(d_in, left_in, right_in, d_out, left_new, right_new, sem):
    copies = []
    for n, (src, dst) in enumerate(((left_in, left_new), (right_in, right_new))):
        for j in range(2):
            copies.append(pltpu.make_async_copy(src.at[j], dst.at[j], sem.at[2 * n + j]))
    copies.append(pltpu.make_async_copy(d_in, d_out, sem.at[4]))
    for copy in copies:
        copy.start()
    for copy in copies:
        copy.wait()


SMEM = pl.BlockSpec(memory_space=pltpu.SMEM)
VMEM = pl.BlockSpec(memory_space=pltpu.VMEM)
ANY = pl.BlockSpec(memory_space=pl.ANY)
DMA = pltpu.SemaphoreType.DMA


def body(grads, left_prev, right_prev, block_owner, block_row, block_col):
    rows = grads.shape[1]
    direction, left_new, right_new = pl.pallas_call(
        step_kernel,
        out_shape=(
            pltpu.VMEM((TILES, 2, SUB, COLB * BLK), BF),
            pltpu.VMEM((2, BLK, BLK), F32),
            pltpu.VMEM((2, BLK, BLK), F32),
        ),
        in_specs=[SMEM, SMEM, SMEM, ANY, ANY, ANY],
        out_specs=(VMEM, VMEM, VMEM),
        scratch_shapes=[
            pltpu.VMEM((HALF, 2, 2, SUB, BLK), BF),
            pltpu.VMEM((2, 2 * HALF, SUB, BLK), F32),
            pltpu.VMEM((2, 2 * HALF, SUB, BLK), F32),
            pltpu.VMEM((TILES, SUB, COLB * BLK), BF),
            pltpu.VMEM((TILES, SUB, COLB * BLK), BF),
            pltpu.VMEM((COLB, TILES, SUB, BLK), BF),
            pltpu.VMEM((XS - 1, TILES, SUB, BLK), BF),
            pltpu.VMEM((TILES, SUB, BLK), BF),
            pltpu.VMEM((XS - 1, COLB, TILES, SUB, LANE), BF),
            pltpu.VMEM((TILES, COLB, SUB, LANE), BF),
            pltpu.VMEM((2, 2 * HALF, SUB, LANE), F32),
            pltpu.VMEM((2 * HALF, 2, SUB, LANE), BF),
            pltpu.VMEM((2 * SHARDS, SUB, LANE), BF),
            pltpu.VMEM((CELLS, SUB, LANE), BF),
            pltpu.VMEM((2 * HALF, SUB, BLK), BF),
            pltpu.VMEM((HALF, 2, SUB, BLK), BF),
            pltpu.VMEM((CELLS, SUB, LANE), BF),
            pltpu.VMEM((SHARDS, 2, SUB, LANE), BF),
            pltpu.VMEM((BLK, BLK), F32),
            pltpu.VMEM((2, BLK, BLK), BF),
            pltpu.VMEM((2, 8, LANE), F32),
            pltpu.VMEM((HALF, 2, SUB, BLK), BF),
            pltpu.VMEM((COLB, TILES, 2, SUB, BLK), BF),
            pltpu.VMEM((8, LANE), jnp.int32),
            pltpu.SMEM((8, LANE), jnp.int32),
            DMA, DMA, DMA((2,)), DMA((3,)), DMA((3,)),
            DMA, DMA, DMA, DMA, DMA((2,)), DMA, DMA((2,)), DMA, DMA, DMA, DMA, DMA((7,)), DMA((7,)),
            DMA((6,)), DMA((3,)), DMA, DMA((7,)), DMA((6,)), DMA, DMA((2,)), DMA((3,)), DMA((3,)), pltpu.SemaphoreType.REGULAR, pltpu.SemaphoreType.REGULAR,
        ],
        compiler_params=pltpu.CompilerParams(
            collective_id=0, has_side_effects=True, vmem_limit_bytes=58 * 1024 * 1024
        ),
        name="shampoo_step",
    )(
        block_owner,
        block_row,
        block_col,
        grads.reshape(TILES, 2, SUB, COLB * BLK),
        left_prev.reshape(2, 2 * HALF, SUB, BLK),
        right_prev.reshape(2, 2 * HALF, SUB, BLK),
    )

    sq = jax.ShapeDtypeStruct((2, BLK, BLK), F32)
    results = [pltpu.with_memory_space_constraint(v, pltpu.VMEM) for v in (direction, left_new, right_new)]
    direction, left_new, right_new = pl.pallas_call(
        store_kernel,
        out_shape=(jax.ShapeDtypeStruct((TILES, 2, SUB, COLB * BLK), BF), sq, sq),
        in_specs=[VMEM, VMEM, VMEM],
        out_specs=(ANY, ANY, ANY),
        scratch_shapes=[DMA((5,))],
        compiler_params=pltpu.CompilerParams(vmem_limit_bytes=16 * 1024 * 1024),
        cost_estimate=pl.CostEstimate(flops=0, bytes_accessed=9 * 2**20, transcendentals=0),
        name="store_results",
    )(*results)
    return direction.reshape(rows, COLB * BLK), left_new, right_new


def solution(mesh):
    in_specs = (P("rep", "shard", None), P("shard", None, None), P("shard", None, None), P(), P(), P())
    out_specs = (P("shard", None), P("shard", None, None), P("shard", None, None))
    return jax.shard_map(body, mesh=mesh, in_specs=in_specs, out_specs=out_specs, check_vma=False)
```

```python
import jax
import jax.numpy as jnp
from jax import lax
from jax.experimental import pallas as pl
from jax.experimental.pallas import tpu as pltpu
from jax.sharding import PartitionSpec as P

BLK = 512
COLB = 3
ROWB = 10
CELLS = 30
SHARDS = 32
HALF = 16
TILES = 5
LANE = 128
SUB = 16
XS = 4
MESH = pl.DeviceIdType.MESH
BF = jnp.bfloat16
F32 = jnp.float32


def place():
    rep = lax.axis_index("rep")
    shard = lax.axis_index("shard")
    x = rep // 2
    h = rep % 2
    return rep, shard, x, h


def send(src, dst, send_sem, recv_sem, rep, shard):
    return pltpu.make_async_remote_copy(
        src_ref=src,
        dst_ref=dst,
        send_sem=send_sem,
        recv_sem=recv_sem,
        device_id=(rep, shard),
        device_id_type=MESH,
    )


def greet(barrier, rep, shard):
    pl.semaphore_signal(barrier, inc=1, device_id=(rep, shard), device_id_type=MESH)


def eye(size):
    row = lax.broadcasted_iota(jnp.int32, (size, size), 0)
    col = lax.broadcasted_iota(jnp.int32, (size, size), 1)
    return row == col


def mm(a, b):
    return jnp.dot(a, b, preferred_element_type=F32)


def root_less_one(new, scale):
    diag = eye(BLK)
    e = 0.25 * (jnp.where(diag, 1.0, 0.0) - new * (1.0 / scale))
    eb = e.astype(BF)
    u = 2.0 * e + mm(eb, eb)
    ub = u.astype(BF)
    v = 2.0 * u + mm(ub, ub)
    w = 4.0 * u - 5.0 * e
    return u - 0.25 * v, v.astype(BF), w.astype(BF)


def fill_tables(tab, block_owner, block_row, block_col):
    sub = lax.broadcasted_iota(jnp.int32, (32, LANE), 0)
    lane = lax.broadcasted_iota(jnp.int32, (32, LANE), 1)
    owner = jnp.full((32, LANE), -1, jnp.int32)
    other = jnp.full((32, LANE), -2, jnp.int32)
    cell = jnp.full((32, LANE), -1, jnp.int32)
    for b in range(CELLS):
        owner = jnp.where(sub == b, block_owner[b], owner)
        other = jnp.where(lane == b, block_owner[b], other)
        cell = jnp.where(sub == b, block_row[b] // BLK * COLB + block_col[b] // BLK, cell)
    earlier = ((owner == other) & (lane < sub)).astype(jnp.int32)
    slot = 2 * owner + jnp.sum(earlier, axis=1, keepdims=True)
    cells = jnp.sum(jnp.where(slot == lane, cell, 0), axis=0, keepdims=True)
    slots = jnp.sum(jnp.where(cell == lane, slot, 0), axis=0, keepdims=True)
    tab[0:1] = jnp.clip(cells, 0, CELLS - 1)
    tab[1:2] = jnp.clip(slots, 0, 2 * SHARDS - 1)
    tab[2:3] = jnp.sum((slot == lane).astype(jnp.int32), axis=0, keepdims=True)


def step_kernel(
    block_owner, block_row, block_col, grads, left_prev, right_prev, d_out, left_out, right_out,
    g_own, lp, rp, own, pair, part, xin, red, xq, redq, pvf, pvb, pm, po, pv, gc, mid, outb, acc, zb, scl, pb, full, tab, look,
    own_sem, pvf_sem, pair_sem, xs_sem, xr_sem, p1_sem, p1r_sem, p2_sem, p2r_sem, gs_sem, gr_sem, ge_sem,
    t1_sem, t1r_sem, t2_sem, t2r_sem, os_sem, or_sem, z_sem, ss_sem, sr_sem, ds_sem, dr_sem, tab_sem, in_sem, qs_sem, qr_sem, ready, rows_in,
):
    rep = lax.axis_index("rep")
    shard = lax.axis_index("shard")
    x = rep // 2
    h = rep % 2
    half = shard // HALF
    w = shard % HALF
    r = w // 3
    j = w % 3
    partner = 2 * x + 1 - h
    summing = x < COLB
    def spot(a_shard):
        at = a_shard % HALF
        group, side = at // 3, at % 3
        is_home = ((side == 1) & (group < 3)) | ((side == 2) & (group >= 3))
        number = at
        for n in (1, 4, 7, 11, 14):
            number = number - (at > n).astype(jnp.int32)
        return a_shard // HALF, group, is_home, number

    _, _, home_row, number = spot(shard)
    home = summing & home_row
    passing = jnp.logical_not(home_row) & (number >= 3 * h) & (number < 3 * h + 8)

    def numbered(n):
        return (3 * n + 1 - (n > 6).astype(jnp.int32)) // 2

    def home_shard(group):
        return 3 * group + 1 + (group > 2).astype(jnp.int32)

    passed_tile = jnp.where(passing, 8 * half + number - 3 * h, 0)
    lanes = pl.ds(pl.multiple_of(x * LANE, LANE), LANE)
    barrier = pltpu.get_barrier_semaphore()

    def pass_on(src, dst, send_sem, recv_sem, to_rep, to_shard):
        me = (to_rep == rep) & (to_shard == shard)

        @pl.when(jnp.logical_not(me))
        def _():
            send(src, dst, send_sem, recv_sem, to_rep, to_shard).start()

        @pl.when(me)
        def _():
            pltpu.make_async_copy(src, dst, recv_sem).start()

    def arrived(ref, sem):
        pltpu.make_async_copy(ref, ref, sem).wait()

    def loop(count, fn):
        def step(n, carry):
            fn(n)
            return carry

        lax.fori_loop(0, count, step, 0)

    def far(n):
        i, m = n // 4, n % 4
        dz = 4 + jnp.where(i % 2 == 0, i // 2, -((i + 1) // 2))
        dy = 2 + jnp.where(m % 2 == 0, m // 2, -((m + 1) // 2))
        return (shard // 8 + dy) % 4 * 8 + (shard % 8 + dz) % 8

    row0 = shard // 8 * 8
    loop(7, lambda n: greet(barrier, rep, row0 + (shard + 1 + n) % 8))
    loop(3, lambda n: greet(barrier, rep, (shard + 8 * n + 8) % SHARDS))
    for n in range(1, XS):
        greet(barrier, 2 * ((x + n) % XS) + h, shard)
    greet(barrier, partner, shard)
    load = pltpu.make_async_copy(grads.at[:, h], own, own_sem)
    load.start()

    @pl.when(h == 0)
    def _():
        pltpu.make_async_copy(left_prev.at[:, :, :, lanes], pvf, pvf_sem).start()

    @pl.when(h == 1)
    def _():
        pltpu.make_async_copy(right_prev.at[:, :, :, lanes], pvf, pvf_sem).start()

    whole = [
        pltpu.make_async_copy(left_prev, lp, in_sem.at[0]),
        pltpu.make_async_copy(right_prev, rp, in_sem.at[1]),
    ]
    arrived(pvf, pvf_sem)
    for n in range(2):
        pvb[:, n] = pvf[n].astype(BF)
    pl.semaphore_wait(barrier, 10 + XS)

    swap = send(grads.at[:, 1 - h], pair, pair_sem.at[0], pair_sem.at[1], partner, shard)
    swap.start()
    def row_in(n):
        pl.semaphore_signal(
            rows_in, inc=1, device_id=(rep, (shard + 8 * n + 8) % SHARDS), device_id_type=MESH
        )

    loop(3, row_in)
    fill_tables(tab, block_owner, block_row, block_col)
    tables = pltpu.make_async_copy(tab, look, tab_sem)
    tables.start()
    pl.semaphore_wait(rows_in, 3)
    for n in range(1, XS):
        pl.semaphore_signal(
            ready, inc=1, device_id=(2 * ((x + n) % XS) + h, shard), device_id_type=MESH
        )
    def taker(a_shard):
        of, group, is_home, number = spot(a_shard)
        free = number - 8 * (1 - h)
        here = jnp.logical_not(summing) | is_home | ((free >= 0) & (free < 3))
        rows = 8 * jnp.where(of == 0, x, (x + 1) % COLB) + jnp.where(is_home, group, 5 + free)
        return here, jnp.where(here, jnp.where(summing, rows, a_shard), 0)

    old_here, old_tile = taker(shard)
    mine = pm.at[pl.ds(2 * shard, 2)]
    def give_old(n):
        to = far(n)
        here, t = taker(to)

        @pl.when(here)
        def _():
            send(pvb.at[t], mine, p1_sem, p1r_sem, rep, to).start()

    loop(SHARDS - 1, give_old)

    @pl.when(old_here)
    def _():
        pltpu.make_async_copy(pvb.at[old_tile], mine, p1r_sem).start()

    for copy in whole:
        copy.start()
    load.wait()
    swap.wait_recv()
    for c in range(COLB):
        cols = slice(c * BLK, (c + 1) * BLK)
        part[c] = (own[:, :, cols].astype(F32) + pair[:, :, cols].astype(F32)).astype(BF)
    shares = []
    for n in range(1, XS):
        to = (x + n) % XS
        cols = pl.ds(pl.multiple_of(to * LANE, LANE), LANE)
        shares.append(
            send(part.at[:, :, :, cols], xq.at[n - 1], qs_sem.at[n - 1], qr_sem.at[n - 1], 2 * to + h, shard)
        )
    for copy in shares:
        copy.start()

    for c in range(COLB):

        @pl.when(x != c)
        def _():
            n = (c - x + XS) % XS - 1
            send(part.at[c], xin.at[n], xs_sem.at[c], xr_sem.at[n], 2 * c + h, shard).start()

    tables.wait()
    pl.semaphore_wait(ready, XS - 1)
    def to_homes(act):
        @pl.when((j == 2) & (r < 3))
        def _():
            act(0, red, gc.at[pl.ds(10 - r, TILES), h], shard - 1)

        @pl.when((j == 1) & (r >= 3))
        def _():
            act(0, red, gc.at[pl.ds(TILES - r, TILES), h], shard + 1)

        for n in range(6):

            @pl.when((j == 0) & (r == n))
            def _():
                if n > 0:
                    act(0, red.at[0:n], gc.at[16 - n:16, h], shard - (2 if n < 4 else 1))
                if n < TILES:
                    act(1, red.at[n:TILES], gc.at[0:TILES - n, h], shard + (1 if n < 3 else 2))

    def passing_tile(n):
        u = TILES * w + n
        k = u % HALF
        to = HALF * (k // 8) + numbered(k % 8 + 3 * h)
        return redq.at[n], mid.at[pl.ds(COLB * (5 * half + u // HALF), COLB)], to

    tile_at_home = pv.at[old_tile, :, lanes]

    def give_group(to, start):
        of, group, _, _ = spot(to)
        for c in range(COLB):
            cell = COLB * (5 * of + group) + c
            po[cell] = pm[look[1, cell]]
            start(po.at[cell], tile_at_home, p2_sem, p2r_sem, 2 * c + h, to)

    def give_factors(n):
        to = far(n)

        @pl.when(spot(to)[2])
        def _():
            give_group(to, lambda *args: send(*args).start())

    @pl.when(old_here)
    def _():
        arrived(pm, p1r_sem)
        loop(SHARDS - 1, give_factors)

        @pl.when(home_row)
        def _():
            give_group(shard, pass_on)


    for copy in shares:
        copy.wait_recv()
    for c in range(COLB):
        redq[:, c] = (
            (part[c, :, :, lanes].astype(F32) + xq[0, c].astype(F32))
            + (xq[1, c].astype(F32) + xq[2, c].astype(F32))
        ).astype(BF)
    for n in range(TILES):
        src, dst, to = passing_tile(n)
        pass_on(src, dst, t1_sem, t1r_sem, rep, to)

    @pl.when(summing)
    def _():
        for n in range(XS - 1):
            arrived(xin.at[n], xr_sem.at[n])
        red[...] = (
            (part[x].astype(F32) + xin[0].astype(F32)) + (xin[1].astype(F32) + xin[2].astype(F32))
        ).astype(BF)
        to_homes(lambda n, src, dst, to: send(src, dst, gs_sem.at[n], gr_sem, rep, to).start())

        @pl.when(home)
        def _():
            pltpu.make_async_copy(red, gc.at[pl.ds(TILES * j - r, TILES), h], gr_sem).start()

    half_block = send(gc.at[:, h], gc.at[:, h], ge_sem.at[0], ge_sem.at[1], partner, shard)

    @pl.when(home)
    def _():
        arrived(gc.at[:, h], gr_sem)
        half_block.start()

    def view(hh, col):
        return g_own.at[:, :, hh, :, pl.ds(pl.multiple_of(col * LANE, LANE), LANE)]

    @pl.when(passing)
    def _():
        arrived(mid, t1r_sem)

        def fill(o):
            for n in range(2):
                outb[o, n] = mid[look[0, 2 * o + n]]

        slots_at_owner = g_own.at[passed_tile, :, h, :, lanes]

        def give_slots(n):
            o = far(n)
            fill(o)
            send(outb.at[o], slots_at_owner, t2_sem, t2r_sem, rep, o).start()

        loop(SHARDS - 1, give_slots)
        fill(shard)
        pltpu.make_async_copy(outb.at[shard], slots_at_owner, t2r_sem).start()

    halves = (pl.ds(0, BLK // 2), pl.ds(BLK // 2, BLK // 2))
    roots = [
        send(zb.at[h, rows], zb.at[h, rows], z_sem.at[n], z_sem.at[3 + n], partner, shard)
        for n, rows in enumerate(halves)
    ]
    roots.append(send(scl.at[h], scl.at[h], z_sem.at[2], z_sem.at[5], partner, shard))

    def to_rows(act, n):
        early = n < 3
        act(0, pb.at[0:TILES - n, h], full.at[x, n:TILES, h], shard - (1 if early else 2))
        if early:
            act(1, pb.at[10 - n:15 - n, h], full.at[x, :, h], shard + 1)
        else:
            act(1, pb.at[5 - n:10 - n, h], full.at[x, :, h], shard - 1)
        act(2, pb.at[15 - n:16, h], full.at[x, 0:1 + n, h], shard + (2 if early else 1))

    @pl.when(home)
    def _():
        other = gc.at[:, 1 - h]
        arrived(other, ge_sem.at[1])
        g = gc[...].reshape(BLK, BLK)
        gt = g.T
        gf = g.astype(F32)
        sg = jnp.full((8, LANE), jnp.sum(gf * gf), F32)

        @pl.when(h == 0)
        def _():
            acc[...] = mm(g, gt)

        @pl.when(h == 1)
        def _():
            acc[...] = mm(gt, g)

        arrived(pv.at[0:20], p2r_sem)
        for a, b in ((2, 0), (0, 1), (1, 2), (3, 0), (3, 1), (3, 2)):
            there = pv[8 * b:8 * b + 8, :, a * LANE:(a + 1) * LANE].reshape(LANE, LANE)
            pv[8 * a:8 * a + 8, :, b * LANE:(b + 1) * LANE] = there.T.reshape(8, SUB, LANE)
        val = acc[...] + pv[...].reshape(BLK, BLK).astype(F32)
        scale = jnp.sum(jnp.where(eye(BLK), val, 0.0)) * (1.0 / BLK)
        scl[h] = lax.rsqrt(jnp.sqrt(jnp.full((8, LANE), scale, F32)))
        roots[2].start()
        rest, v, u = root_less_one(val, scale)
        for n, rows in enumerate(halves):
            part_v = v[n * (BLK // 2):(n + 1) * (BLK // 2)]
            zb[h, rows] = (rest[n * (BLK // 2):(n + 1) * (BLK // 2)] + 0.25 * mm(part_v, u)).astype(BF)
            roots[n].start()

        @pl.when(h == 0)
        def _():
            acc[...] = scl[0, 0:1, 0:1] * (gf + mm(zb[0], g))

        @pl.when(h == 1)
        def _():
            acc[...] = scl[1, 0:1, 0:1] * (gf + mm(g, zb[1]))

        y = acc[...]
        for n, rows in enumerate(halves):
            arrived(zb.at[1 - h, rows], z_sem.at[3 + n])
        arrived(scl.at[1 - h], z_sem.at[5])

        @pl.when(h == 0)
        def _():
            acc[...] = scl[1, 0:1, 0:1] * (y + mm(y.astype(BF), zb[1]))

        @pl.when(h == 1)
        def _():
            acc[...] = scl[0, 0:1, 0:1] * (y + mm(zb[0], y.astype(BF)))

        p = acc[...]
        sp = jnp.full((8, LANE), jnp.sum(p * p), F32)
        ratio = jnp.sqrt(sg / (sp + 1e-06))[0:1, 0:1]
        pb[...] = (p * ratio).astype(BF).reshape(HALF, 2, SUB, BLK)
        for n in range(TILES):

            @pl.when(r == n)
            def _():
                to_rows(lambda i, src, dst, to: send(src, dst, ss_sem.at[i], sr_sem, rep, to).start(), n)
                at = (5 if n < 3 else 10) - n
                pltpu.make_async_copy(pb.at[at:at + TILES, h], full.at[x, :, h], sr_sem).start()

    owned = view(h, x)
    arrived(owned, t2r_sem)
    outs = []
    for n in (2, 1, 3):
        outs.append(send(owned, owned, os_sem.at[n], or_sem.at[n], 2 * ((x + n) % XS) + h, shard))
    outs.append(send(owned, owned, os_sem.at[0], or_sem.at[0], partner, shard))
    for copy in outs:
        copy.start()

    rows = full.at[x, :, h]
    row_sends = [
        send(rows, rows, ds_sem.at[n], dr_sem.at[x], 2 * ((x + n) % XS) + h, shard) for n in (2, 1, 3)
    ]
    row_sends.append(send(rows, rows, ds_sem.at[0], dr_sem.at[COLB + x], partner, shard))

    @pl.when(summing)
    def _():
        arrived(rows, sr_sem)
        for copy in row_sends:
            copy.start()

    def to_partner(n):
        piece = view(h, (x + XS - n) % XS)
        arrived(piece, or_sem.at[n])
        copy = send(piece, piece, os_sem.at[3 + n], or_sem.at[3 + n], partner, shard)
        copy.start()
        outs.append(copy)

    for n in (1, 3, 2):
        to_partner(n)

    def onward(c):
        return send(
            full.at[c, :, h], full.at[c, :, h], ds_sem.at[XS + c], dr_sem.at[COLB + c], partner, shard
        )

    for c in range(COLB):

        @pl.when(x != c)
        def _():
            arrived(full.at[c, :, h], dr_sem.at[c])
            onward(c).start()

    for copy in whole:
        copy.wait()

    def factors(n):
        on = look[2, 2 * shard + n] > 0
        g = g_own[:, n].reshape(BLK, BLK)
        g = jnp.where(on, g, jnp.zeros_like(g))
        gt = g.T
        for prev, out, a, b in ((lp, left_out, g, gt), (rp, right_out, gt, g)):
            new = prev[n].reshape(BLK, BLK) + mm(a, b)
            out[n] = jnp.where(on, new, jnp.zeros_like(new))

    for index, m in ((0, 0), (4, 1), (6, 3), (5, 2)):
        arrived(view(1 - h, (x + XS - m) % XS), or_sem.at[index])
    for n in range(2):
        factors(n)
    for c in range(COLB):
        arrived(full.at[c, :, 1 - h], dr_sem.at[COLB + c])
        d_out[:, :, :, c * BLK:(c + 1) * BLK] = full[c]

    kept = passing & ((passed_tile - TILES * w + 5 * HALF) % HALF < TILES)

    @pl.when(kept)
    def _():
        arrived(mid.at[0:COLB * (TILES - 1)], t1_sem)

    @pl.when(jnp.logical_not(kept))
    def _():
        arrived(mid.at[0:COLB * TILES], t1_sem)

    for copy in shares:
        copy.wait_send()
    swap.wait_send()
    for count, kept in ((16, 0), (16, 1), (32, 1)):

        @pl.when((jnp.where(summing, HALF, SHARDS) == count) & (old_here.astype(jnp.int32) == kept))
        def _():
            arrived(pvb.at[0:count - kept], p1_sem)

    @pl.when(old_here & home)
    def _():
        arrived(po.at[0:CELLS - 1], p2_sem)

    @pl.when(old_here & jnp.logical_not(home))
    def _():
        arrived(po, p2_sem)

    for c in range(COLB):

        @pl.when(x != c)
        def _():
            n = (c - x + XS) % XS - 1
            send(part.at[c], xin.at[n], xs_sem.at[c], xr_sem.at[n], 2 * c + h, shard).wait_send()
            onward(c).wait_send()

    @pl.when(summing)
    def _():
        to_homes(lambda n, src, dst, to: send(src, dst, gs_sem.at[n], gr_sem, rep, to).wait_send())

        for copy in row_sends:
            copy.wait_send()

    @pl.when(passing)
    def _():
        arrived(outb.at[0:SHARDS - 1], t2_sem)

    @pl.when(home)
    def _():
        half_block.wait_send()
        for copy in roots:
            copy.wait_send()
        for n in range(TILES):

            @pl.when(r == n)
            def _():
                to_rows(lambda i, src, dst, to: send(src, dst, ss_sem.at[i], sr_sem, rep, to).wait_send(), n)

    for copy in outs:
        copy.wait_send()


def store_kernel(d_in, left_in, right_in, d_out, left_new, right_new, sem):
    copies = []
    for n, (src, dst) in enumerate(((left_in, left_new), (right_in, right_new))):
        for j in range(2):
            copies.append(pltpu.make_async_copy(src.at[j], dst.at[j], sem.at[2 * n + j]))
    copies.append(pltpu.make_async_copy(d_in, d_out, sem.at[4]))
    for copy in copies:
        copy.start()
    for copy in copies:
        copy.wait()


SMEM = pl.BlockSpec(memory_space=pltpu.SMEM)
VMEM = pl.BlockSpec(memory_space=pltpu.VMEM)
ANY = pl.BlockSpec(memory_space=pl.ANY)
DMA = pltpu.SemaphoreType.DMA


def body(grads, left_prev, right_prev, block_owner, block_row, block_col):
    rows = grads.shape[1]
    direction, left_new, right_new = pl.pallas_call(
        step_kernel,
        out_shape=(
            pltpu.VMEM((TILES, 2, SUB, COLB * BLK), BF),
            pltpu.VMEM((2, BLK, BLK), F32),
            pltpu.VMEM((2, BLK, BLK), F32),
        ),
        in_specs=[SMEM, SMEM, SMEM, ANY, ANY, ANY],
        out_specs=(VMEM, VMEM, VMEM),
        scratch_shapes=[
            pltpu.VMEM((HALF, 2, 2, SUB, BLK), BF),
            pltpu.VMEM((2, 2 * HALF, SUB, BLK), F32),
            pltpu.VMEM((2, 2 * HALF, SUB, BLK), F32),
            pltpu.VMEM((TILES, SUB, COLB * BLK), BF),
            pltpu.VMEM((TILES, SUB, COLB * BLK), BF),
            pltpu.VMEM((COLB, TILES, SUB, BLK), BF),
            pltpu.VMEM((XS - 1, TILES, SUB, BLK), BF),
            pltpu.VMEM((TILES, SUB, BLK), BF),
            pltpu.VMEM((XS - 1, COLB, TILES, SUB, LANE), BF),
            pltpu.VMEM((TILES, COLB, SUB, LANE), BF),
            pltpu.VMEM((2, 2 * HALF, SUB, LANE), F32),
            pltpu.VMEM((2 * HALF, 2, SUB, LANE), BF),
            pltpu.VMEM((2 * SHARDS, SUB, LANE), BF),
            pltpu.VMEM((CELLS, SUB, LANE), BF),
            pltpu.VMEM((2 * HALF, SUB, BLK), BF),
            pltpu.VMEM((HALF, 2, SUB, BLK), BF),
            pltpu.VMEM((CELLS, SUB, LANE), BF),
            pltpu.VMEM((SHARDS, 2, SUB, LANE), BF),
            pltpu.VMEM((BLK, BLK), F32),
            pltpu.VMEM((2, BLK, BLK), BF),
            pltpu.VMEM((2, 8, LANE), F32),
            pltpu.VMEM((HALF, 2, SUB, BLK), BF),
            pltpu.VMEM((COLB, TILES, 2, SUB, BLK), BF),
            pltpu.VMEM((8, LANE), jnp.int32),
            pltpu.SMEM((8, LANE), jnp.int32),
            DMA, DMA, DMA((2,)), DMA((3,)), DMA((3,)),
            DMA, DMA, DMA, DMA, DMA((2,)), DMA, DMA((2,)), DMA, DMA, DMA, DMA, DMA((7,)), DMA((7,)),
            DMA((6,)), DMA((3,)), DMA, DMA((7,)), DMA((6,)), DMA, DMA((2,)), DMA((3,)), DMA((3,)), pltpu.SemaphoreType.REGULAR, pltpu.SemaphoreType.REGULAR,
        ],
        compiler_params=pltpu.CompilerParams(
            collective_id=0, has_side_effects=True, vmem_limit_bytes=58 * 1024 * 1024
        ),
        name="shampoo_step",
    )(
        block_owner,
        block_row,
        block_col,
        grads.reshape(TILES, 2, SUB, COLB * BLK),
        left_prev.reshape(2, 2 * HALF, SUB, BLK),
        right_prev.reshape(2, 2 * HALF, SUB, BLK),
    )

    sq = jax.ShapeDtypeStruct((2, BLK, BLK), F32)
    results = [pltpu.with_memory_space_constraint(v, pltpu.VMEM) for v in (direction, left_new, right_new)]
    direction, left_new, right_new = pl.pallas_call(
        store_kernel,
        out_shape=(jax.ShapeDtypeStruct((TILES, 2, SUB, COLB * BLK), BF), sq, sq),
        in_specs=[VMEM, VMEM, VMEM],
        out_specs=(ANY, ANY, ANY),
        scratch_shapes=[DMA((5,))],
        compiler_params=pltpu.CompilerParams(vmem_limit_bytes=16 * 1024 * 1024),
        cost_estimate=pl.CostEstimate(flops=0, bytes_accessed=9 * 2**20, transcendentals=0),
        name="store_results",
    )(*results)
    return direction.reshape(rows, COLB * BLK), left_new, right_new


def solution(mesh):
    in_specs = (P("rep", "shard", None), P("shard", None, None), P("shard", None, None), P(), P(), P())
    out_specs = (P("shard", None), P("shard", None, None), P("shard", None, None))
    return jax.shard_map(body, mesh=mesh, in_specs=in_specs, out_specs=out_specs, check_vma=False)
```
